32 devices in a mesh: seq: 16 (over z, y, x), fsdp: 2 (over core).
Axes of the slice: x: 2, y: 2, z: 4, core: 2. Of those that a mesh axis runs over, the one named last changes fastest.
Arguments:
- tokens: bfloat16 [2, 2, 2048, 1024], P(None, 'fsdp', 'seq'), may hold values from -6 to 6
- lengths: int32 [2, 2], replicated, may hold values from 1024 to 2048, as said below
- first_gain: bfloat16 [1024], P('fsdp'), may hold values from 0.099609375 to 1.8984375
- query_weight: bfloat16 [1024, 512], P('fsdp'), may hold values from -0.1875 to 0.1875
- key_weight: bfloat16 [1024, 512], P('fsdp'), may hold values from -0.1875 to 0.1875
- value_weight: bfloat16 [1024, 1024], P('fsdp'), may hold values from -0.1875 to 0.1875
- outgate_weight: bfloat16 [1024, 1024], P('fsdp'), may hold values from -0.1875 to 0.1875
- lowrank_in: bfloat16 [1024, 16], P('fsdp'), may hold values from -0.1875 to 0.1875
- lowrank_out: bfloat16 [16, 512], P(None, 'fsdp'), may hold values from -1.5 to 1.5
- decay_bias: bfloat16 [512], P('fsdp'), may hold values from 0 to 12
- head_gain: bfloat16 [256], P('fsdp'), may hold values from 0.099609375 to 1.8984375
- output_weight: bfloat16 [1024, 1024], P('fsdp'), may hold values from -0.1875 to 0.1875
- second_gain: bfloat16 [1024], P('fsdp'), may hold values from 0.099609375 to 1.8984375
- gate_weight: bfloat16 [1024, 2816], P('fsdp'), may hold values from -0.1875 to 0.1875
- up_weight: bfloat16 [1024, 2816], P('fsdp'), may hold values from -0.1875 to 0.1875
- down_weight: bfloat16 [2816, 1024], P('fsdp'), may hold values from -0.109375 to 0.109375
- cotangent: bfloat16 [2, 2, 2048, 1024], P(None, 'fsdp', 'seq'), may hold values from -6 to 6
Outputs:
- output: float32 [2, 2, 2048, 1024], P(None, 'fsdp', 'seq')
- tokens_grad: float32 [2, 2, 2048, 1024], P(None, 'fsdp', 'seq')
- first_gain_grad: float32 [1024], P('fsdp')
- query_weight_grad: float32 [1024, 512], P('fsdp')
- key_weight_grad: float32 [1024, 512], P('fsdp')
- value_weight_grad: float32 [1024, 1024], P('fsdp')
- outgate_weight_grad: float32 [1024, 1024], P('fsdp')
- lowrank_in_grad: float32 [1024, 16], P('fsdp')
- lowrank_out_grad: float32 [16, 512], P(None, 'fsdp')
- decay_bias_grad: float32 [512], P('fsdp')
- head_gain_grad: float32 [256], P('fsdp')
- output_weight_grad: float32 [1024, 1024], P('fsdp')
- second_gain_grad: float32 [1024], P('fsdp')
- gate_weight_grad: float32 [1024, 2816], P('fsdp')
- up_weight_grad: float32 [1024, 2816], P('fsdp')
- down_weight_grad: float32 [2816, 1024], P('fsdp')
The draws below stay inside these ranges and needn't reach their ends.
Inputs may be any that keep to these rules, and one draw needn't show every extreme that they name: `lengths`: in every column one micro-batch's sequence has all 2048 tokens valid.
All inputs are finite; a program needn't handle non-finite values.
Results may differ from the reference program's by a relative error of at most 0.025.
Values may be sent and summed in bfloat16 or wider, within the bound.
No kernel may reach another device: no remote copies, remote signals or barrier semaphores. Data moves between devices by JAX's collectives and lax.ppermute only.
A program may use at most 576 MiB of HBM per device.

```python
import jax
import jax.numpy as jnp
from jax import lax

D = 1024
FF = 2816
HEADS = 4
HV = 256
RANK = 16
SPAN = 64
MB = 2
KEY = 512
VAL = 1024
SEQS = 2
SEQ_LEN = 2048


def draw_lengths(key, part):
    key = jax.random.fold_in(key, 7)
    low_end = max(SEQ_LEN // 8, min(1024, SEQ_LEN // 2))
    first_key, second_key = jax.random.split(key)
    drawn = jax.random.randint(first_key, (MB, SEQS), low_end, SEQ_LEN + 1)
    chosen = jax.random.randint(second_key, (SEQS,), 0, MB)
    row_ids = jnp.arange(MB, dtype=jnp.int32)[:, None]
    return jnp.where(row_ids == chosen[None, :], SEQ_LEN, drawn).astype(jnp.int32)


def steps_of(own_key, shape, shards, least, largest):
    level = 1.0
    for axis_at, blocks in shards:
        draws = jax.random.uniform(jax.random.fold_in(jax.random.fold_in(own_key, 6), axis_at), (blocks,), jnp.float32, least / len(shards), largest / len(shards))
        level = level * jnp.repeat(jnp.exp(draws), shape[axis_at] // blocks).reshape((-1,) + (1,) * (len(shape) - 1 - axis_at))
    return level


def centred(rng, extent, scale, reach, cuts=(), kind=jnp.bfloat16):
    values = scale * jax.random.normal(rng, extent, jnp.float32)
    if cuts:
        values = values * steps_of(rng, extent, cuts, -0.22, 0.18)
    return jnp.clip(values, -reach, reach).astype(kind)


def setup_inputs(seed: int = 0) -> dict:
    keys = jax.random.split(jax.random.key(seed), 18)
    tokens = centred(keys[0], (MB, SEQS, SEQ_LEN, D), 1.0, 6.0, ((1, 2), (2, 16)))
    lengths = draw_lengths(jax.random.fold_in(keys[17], 71), 0)
    first_gain = jnp.clip(1.0 + 0.18 * jax.random.normal(keys[2], (D,), jnp.float32), 0.099609375, 1.8984375).astype(jnp.bfloat16)
    query_weight = centred(keys[3], (D, KEY), D ** -0.5, 0.1875, ((0, 2),))
    key_weight = centred(keys[4], (D, KEY), D ** -0.5, 0.1875, ((0, 2),))
    value_weight = centred(keys[5], (D, VAL), D ** -0.5, 0.1875, ((0, 2),))
    outgate_weight = centred(keys[6], (D, VAL), D ** -0.5, 0.1875, ((0, 2),))
    lowrank_in = centred(keys[7], (D, RANK), D ** -0.5, 0.1875, ((0, 2),))
    lowrank_out = centred(keys[8], (RANK, KEY), RANK ** -0.5, 1.5, ((1, 2),))
    decay_bias = jnp.clip(12.0 * jax.random.uniform(keys[9], (KEY,), jnp.float32) ** steps_of(keys[9], (KEY,), ((0, 2),), -0.2, 0.2), 0.0, 12.0).astype(jnp.bfloat16)
    head_gain = jnp.clip(1.0 + 0.18 * jax.random.normal(keys[10], (HV,), jnp.float32), 0.099609375, 1.8984375).astype(jnp.bfloat16)
    output_weight = centred(keys[11], (VAL, D), VAL ** -0.5, 0.1875, ((0, 2),))
    second_gain = jnp.clip(1.0 + 0.18 * jax.random.normal(keys[12], (D,), jnp.float32), 0.099609375, 1.8984375).astype(jnp.bfloat16)
    gate_weight = centred(keys[13], (D, FF), D ** -0.5, 0.1875, ((0, 2),))
    up_weight = centred(keys[14], (D, FF), D ** -0.5, 0.1875, ((0, 2),))
    down_weight = centred(keys[15], (FF, D), FF ** -0.5, 0.109375, ((0, 2),))
    cotangent = centred(keys[16], (MB, SEQS, SEQ_LEN, D), 1.0, 6.0, ((1, 2), (2, 16)))
    return {"tokens": tokens, "lengths": lengths, "first_gain": first_gain, "query_weight": query_weight, "key_weight": key_weight, "value_weight": value_weight, "outgate_weight": outgate_weight, "lowrank_in": lowrank_in, "lowrank_out": lowrank_out, "decay_bias": decay_bias, "head_gain": head_gain, "output_weight": output_weight, "second_gain": second_gain, "gate_weight": gate_weight, "up_weight": up_weight, "down_weight": down_weight, "cotangent": cotangent}


@jax.custom_vjp
def low(v):
    return lax.optimization_barrier(v.astype(jnp.bfloat16)).astype(jnp.float32)

@jax.custom_vjp
def low_back(v):
    return v

def low_keep(v):
    return (low(v), None)

def low_pass(kept, grad):
    return (grad,)

def back_keep(v):
    return (v, None)

def back_low(kept, grad):
    return (low(grad),)
low.defvjp(low_keep, low_pass)
low_back.defvjp(back_keep, back_low)
HIGH = lax.Precision.HIGHEST

def matmul(first_op, second_op):
    return jnp.dot(first_op, second_op, precision=HIGH, preferred_element_type=jnp.float32)

def rms_norm(value_in, gain_in, epsilon):
    return value_in * lax.rsqrt(lax.optimization_barrier(jnp.mean(value_in * value_in, axis=-1, keepdims=True)) + epsilon) * gain_in

def block_step(carried, pieces):
    queries, key_rows, values, decays = pieces
    factor = queries.shape[-1] ** (-0.5)
    length_block = queries.shape[1]
    cumulative = jnp.cumsum(decays, axis=1)
    last_cum = cumulative[:, -1]
    row_pos = jnp.arange(length_block, dtype=jnp.int32)
    causal = (row_pos[:, None] >= row_pos[None, :]).astype(jnp.float32)[None, :, :, None, None]
    gaps = cumulative[:, :, None] - cumulative[:, None, :]
    decay_weights = jnp.exp(jnp.where(causal > 0, gaps, 0.0)) * causal
    scores = lax.optimization_barrier(jnp.sum(queries[:, :, None] * key_rows[:, None] * decay_weights, axis=-1))
    within = jnp.einsum('pijh,pjhv->pihv', scores, values, precision=HIGH)
    cross = jnp.einsum('pihk,phkv->pihv', queries * jnp.exp(cumulative), carried, precision=HIGH)
    updated = jnp.exp(last_cum)[..., None] * carried + jnp.einsum('pjhk,pjhv->phkv', key_rows * jnp.exp(last_cum[:, None] - cumulative), values, precision=HIGH)
    return (updated, (within + cross) * factor)

def recurrence(queries, key_rows, values, decays):
    pair_count, seq_len = (queries.shape[0], queries.shape[1])

    def to_blocks(array):
        return jnp.moveaxis(array.reshape((pair_count, seq_len // SPAN, SPAN) + array.shape[2:]), 1, 0)
    start_state = jnp.zeros((pair_count, queries.shape[2], queries.shape[3], values.shape[3]), jnp.float32)
    closing, outputs = lax.scan(jax.checkpoint(block_step), start_state, (to_blocks(queries), to_blocks(key_rows), to_blocks(values), to_blocks(decays)))
    return jnp.moveaxis(outputs, 0, 1).reshape(values.shape)

def whole_layer(inputs_all, lengths, first_gain, query_weight, key_weight, value_weight, outgate_weight, lowrank_in, lowrank_out, decay_bias, head_gain, output_weight, second_gain, gate_weight, up_weight, down_weight):

    def micro_batch(batch):
        inputs, length = batch
        seq_count, seq_len = (inputs.shape[0], inputs.shape[1])
        heads_shape = (seq_count, seq_len, HEADS, -1)
        normed = low(rms_norm(inputs, first_gain, 1e-06))
        queries = low(low_back(matmul(normed, query_weight))).reshape(heads_shape)
        key_rows = low(low_back(matmul(normed, key_weight))).reshape(heads_shape)
        values = low(low_back(matmul(normed, value_weight))).reshape(heads_shape)
        outgate = low_back(matmul(normed, outgate_weight)).reshape(heads_shape)
        lowrank = low(low_back(matmul(normed, lowrank_in)))
        logits = low_back(matmul(lowrank, lowrank_out)) + decay_bias
        decays = (jax.nn.log_sigmoid(logits) / 16.0).reshape(heads_shape)
        mixture = recurrence(queries, key_rows, values, decays)
        gated_out = low(rms_norm(mixture, head_gain, 1e-05) * jax.nn.silu(outgate)).reshape(seq_count, seq_len, -1)
        hidden = inputs + low_back(matmul(gated_out, output_weight))
        second_normed = low(rms_norm(hidden, second_gain, 1e-06))
        gate_proj = low_back(matmul(second_normed, gate_weight))
        up_proj = low_back(matmul(second_normed, up_weight))
        hidden_act = low(jax.nn.silu(gate_proj) * up_proj)
        positions = jnp.arange(seq_len, dtype=jnp.int32)
        valid_mask = (positions[None, :] < length[:, None]).astype(jnp.float32)
        return (hidden + matmul(hidden_act, down_weight)) * valid_mask[:, :, None]
    return lax.map(jax.checkpoint(micro_batch), (inputs_all, lengths))

def reference(tokens, lengths, first_gain, query_weight, key_weight, value_weight, outgate_weight, lowrank_in, lowrank_out, decay_bias, head_gain, output_weight, second_gain, gate_weight, up_weight, down_weight, cotangent):
    weights = (first_gain, query_weight, key_weight, value_weight, outgate_weight, lowrank_in, lowrank_out, decay_bias, head_gain, output_weight, second_gain, gate_weight, up_weight, down_weight)
    floats = tuple((array.astype(jnp.float32) for array in weights))

    def wrapped(inputs_all, *params):
        return whole_layer(inputs_all, lengths, *params)
    output, pullback = jax.vjp(wrapped, tokens.astype(jnp.float32), *floats)
    gradients = pullback(cotangent.astype(jnp.float32))
    return (output, gradients[0], gradients[1], gradients[2], gradients[3], gradients[4], gradients[5], gradients[6], gradients[7], gradients[8], gradients[9], gradients[10], gradients[11], gradients[12], gradients[13], gradients[14])
```

```python
from functools import partial

import jax
import jax.numpy as jnp
from jax import lax
from jax.experimental import pallas as pl
from jax.experimental.pallas import tpu as pltpu
from jax.sharding import PartitionSpec as P

HEADS = 4
F32 = jnp.float32
BF16 = jnp.bfloat16
MIB = 1024 * 1024


def dot(first_op, second_op):
    return jnp.dot(first_op, second_op, preferred_element_type=F32)


def dot_t(first_op, second_op):
    return lax.dot_general(
        first_op, second_op, (((1,), (1,)), ((), ())), preferred_element_type=F32
    )


def t_dot(first_op, second_op):
    return lax.dot_general(
        first_op, second_op, (((0,), (0,)), ((), ())), preferred_element_type=F32
    )


def two_part(value):
    high = value.astype(BF16)
    return high, (value - high.astype(F32)).astype(BF16)


def mask_dot(mask, value):
    high, rest = two_part(value)
    return dot(mask, high) + dot(mask, rest)


def sigmoid(value):
    return 1.0 / (1.0 + jnp.exp(-value))


def pair_iota(size):
    return (
        lax.broadcasted_iota(jnp.int32, (size, size), 0),
        lax.broadcasted_iota(jnp.int32, (size, size), 1),
    )


def level_masks(size):
    row, col = pair_iota(size)
    out = []
    half = size // 2
    while half >= 1:
        block = 2 * half
        row_block = row // block
        middle = row_block * block + half - 1
        upper = row > middle
        sums = (upper & (col > middle) & (col <= row)) | (
            jnp.logical_not(upper) & (col > row) & (col <= middle)
        )
        same = row_block == col // block
        pairs = same & upper & (col <= middle)
        both = same & (upper != (col > middle))
        out.append((sums.astype(F32).astype(BF16), pairs, both, half))
        half //= 2
    return out


def upper_rows(half, width, size):
    row = lax.broadcasted_iota(jnp.int32, (size, width), 0)
    return row % (2 * half) >= half


def seat(idx_ref):
    return idx_ref[0], idx_ref[1]


def mine_at(idx_ref, width):
    return pl.ds(pl.multiple_of(idx_ref[0] * width, 128), width)


def theirs_at(idx_ref, width):
    return pl.ds(pl.multiple_of((1 - idx_ref[0]) * width, 128), width)


SMEM = pl.BlockSpec(memory_space=pltpu.SMEM)
VMEM = pl.BlockSpec(memory_space=pltpu.VMEM)


def call(name, body, idx, inputs, outs, scratch=(), flops=0, limit=32):
    shapes = [jax.ShapeDtypeStruct(s, d) for s, d in outs]
    moved = sum(a.size * a.dtype.itemsize for a in inputs) + sum(
        s.size * s.dtype.itemsize for s in shapes
    )
    result = pl.pallas_call(
        body,
        name=name,
        out_shape=shapes,
        in_specs=[SMEM] + [VMEM] * len(inputs),
        out_specs=[VMEM] * len(shapes),
        scratch_shapes=[pltpu.VMEM(s, d) for s, d in scratch],
        compiler_params=pltpu.CompilerParams(vmem_limit_bytes=limit * MIB),
        cost_estimate=pl.CostEstimate(
            flops=int(flops), bytes_accessed=int(moved), transcendentals=0
        ),
    )(idx, *inputs)
    return result


def put_message(ref, rows, total):
    count = rows.shape[0]
    ref[pl.ds(0, count), :] = rows.astype(BF16)
    high = total.astype(BF16)
    rest = total - high.astype(F32)
    middle = rest.astype(BF16)
    low = (rest - middle.astype(F32)).astype(BF16)
    tail = jnp.concatenate(
        [high, middle, low, jnp.zeros((13,) + total.shape[1:], BF16)], axis=0
    )
    ref[pl.ds(count, 16), :] = tail


def get_message(ref):
    count = ref.shape[0] - 16
    tail = ref[pl.ds(count, 16), :].astype(F32)
    return ref[pl.ds(0, count), :].astype(F32), tail[0:1] + tail[1:2] + tail[2:3]


def write_quarters(idx_ref, state, totals, messages, seq_count):
    low = lax.rem(idx_ref[1], 4)
    for other in range(4):
        quarter = low ^ other
        total = totals[0]
        for one in range(1, seq_count):
            total = jnp.where(quarter * seq_count // 4 >= one, totals[one], total)
        put_message(messages[other], state[quarter], total)


def group_total(reverse, idx_ref, *refs):
    out_ref, kept, held = refs[4], refs[5], refs[6]
    low = lax.rem(idx_ref[1], 4)
    for other in range(4):
        rows, total = get_message(refs[other])
        kept[low ^ other] = rows
        held[low ^ other] = total
    order = (3, 2, 1, 0) if reverse else (0, 1, 2, 3)
    rows, total = kept[order[0]], held[order[0]]
    for one in order[1:]:
        rows = held[one] * rows + kept[one]
        total = total * held[one]
    put_message(out_ref, rows, total)


def group_entering(reverse, far_count, idx_ref, *refs):
    far, near = refs[:far_count], refs[far_count : far_count + 4]
    outs = refs[far_count + 4 : far_count + 8]
    kept, held, entering = refs[far_count + 8 :]
    low = lax.rem(idx_ref[1], 4)
    for other in range(4):
        rows, total = get_message(near[other])
        kept[low ^ other] = rows
        held[low ^ other] = total
    rows = jnp.zeros(kept.shape[1:], F32)
    for one in far[::-1]:
        part, total = get_message(one)
        rows = total * rows + part
    for one in (3, 2, 1, 0) if reverse else (0, 1, 2, 3):
        entering[one] = rows
        rows = held[one] * rows + kept[one]
    for other in range(4):
        outs[other][...] = entering[low ^ other].astype(BF16)


def load_state(idx_ref, pieces, state):
    low = lax.rem(idx_ref[1], 4)
    for other in range(4):
        state[low ^ other] = pieces[other][...]


def keys_kernel(dims, idx_ref, x_ref, g1_own, g1_oth, wk_own, wk_oth, wv_own, wv_oth, li_own, li_oth,
                lo_own, lo_oth, b_own, b_oth, nm_ref, no_ref, k_ref, v_ref, lr_ref, lg_ref, kd_ref, tot_ref,
                m0, m1, m2, m3, state):
    seqs, span = dims
    half = g1_own.shape[1]
    xm = x_ref[:, mine_at(idx_ref, half)].astype(F32)
    xo = x_ref[:, theirs_at(idx_ref, half)].astype(F32)
    square = jnp.sum(xm * xm, axis=1, keepdims=True) + jnp.sum(xo * xo, axis=1, keepdims=True)
    root = lax.rsqrt(square / (2 * half) + 1e-6)
    nm = (xm * root * g1_own[...].astype(F32)).astype(BF16)
    no = (xo * root * g1_oth[...].astype(F32)).astype(BF16)
    nm_ref[...] = nm
    no_ref[...] = no
    lr = (dot(nm, li_own[...]) + dot(no, li_oth[...])).astype(BF16)
    lr_ref[...] = lr
    part = lo_own.shape[1]
    lg_ref[:, mine_at(idx_ref, part)] = dot(lr, lo_own[...]) + b_own[...].astype(F32)
    lg_ref[:, theirs_at(idx_ref, part)] = dot(lr, lo_oth[...]) + b_oth[...].astype(F32)
    keys = (dot(nm, wk_own[...]) + dot(no, wk_oth[...])).astype(BF16)
    k_ref[...] = keys
    values = (dot(nm, wv_own[...]) + dot(no, wv_oth[...])).astype(BF16)
    v_ref[...] = values
    row, col = pair_iota(span)
    later = (col > row).astype(F32).astype(BF16)
    wide = keys.shape[1] // HEADS
    tall = values.shape[1] // HEADS
    quarter = state.shape[1]
    totals = []
    for s in range(seqs):
        at = slice(s * span, (s + 1) * span)
        logits = lg_ref[at, :]
        decays = (jnp.minimum(logits, 0.0) - jnp.log1p(jnp.exp(-jnp.abs(logits)))) / 16.0
        ahead = mask_dot(later, decays)
        totals.append(jnp.exp(jnp.sum(decays, axis=0, keepdims=True)))
        tot_ref[pl.ds(s, 1), :] = totals[s]
        faded = (keys[at].astype(F32) * jnp.exp(ahead)).astype(BF16)
        kd_ref[at, :] = faded
        for h in range(HEADS):
            part = t_dot(values[at, h * tall : (h + 1) * tall], faded[:, h * wide : (h + 1) * wide])
            per = tall // quarter
            for q in range(per):
                state[s * per + q, :, h * wide : (h + 1) * wide] = part[q * quarter : (q + 1) * quarter]
    write_quarters(idx_ref, state, totals, (m0, m1, m2, m3), seqs)


def inner_kernel(dims, idx_ref, nm_ref, no_ref, wq_own, wq_oth, wg_own, wg_oth, k_ref, v_ref, lg_ref,
                 q_ref, og_ref, mix_ref, a_ref, qb_ref):
    seqs, span = dims
    nm, no = nm_ref[...], no_ref[...]
    queries = (dot(nm, wq_own[...]) + dot(no, wq_oth[...])).astype(BF16)
    q_ref[...] = queries
    og_ref[...] = dot(nm, wg_own[...]) + dot(no, wg_oth[...])
    row, col = pair_iota(span)
    upto = (col <= row).astype(F32).astype(BF16)
    diagonal = row == col
    levels = level_masks(span)
    wide = queries.shape[1] // HEADS
    tall = v_ref.shape[1] // HEADS
    for s in range(seqs):
        at = slice(s * span, (s + 1) * span)
        logits = lg_ref[at, :]
        decays = (jnp.minimum(logits, 0.0) - jnp.log1p(jnp.exp(-jnp.abs(logits)))) / 16.0
        high, rest = two_part(decays)
        qs, ks = queries[at], k_ref[at, :]
        qs32, ks32 = qs.astype(F32), ks.astype(F32)
        qb_ref[at, :] = (qs32 * jnp.exp(dot(upto, high) + dot(upto, rest))).astype(BF16)
        scores = []
        for h in range(HEADS):
            hs = slice(h * wide, (h + 1) * wide)
            scores.append(jnp.where(diagonal, dot_t(qs[:, hs], ks[:, hs]), 0.0))
        for sums, pairs, _, half in levels:
            fade = jnp.exp(dot(sums, high) + dot(sums, rest))
            side = (jnp.where(upper_rows(half, qs.shape[1], span), qs32, ks32) * fade).astype(BF16)
            for h in range(HEADS):
                part = side[:, h * wide : (h + 1) * wide]
                scores[h] = scores[h] + jnp.where(pairs, dot_t(part, part), 0.0)
        for h in range(HEADS):
            low = scores[h].astype(BF16)
            a_ref[s * HEADS + h] = low
            vs = slice(h * tall, (h + 1) * tall)
            mix_ref[at, vs] = dot(low, v_ref[at, vs])


def hidden_kernel(dims, idx_ref, mix_ref, qb_ref, e0, e1, e2, e3, og_ref, hg_own, hg_oth, x_ref, wo_own, wo_oth,
                  g2_own, g2_oth, mixture_ref, gm_ref, go_ref, hid_ref, sm_ref, so_ref, st_ref,
                  gain, gated):
    seqs, span = dims
    load_state(idx_ref, (e0, e1, e2, e3), st_ref)
    gain[:, mine_at(idx_ref, hg_own.shape[1])] = hg_own[...].astype(F32)
    gain[:, theirs_at(idx_ref, hg_own.shape[1])] = hg_oth[...].astype(F32)
    wide = qb_ref.shape[1] // HEADS
    tall = mix_ref.shape[1] // HEADS
    factor = wide ** (-0.5)
    quarter = st_ref.shape[1]
    per = tall // quarter
    head_gain = gain[...]
    for s in range(seqs):
        at = slice(s * span, (s + 1) * span)
        for h in range(HEADS):
            hs = slice(h * wide, (h + 1) * wide)
            for q in range(per):
                vs = slice(h * tall + q * quarter, h * tall + (q + 1) * quarter)
                carried = dot_t(qb_ref[at, hs], st_ref[s * per + q, :, hs])
                mixture_ref[at, vs] = (mix_ref[at, vs] + carried) * factor
            vs = slice(h * tall, (h + 1) * tall)
            mixture = mixture_ref[at, vs]
            root = lax.rsqrt(jnp.mean(mixture * mixture, axis=1, keepdims=True) + 1e-5)
            opened = og_ref[at, vs]
            gated[at, vs] = (mixture * root * head_gain * (opened * sigmoid(opened))).astype(BF16)
    half = wo_own.shape[0]
    gm = gated[:, mine_at(idx_ref, half)]
    go = gated[:, theirs_at(idx_ref, half)]
    gm_ref[...] = gm
    go_ref[...] = go
    hid_ref[...] = x_ref[...].astype(F32) + dot(gm, wo_own[...]) + dot(go, wo_oth[...])
    half = g2_own.shape[1]
    hm = hid_ref[:, mine_at(idx_ref, half)]
    ho = hid_ref[:, theirs_at(idx_ref, half)]
    square = jnp.sum(hm * hm, axis=1, keepdims=True) + jnp.sum(ho * ho, axis=1, keepdims=True)
    root = lax.rsqrt(square / (2 * half) + 1e-6)
    sm_ref[...] = (hm * root * g2_own[...].astype(F32)).astype(BF16)
    so_ref[...] = (ho * root * g2_oth[...].astype(F32)).astype(BF16)


def ffn_kernel(dims, idx_ref, sm_ref, so_ref, hid_ref, cot_ref, wg_own, wg_oth, wu_own, wu_oth, wd_own, wd_oth,
               out_ref, e_ref, am_ref, ao_ref, gg_ref, ug_ref, dm_ref, do_ref):
    seqs, span = dims
    rows, width = hid_ref.shape
    for s in range(seqs):
        at = slice(s * span, (s + 1) * span)
        places = lax.broadcasted_iota(jnp.int32, (span, width), 0) + idx_ref[1] * span
        valid = places < idx_ref[2 + s]
        e_ref[at, :] = jnp.where(valid, cot_ref[at, :].astype(F32), 0.0).astype(BF16)
    sm, so, cots = sm_ref[...], so_ref[...], e_ref[...]
    half = wd_own.shape[0]
    out_ref[...] = hid_ref[...]
    for step in range(2):
        at = (mine_at, theirs_at)[step](idx_ref, half)
        down = (wd_own, wd_oth)[step]
        act_ref = (am_ref, ao_ref)[step]
        gates = dot(sm, wg_own[:, at]) + dot(so, wg_oth[:, at])
        ups = dot(sm, wu_own[:, at]) + dot(so, wu_oth[:, at])
        sig = sigmoid(gates)
        opened = gates * sig
        act = (opened * ups).astype(BF16)
        act_ref[...] = act
        grads = dot_t(cots, down[...])
        gate_grad = (grads * ups * sig * (1.0 + gates * (1.0 - sig))).astype(BF16)
        up_grad = (grads * opened).astype(BF16)
        gg_ref[:, at] = gate_grad
        ug_ref[:, at] = up_grad
        out_ref[...] += dot(act, down[...])
        dm = dot_t(gate_grad, wg_own[:, at]) + dot_t(up_grad, wu_own[:, at])
        do = dot_t(gate_grad, wg_oth[:, at]) + dot_t(up_grad, wu_oth[:, at])
        if step == 0:
            dm_ref[...] = dm
            do_ref[...] = do
        else:
            dm_ref[...] += dm
            do_ref[...] += do
    for s in range(seqs):
        at = slice(s * span, (s + 1) * span)
        places = lax.broadcasted_iota(jnp.int32, (span, width), 0) + idx_ref[1] * span
        out_ref[at, :] = jnp.where(places < idx_ref[2 + s], out_ref[at, :], 0.0)


def gate_back_kernel(dims, idx_ref, hid_ref, dm_ref, do_ref, g2_own, g2_oth, e_ref, wo_own, wo_oth, mixture_ref,
                     og_ref, hg_own, hg_oth, qb_ref, tot_ref,
                     hg_ref, hl_ref, mg_ref, ol_ref, g2m_ref, g2o_ref, hgm_ref, hgo_ref, m0, m1, m2, m3,
                     gain, gated, gain_sum, state):
    seqs, span = dims
    half = g2_own.shape[1]
    mine, theirs = mine_at(idx_ref, half), theirs_at(idx_ref, half)
    hm, ho = hid_ref[:, mine], hid_ref[:, theirs]
    square = jnp.sum(hm * hm, axis=1, keepdims=True) + jnp.sum(ho * ho, axis=1, keepdims=True)
    root = lax.rsqrt(square / (2 * half) + 1e-6)
    dm, do = dm_ref[...], do_ref[...]
    g2m_ref[...] = jnp.sum(dm * hm * root, axis=0, keepdims=True)
    g2o_ref[...] = jnp.sum(do * ho * root, axis=0, keepdims=True)
    dm = dm * g2_own[...].astype(F32)
    do = do * g2_oth[...].astype(F32)
    along = jnp.sum(dm * hm, axis=1, keepdims=True) + jnp.sum(do * ho, axis=1, keepdims=True)
    along = along * (root * root * root) / (2 * half)
    hg_ref[:, mine] = e_ref[:, mine].astype(F32) + dm * root - hm * along
    hg_ref[:, theirs] = e_ref[:, theirs].astype(F32) + do * root - ho * along
    low = hg_ref[...].astype(BF16)
    hl_ref[...] = low
    half = wo_own.shape[0]
    gated[:, mine_at(idx_ref, half)] = dot_t(low, wo_own[...])
    gated[:, theirs_at(idx_ref, half)] = dot_t(low, wo_oth[...])
    gain[:, mine_at(idx_ref, hg_own.shape[1])] = hg_own[...].astype(F32)
    gain[:, theirs_at(idx_ref, hg_own.shape[1])] = hg_oth[...].astype(F32)
    head_gain = gain[...]
    wide = qb_ref.shape[1] // HEADS
    tall = mixture_ref.shape[1] // HEADS
    factor = wide ** (-0.5)
    quarter = state.shape[1]
    per = tall // quarter
    gain_grad = jnp.zeros((1, tall), F32)
    for s in range(seqs):
        at = slice(s * span, (s + 1) * span)
        for h in range(HEADS):
            vs = slice(h * tall, (h + 1) * tall)
            hs = slice(h * wide, (h + 1) * wide)
            mixture, opened, grad = mixture_ref[at, vs], og_ref[at, vs], gated[at, vs]
            root = lax.rsqrt(jnp.mean(mixture * mixture, axis=1, keepdims=True) + 1e-5)
            sig = sigmoid(opened)
            flat = mixture * root
            ol_ref[at, vs] = (grad * flat * head_gain * sig * (1.0 + opened * (1.0 - sig))).astype(BF16)
            grad = grad * (opened * sig)
            gain_grad += jnp.sum(grad * flat, axis=0, keepdims=True)
            grad = grad * head_gain
            along = jnp.mean(grad * flat, axis=1, keepdims=True)
            mixed = (grad - flat * along) * (root * factor)
            mg_ref[at, vs] = mixed
            part = t_dot(mixed.astype(BF16), qb_ref[at, hs])
            for q in range(per):
                state[s * per + q, :, hs] = part[q * quarter : (q + 1) * quarter]
    gain_sum[...] = gain_grad
    hgm_ref[...] = gain_sum[:, mine_at(idx_ref, hg_own.shape[1])]
    hgo_ref[...] = gain_sum[:, theirs_at(idx_ref, hg_own.shape[1])]
    totals = [tot_ref[pl.ds(s, 1), :] for s in range(seqs)]
    write_quarters(idx_ref, state, totals, (m0, m1, m2, m3), seqs)


def inner_back_kernel(dims, idx_ref, q_ref, k_ref, v_ref, lg_ref, a_ref, mg_ref, qb_ref, st_ref,
                      dq_ref, dk_ref, dv_ref, dc_ref):
    seqs, span = dims
    row, col = pair_iota(span)
    upto = (col <= row).astype(F32).astype(BF16)
    diagonal = row == col
    levels = level_masks(span)
    wide = q_ref.shape[1] // HEADS
    tall = v_ref.shape[1] // HEADS
    quarter = st_ref.shape[1]
    per = tall // quarter
    for s in range(seqs):
        at = slice(s * span, (s + 1) * span)
        logits = lg_ref[at, :]
        decays = (jnp.minimum(logits, 0.0) - jnp.log1p(jnp.exp(-jnp.abs(logits)))) / 16.0
        high, rest = two_part(decays)
        qs32, ks32 = q_ref[at, :].astype(F32), k_ref[at, :].astype(F32)
        begun = jnp.exp(dot(upto, high) + dot(upto, rest))
        pair_grads = []
        for h in range(HEADS):
            hs = slice(h * wide, (h + 1) * wide)
            vs = slice(h * tall, (h + 1) * tall)
            mixed, more = two_part(mg_ref[at, vs])
            values = v_ref[at, vs]
            full = dot_t(mixed, values) + dot_t(more, values)
            back = dot_t(values, mixed) + dot_t(values, more)
            pair_grads.append(jnp.where(row >= col, full, back))
            dv_ref[at, vs] = t_dot(a_ref[s * HEADS + h], mixed)
            own = jnp.sum(jnp.where(diagonal, full, 0.0), axis=1, keepdims=True)
            crossed = jnp.zeros((span, wide), F32)
            for q in range(per):
                part = slice(h * tall + q * quarter, h * tall + (q + 1) * quarter)
                crossed += dot(mg_ref[at, part].astype(BF16), st_ref[s * per + q, :, hs])
            dq_ref[at, hs] = own * ks32[:, hs] + begun[:, hs] * crossed
            dk_ref[at, hs] = own * qs32[:, hs]
            dc_ref[at, hs] = qb_ref[at, hs].astype(F32) * crossed
        for sums, _, both, half in levels:
            fade = jnp.exp(dot(sums, high) + dot(sums, rest))
            upper = upper_rows(half, qs32.shape[1], span)
            side = (jnp.where(upper, qs32, ks32) * fade).astype(BF16)
            for h in range(HEADS):
                hs = slice(h * wide, (h + 1) * wide)
                grads = dot(jnp.where(both, pair_grads[h], 0.0).astype(BF16), side[:, hs])
                moved = side[:, hs].astype(F32) * grads
                faded = fade[:, hs] * grads
                over = upper[:, hs]
                dc_ref[at, hs] += jnp.where(over, moved, -moved)
                dq_ref[at, hs] += jnp.where(over, faded, 0.0)
                dk_ref[at, hs] += jnp.where(over, 0.0, faded)


def inputs_back_kernel(dims, idx_ref, dq_ref, dk_ref, dv_ref, dc_ref, ol_ref, kd_ref, v_ref, lg_ref, tot_ref, st_ref,
                       l0, l1, l2, l3, x_ref, hg_ref, g1_own, g1_oth, wq_own, wq_oth, wk_own, wk_oth, wv_own, wv_oth,
                       wg_own, wg_oth, li_own, li_oth, lo_own, lo_oth,
                       tg_ref, ga_ref, llm_ref, llo_ref, g1m_ref, g1o_ref, bm_ref, bo_ref,
                       leaving, logit, bias):
    seqs, span = dims
    load_state(idx_ref, (l0, l1, l2, l3), leaving)
    row, col = pair_iota(span)
    later = (col > row).astype(F32).astype(BF16)
    since = (col >= row).astype(F32).astype(BF16)
    before = (col < row).astype(F32).astype(BF16)
    keys = kd_ref.shape[1]
    vals = v_ref.shape[1]
    wide, tall = keys // HEADS, vals // HEADS
    quarter = st_ref.shape[1]
    per = tall // quarter
    bias_sum = jnp.zeros((1, keys), F32)
    for s in range(seqs):
        at = slice(s * span, (s + 1) * span)
        logits = lg_ref[at, :]
        decays = (jnp.minimum(logits, 0.0) - jnp.log1p(jnp.exp(-jnp.abs(logits)))) / 16.0
        ahead = jnp.exp(mask_dot(later, decays))
        for h in range(HEADS):
            hs = slice(h * wide, (h + 1) * wide)
            faded = kd_ref[at, hs]
            grads = jnp.zeros((span, wide), F32)
            ends = jnp.zeros((1, wide), F32)
            for q in range(per):
                vs = slice(h * tall + q * quarter, h * tall + (q + 1) * quarter)
                at_v = slice(keys * 2 + vs.start, keys * 2 + vs.stop)
                part = leaving[s * per + q, :, hs]
                ga_ref[at, at_v] = (dv_ref[at, vs] + dot_t(faded, part)).astype(BF16)
                grads += dot(v_ref[at, vs], part)
                ends += jnp.sum(
                    st_ref[s * per + q, :, hs].astype(F32) * part.astype(F32), axis=0, keepdims=True
                )
            moved = faded.astype(F32) * grads
            ga_ref[at, keys + h * wide : keys + (h + 1) * wide] = (
                dk_ref[at, hs] + ahead[:, hs] * grads
            ).astype(BF16)
            decay_grad = (
                mask_dot(since, dc_ref[at, hs])
                + mask_dot(before, moved)
                + tot_ref[pl.ds(s, 1), hs] * ends
            )
            logit_grad = decay_grad * sigmoid(-logits[:, hs]) / 16.0
            bias[:, hs] = jnp.sum(logit_grad, axis=0, keepdims=True)
            logit[at, hs] = logit_grad.astype(BF16)
        bias_sum += bias[...]
    bias[...] = bias_sum
    part = lo_own.shape[1]
    bm_ref[...] = bias[:, mine_at(idx_ref, part)]
    bo_ref[...] = bias[:, theirs_at(idx_ref, part)]
    ga_ref[:, 0:keys] = dq_ref[...].astype(BF16)
    ga_ref[:, 2 * keys + vals : 2 * keys + 2 * vals] = ol_ref[...]
    llm, llo = logit[:, mine_at(idx_ref, part)], logit[:, theirs_at(idx_ref, part)]
    llm_ref[...] = llm
    llo_ref[...] = llo
    lrg = (dot_t(llm, lo_own[...]) + dot_t(llo, lo_oth[...])).astype(BF16)
    rank = lrg.shape[1]
    rest = jnp.zeros((lrg.shape[0], 128 - rank), BF16)
    ga_ref[:, 2 * keys + 2 * vals :] = jnp.concatenate([lrg, rest], axis=1)
    qg, kg = ga_ref[:, 0:keys], ga_ref[:, keys : 2 * keys]
    vg = ga_ref[:, 2 * keys : 2 * keys + vals]
    og = ga_ref[:, 2 * keys + vals : 2 * keys + 2 * vals]
    dm = dot_t(qg, wq_own[...]) + dot_t(kg, wk_own[...]) + dot_t(vg, wv_own[...])
    dm = dm + dot_t(og, wg_own[...]) + dot_t(lrg, li_own[...])
    do = dot_t(qg, wq_oth[...]) + dot_t(kg, wk_oth[...]) + dot_t(vg, wv_oth[...])
    do = do + dot_t(og, wg_oth[...]) + dot_t(lrg, li_oth[...])
    half = g1_own.shape[1]
    mine, theirs = mine_at(idx_ref, half), theirs_at(idx_ref, half)
    xm, xo = x_ref[:, mine].astype(F32), x_ref[:, theirs].astype(F32)
    square = jnp.sum(xm * xm, axis=1, keepdims=True) + jnp.sum(xo * xo, axis=1, keepdims=True)
    root = lax.rsqrt(square / (2 * half) + 1e-6)
    g1m_ref[...] = jnp.sum(dm * xm * root, axis=0, keepdims=True)
    g1o_ref[...] = jnp.sum(do * xo * root, axis=0, keepdims=True)
    dm = dm * g1_own[...].astype(F32)
    do = do * g1_oth[...].astype(F32)
    along = jnp.sum(dm * xm, axis=1, keepdims=True) + jnp.sum(do * xo, axis=1, keepdims=True)
    along = along * (root * root * root) / (2 * half)
    tg_ref[:, mine] = hg_ref[:, mine] + dm * root - xm * along
    tg_ref[:, theirs] = hg_ref[:, theirs] + do * root - xo * along


def block_of(position, order):
    block = 0
    for at, bit in enumerate(order):
        if (position >> (3 - at)) & 1:
            block |= bit
    return block


def deal(position, keep_ref, send_ref):
    return keep_ref.at[position] if position < 8 else send_ref.at[position - 8]


def wide_grad_kernel(order, idx_ref, lm_ref, lo_ref, gm_ref, go_ref, keep_ref, send_ref, full):
    place = lax.rem(idx_ref[1], 16)
    full[...] = t_dot(lm_ref[...], gm_ref[...]) + t_dot(lo_ref[...], go_ref[...])
    high = full.shape[0] // 16
    for position in range(16):
        block = block_of(position, order) ^ place
        rows = full[pl.ds(pl.multiple_of(block * high, high), high), :].astype(BF16)
        to = deal(position, keep_ref, send_ref)
        for tile in range(full.shape[1] // 128):
            to[tile * high : (tile + 1) * high, :] = rows[:, tile * 128 : (tile + 1) * 128]


def down_grad_kernel(order, idx_ref, lm_ref, lo_ref, gm_ref, go_ref, keep_ref, send_ref, full):
    place = lax.rem(idx_ref[1], 16)
    full[...] = t_dot(lm_ref[...], gm_ref[...]) + t_dot(lo_ref[...], go_ref[...])
    high = full.shape[0] // 2
    for position in range(16):
        block = block_of(position, order) ^ place
        rows = pl.ds(pl.multiple_of(lax.div(block, 8) * high, 16), high)
        cols = pl.ds(pl.multiple_of(lax.rem(block, 8) * 128, 128), 128)
        deal(position, keep_ref, send_ref)[...] = full[rows, cols].astype(BF16)


def attention_grad_kernel(orders, cuts, idx_ref, nm_ref, no_ref, gm_ref, go_ref, am_ref, ao_ref, hm_ref, ho_ref,
                          lrm_ref, lro_ref, llm_ref, llo_ref, g1_ref, g1o_ref, g2_ref, g2o_ref, b_ref, bo_ref,
                          hg_ref, hgo_ref, k0, s0, k1, s1, k2, s2, full, outer, small):
    place = lax.rem(idx_ref[1], 16)
    full[...] = t_dot(nm_ref[...], gm_ref[...]) + t_dot(no_ref[...], go_ref[...])
    outer[...] = t_dot(am_ref[...], hm_ref[...]) + t_dot(ao_ref[...], ho_ref[...])
    low_out = t_dot(lrm_ref[...], llm_ref[...]) + t_dot(lro_ref[...], llo_ref[...])
    small[...] = jnp.zeros_like(small)
    small[0] = low_out[:, 0:128]
    small[1] = low_out[:, 128:256]
    line = 0
    for first, second in ((g1_ref, g1o_ref), (g2_ref, g2o_ref), (b_ref, bo_ref), (hg_ref, hgo_ref)):
        row = first[...] + second[...]
        for tile in range(row.shape[1] // 128):
            small[2, line : line + 1, :] = row[:, tile * 128 : (tile + 1) * 128]
            line += 1
    high = full.shape[0] // 16
    tiles = full.shape[1] // 128
    for which, refs in enumerate(((k0, s0), (k1, s1), (k2, s2))):
        first, last = cuts[which], cuts[which + 1]
        for position in range(16):
            block = block_of(position, orders[which]) ^ place
            at = pl.ds(pl.multiple_of(block * high, high), high)
            to = deal(position, *refs)
            for tile in range(first, last):
                if tile < tiles:
                    rows = full[at, tile * 128 : (tile + 1) * 128]
                else:
                    rows = outer[at, (tile - tiles) * 128 : (tile - tiles + 1) * 128]
                to[(tile - first) * high : (tile - first + 1) * high, :] = rows.astype(BF16)
            if which == 2:
                to[(last - first) * high :, :] = small[block].astype(BF16)


def wide_open_kernel(order, idx_ref, own_ref, got_ref, out_ref):
    place = lax.rem(idx_ref[1], 16)
    high = out_ref.shape[0] // 16
    for position in range(16):
        block = block_of(position, order) ^ place
        held = deal(position, own_ref, got_ref)
        at = pl.ds(pl.multiple_of(block * high, high), high)
        for tile in range(out_ref.shape[1] // 128):
            out_ref[at, tile * 128 : (tile + 1) * 128] = held[tile * high : (tile + 1) * high, :].astype(F32)


def down_open_kernel(order, idx_ref, own_ref, got_ref, out_ref):
    place = lax.rem(idx_ref[1], 16)
    high = out_ref.shape[0] // 2
    for position in range(16):
        block = block_of(position, order) ^ place
        rows = pl.ds(pl.multiple_of(lax.div(block, 8) * high, 16), high)
        cols = pl.ds(pl.multiple_of(lax.rem(block, 8) * 128, 128), 128)
        out_ref[rows, cols] = deal(position, own_ref, got_ref)[...].astype(F32)


def attention_open_kernel(orders, cuts, idx_ref, o0, r0, o1, r1, o2, r2, q_ref, k_ref, v_ref, og_ref, li_ref, w_ref,
                          lo_ref, g1_ref, g2_ref, b_ref, hg_ref, small):
    place = lax.rem(idx_ref[1], 16)
    high = q_ref.shape[0] // 16
    homes = []
    for ref in (q_ref, k_ref, v_ref, og_ref):
        homes += [(ref, tile) for tile in range(ref.shape[1] // 128)]
    homes.append((li_ref, None))
    homes += [(w_ref, tile) for tile in range(w_ref.shape[1] // 128)]
    for which, refs in enumerate(((o0, r0), (o1, r1), (o2, r2))):
        first, last = cuts[which], cuts[which + 1]
        for position in range(16):
            block = block_of(position, orders[which]) ^ place
            at = pl.ds(pl.multiple_of(block * high, high), high)
            held = deal(position, *refs)
            for tile in range(first, last):
                rows = held[(tile - first) * high : (tile - first + 1) * high, :].astype(F32)
                ref, column = homes[tile]
                if column is None:
                    ref[at, :] = rows[:, : ref.shape[1]]
                else:
                    ref[at, column * 128 : (column + 1) * 128] = rows
            if which == 2:
                small[block] = held[(last - first) * high :, :].astype(F32)
    lo_ref[:, 0:128] = small[0]
    lo_ref[:, 128:256] = small[1]
    line = 0
    for ref in (g1_ref, g2_ref, b_ref, hg_ref):
        for tile in range(ref.shape[1] // 128):
            ref[:, tile * 128 : (tile + 1) * 128] = small[2, line : line + 1, :]
            line += 1


def across(array):
    return lax.ppermute(array, "fsdp", ((0, 1), (1, 0)))


def swap(array, bit):
    count = lax.axis_size("seq")
    return lax.ppermute(array, "seq", tuple((one, one ^ bit) for one in range(count)))


def ahead(array, step):
    count = lax.axis_size("seq")
    return lax.ppermute(
        array,
        "seq",
        tuple((one, one + step) for one in range(count) if 0 <= one + step < count),
    )


def together(arrays):
    return list(lax.optimization_barrier(tuple(arrays)))


def reduce_all(parts, orders):
    count = lax.axis_size("seq")
    kept = [keep for keep, _ in parts]
    sent = [send for _, send in parts]
    for step in range(4):
        got = together([swap(s, order[step]) for s, order in zip(sent, orders)])
        for one, more in enumerate(got):
            if step < 3:
                half = more.shape[0] // 2
                sent[one] = kept[one][half:] + more[half:]
                kept[one] = kept[one][:half] + more[:half]
            else:
                kept[one] = kept[one] + more
    bit = 16
    while bit < count:
        got = together([swap(k, bit) for k in kept])
        kept = [k + more for k, more in zip(kept, got)]
        bit *= 2
    for step in (3, 2, 1, 0):
        got = together([swap(k, order[step]) for k, order in zip(kept, orders)])
        if step:
            kept = [jnp.concatenate([k, more], axis=0) for k, more in zip(kept, got)]
    return list(zip(kept, got))


def scan_states(messages, idx, reverse, mid=None):
    count = lax.axis_size("seq")
    rows, lanes = messages[0].shape
    quarter = rows - 16
    near = [messages[0]] + [swap(messages[o], o) for o in (1, 2, 3)]
    kept = [((4, quarter, lanes), F32), ((4, 1, lanes), F32)]
    total = call("group_total", partial(group_total, reverse), idx, near, [((rows, lanes), BF16)], kept)[0]
    groups = count // 4
    sign = -4 if reverse else 4
    far = [ahead(total, sign * step) for step in range(1, groups)]
    outs = call(
        "group_entering", partial(group_entering, reverse, len(far)), idx, far + near,
        [((quarter, lanes), BF16)] * 4, kept + [((4, quarter, lanes), F32)],
    )
    return [outs[0]] + [swap(outs[o], o) for o in (1, 2, 3)]


def shards(
    tokens,
    lengths,
    first_gain,
    query_weight,
    key_weight,
    value_weight,
    outgate_weight,
    lowrank_in,
    lowrank_out,
    decay_bias,
    head_gain,
    output_weight,
    second_gain,
    gate_weight,
    up_weight,
    down_weight,
    cotangent,
):
    micro_count, pair_count, span, width = tokens.shape
    seqs = micro_count * pair_count
    rows = seqs * span
    dims = (seqs, span)
    core = lax.axis_index("fsdp")
    place = lax.axis_index("seq")
    own_lengths = lax.dynamic_slice_in_dim(lengths, core * pair_count, pair_count, 1).reshape(-1)
    idx = jnp.concatenate([jnp.stack([core, place]).astype(jnp.int32), own_lengths])
    keys, vals, ff = query_weight.shape[1], value_weight.shape[1], gate_weight.shape[1]
    half = query_weight.shape[0]
    tall = vals // HEADS
    quarter = seqs * tall // 4

    x = tokens.reshape(rows, width)
    cot = cotangent.reshape(rows, width)
    first_gain, decay_bias, head_gain, second_gain = (
        a.reshape(1, -1) for a in (first_gain, decay_bias, head_gain, second_gain)
    )
    wk2, g12, li2, lo2, b2 = (across(a) for a in (key_weight, first_gain, lowrank_in, lowrank_out, decay_bias))
    wv2, wq2, wg2 = (across(a) for a in (value_weight, query_weight, outgate_weight))
    hg2, g22, wo2 = (across(a) for a in (head_gain, second_gain, output_weight))
    wgate2, wup2, wdown2 = (across(a) for a in (gate_weight, up_weight, down_weight))

    message = ((quarter + 16, keys), BF16)
    state = ((4, quarter, keys), F32)
    nm, no, k, v, lr, lg, kd, tot, *messages = call(
        "keys", partial(keys_kernel, dims), idx,
        [x, first_gain, g12, key_weight, wk2, value_weight, wv2, lowrank_in, li2, lowrank_out, lo2, decay_bias, b2],
        [((rows, half), BF16), ((rows, half), BF16), ((rows, keys), BF16), ((rows, vals), BF16),
         ((rows, lowrank_in.shape[1]), BF16), ((rows, keys), F32), ((rows, keys), BF16), ((seqs, keys), F32)]
        + [message] * 4,
        [state], flops=2 * rows * width * (keys + vals) + 4 * rows * span * keys,
    )
    pieces = scan_states(messages, idx, False)
    q, og, mix, scores, qb = call(
        "inner", partial(inner_kernel, dims), idx,
        [nm, no, query_weight, wq2, outgate_weight, wg2, k, v, lg],
        [((rows, keys), BF16), ((rows, vals), F32), ((rows, vals), F32), ((seqs * HEADS, span, span), BF16),
         ((rows, keys), BF16)],
        flops=2 * rows * width * (keys + vals) + 60 * rows * span * keys,
    )
    mixture, gm, go, hid, sm, so, st = call(
        "hidden", partial(hidden_kernel, dims), idx,
        [mix, qb, *pieces, og, head_gain, hg2, x, output_weight, wo2, second_gain, g22],
        [((rows, vals), F32), ((rows, vals // 2), BF16), ((rows, vals // 2), BF16), ((rows, width), F32),
         ((rows, half), BF16), ((rows, half), BF16), ((4, quarter, keys), BF16)],
        [((1, tall), F32), ((rows, vals), BF16)], flops=2 * rows * vals * width,
    )
    out, cots, am, ao, gate_grad, up_grad, dm, do = call(
        "ffn", partial(ffn_kernel, dims), idx,
        [sm, so, hid, cot, gate_weight, wgate2, up_weight, wup2, down_weight, wdown2],
        [((rows, width), F32), ((rows, width), BF16), ((rows, ff // 2), BF16), ((rows, ff // 2), BF16),
         ((rows, ff), BF16), ((rows, ff), BF16), ((rows, half), F32), ((rows, half), F32)],
        flops=12 * rows * width * ff, limit=52,
    )

    bits = (1, 2, 4, 8)
    orders = ((bits[0], bits[1], bits[2], bits[3]), (bits[1], bits[2], bits[0], bits[3]), (bits[2], bits[0], bits[1], bits[3]))
    cots2, ao2, so2, gate_grad2, up_grad2 = (across(a) for a in (cots, ao, so, gate_grad, up_grad))
    portion = ff // 128 * (half // 16)
    flat = [((8, portion, 128), BF16)] * 2
    down_parts = call("down_grad", partial(down_grad_kernel, orders[2]), idx, [am, ao2, cots, cots2], flat,
                      [((ff // 2, width), F32)], flops=2 * rows * ff * width)
    gate_parts = call("gate_grad", partial(wide_grad_kernel, orders[0]), idx, [sm, so2, gate_grad, gate_grad2], flat,
                      [((half, ff), F32)], flops=2 * rows * ff * width)
    up_parts = call("up_grad", partial(wide_grad_kernel, orders[1]), idx, [sm, so2, up_grad, up_grad2], flat,
                    [((half, ff), F32)], flops=2 * rows * ff * width)
    gate_halves, up_halves, down_halves = reduce_all([gate_parts, up_parts, down_parts], orders)
    gate_out = call("gate_open", partial(wide_open_kernel, orders[0]), idx, gate_halves, [((half, ff), F32)])[0]
    up_out = call("up_open", partial(wide_open_kernel, orders[1]), idx, up_halves, [((half, ff), F32)])[0]
    down_out = call("down_open", partial(down_open_kernel, orders[2]), idx, down_halves, [((ff // 2, width), F32)])[0]

    hg, hl, mg, ol, g2m, g2o, hgm, hgo, *messages = call(
        "gate_back", partial(gate_back_kernel, dims), idx,
        [hid, dm, do, second_gain, g22, cots, output_weight, wo2, mixture, og, head_gain, hg2, qb, tot],
        [((rows, width), F32), ((rows, width), BF16), ((rows, vals), F32), ((rows, vals), BF16),
         ((1, half), F32), ((1, half), F32), ((1, tall // 2), F32), ((1, tall // 2), F32)] + [message] * 4,
        [((1, tall), F32), ((rows, vals), F32), ((1, tall), F32), state],
        flops=2 * rows * width * vals + 4 * rows * span * keys,
    )
    pieces = scan_states(messages, idx, True)
    dq, dk, dv, dc = call(
        "inner_back", partial(inner_back_kernel, dims), idx, [q, k, v, lg, scores, mg, qb, st],
        [((rows, keys), F32), ((rows, keys), F32), ((rows, vals), F32), ((rows, keys), F32)],
        flops=100 * rows * span * keys,
    )
    lanes = 2 * keys + 2 * vals + 128
    tg, ga, llm, llo, g1m, g1o, bm, bo = call(
        "inputs_back", partial(inputs_back_kernel, dims), idx,
        [dq, dk, dv, dc, ol, kd, v, lg, tot, st, *pieces, x, hg, first_gain, g12, query_weight, wq2, key_weight, wk2,
         value_weight, wv2, outgate_weight, wg2, lowrank_in, li2, lowrank_out, lo2],
        [((rows, width), F32), ((rows, lanes), BF16), ((rows, keys // 2), BF16), ((rows, keys // 2), BF16),
         ((1, half), F32), ((1, half), F32), ((1, keys // 2), F32), ((1, keys // 2), F32)],
        [((4, quarter, keys), BF16), ((rows, keys), BF16), ((1, keys), F32)],
        flops=2 * rows * width * lanes + 8 * rows * span * keys, limit=40,
    )
    go2, hl2, no2, lr2 = (across(a) for a in (go, hl, no, lr))
    ga2, llo2, g1o2, g2o2, bo2, hgo2 = (across(a) for a in (ga, llo, g1o, g2o, bo, hgo))
    tiles = lanes // 128 + width // 128
    cuts = (0, tiles // 3, 2 * tiles // 3, tiles)
    high = half // 16
    shapes = []
    for which in range(3):
        size = (cuts[which + 1] - cuts[which]) * high + (16 if which == 2 else 0)
        shapes += [((8, size, 128), BF16)] * 2
    parts = call(
        "attention_grad", partial(attention_grad_kernel, orders, cuts), idx,
        [nm, no2, ga, ga2, gm, go2, hl, hl2, lr, lr2, llm, llo2, g1m, g1o2, g2m, g2o2, bm, bo2, hgm, hgo2],
        shapes, [((half, lanes), F32), ((vals // 2, width), F32), ((16, 16, 128), F32)],
        flops=2 * 2 * rows * (half * lanes + width * vals // 2),
    )
    halves = reduce_all([parts[0:2], parts[2:4], parts[4:6]], orders)
    opened = call(
        "attention_open", partial(attention_open_kernel, orders, cuts), idx, [a for pair in halves for a in pair],
        [((half, keys), F32), ((half, keys), F32), ((half, vals), F32), ((half, vals), F32),
         ((half, lowrank_in.shape[1]), F32), ((vals // 2, width), F32), ((lowrank_out.shape[0], keys // 2), F32),
         ((1, half), F32), ((1, half), F32), ((1, keys // 2), F32), ((1, tall // 2), F32)],
        [((16, 16, 128), F32)],
    )
    q_out, k_out, v_out, og_out, li_out, w_out, lo_out, g1_out, g2_out, b_out, hg_out = opened
    return (
        out.reshape(tokens.shape),
        tg.reshape(tokens.shape),
        g1_out.reshape(-1),
        q_out,
        k_out,
        v_out,
        og_out,
        li_out,
        lo_out,
        b_out.reshape(-1),
        hg_out.reshape(-1),
        w_out,
        g2_out.reshape(-1),
        gate_out,
        up_out,
        down_out,
    )


def solution(mesh):
    shard, column = P("fsdp", None), P(None, "fsdp")
    stream, line = P(None, "fsdp", "seq", None), P("fsdp")
    weights = (line, shard, shard, shard, shard, shard, column, line, line, shard, line, shard, shard, shard)
    return jax.shard_map(
        shards,
        mesh=mesh,
        in_specs=(stream, P()) + weights + (stream,),
        out_specs=(stream, stream) + weights,
        check_vma=False,
    )
```

```python
from functools import partial

import jax
import jax.numpy as jnp
from jax import lax
from jax.experimental import pallas as pl
from jax.experimental.pallas import tpu as pltpu
from jax.sharding import PartitionSpec as P

HEADS = 4
F32 = jnp.float32
BF16 = jnp.bfloat16
MIB = 1024 * 1024


def dot(first_op, second_op):
    return jnp.dot(first_op, second_op, preferred_element_type=F32)


def dot_t(first_op, second_op):
    return lax.dot_general(
        first_op, second_op, (((1,), (1,)), ((), ())), preferred_element_type=F32
    )


def t_dot(first_op, second_op):
    return lax.dot_general(
        first_op, second_op, (((0,), (0,)), ((), ())), preferred_element_type=F32
    )


def two_part(value):
    high = value.astype(BF16)
    return high, (value - high.astype(F32)).astype(BF16)


def mask_dot(mask, value):
    high, rest = two_part(value)
    return dot(mask, high) + dot(mask, rest)


def sigmoid(value):
    return 1.0 / (1.0 + jnp.exp(-value))


def pair_iota(size):
    return (
        lax.broadcasted_iota(jnp.int32, (size, size), 0),
        lax.broadcasted_iota(jnp.int32, (size, size), 1),
    )


def level_masks(size):
    row, col = pair_iota(size)
    out = []
    half = size // 2
    while half >= 1:
        block = 2 * half
        row_block = row // block
        middle = row_block * block + half - 1
        upper = row > middle
        sums = (upper & (col > middle) & (col <= row)) | (
            jnp.logical_not(upper) & (col > row) & (col <= middle)
        )
        same = row_block == col // block
        pairs = same & upper & (col <= middle)
        both = same & (upper != (col > middle))
        out.append((sums.astype(F32).astype(BF16), pairs, both, half))
        half //= 2
    return out


def upper_rows(half, width, size):
    row = lax.broadcasted_iota(jnp.int32, (size, width), 0)
    return row % (2 * half) >= half


def seat(idx_ref):
    return idx_ref[0], idx_ref[1]


def mine_at(idx_ref, width):
    return pl.ds(pl.multiple_of(idx_ref[0] * width, 128), width)


def theirs_at(idx_ref, width):
    return pl.ds(pl.multiple_of((1 - idx_ref[0]) * width, 128), width)


SMEM = pl.BlockSpec(memory_space=pltpu.SMEM)
VMEM = pl.BlockSpec(memory_space=pltpu.VMEM)


def call(name, body, idx, inputs, outs, scratch=(), flops=0, limit=32, far=0):
    shapes = [jax.ShapeDtypeStruct(s, d) for s, d in outs]
    moved = sum(a.size * a.dtype.itemsize for a in inputs) + sum(
        s.size * s.dtype.itemsize for s in shapes
    )
    result = pl.pallas_call(
        body,
        name=name,
        out_shape=shapes,
        in_specs=[SMEM] + [VMEM] * (len(inputs) - far) + [pl.BlockSpec(memory_space=pl.ANY)] * far,
        out_specs=[VMEM] * len(shapes),
        scratch_shapes=[pltpu.VMEM(*s) if isinstance(s, tuple) else s for s in scratch],
        compiler_params=pltpu.CompilerParams(vmem_limit_bytes=limit * MIB),
        cost_estimate=pl.CostEstimate(
            flops=int(flops), bytes_accessed=int(moved), transcendentals=0
        ),
    )(idx, *inputs)
    return result


def put_message(ref, rows, total):
    count = rows.shape[0]
    ref[pl.ds(0, count), :] = rows.astype(BF16)
    high = total.astype(BF16)
    rest = total - high.astype(F32)
    middle = rest.astype(BF16)
    low = (rest - middle.astype(F32)).astype(BF16)
    tail = jnp.concatenate(
        [high, middle, low, jnp.zeros((13,) + total.shape[1:], BF16)], axis=0
    )
    ref[pl.ds(count, 16), :] = tail


def get_message(ref):
    count = ref.shape[0] - 16
    tail = ref[pl.ds(count, 16), :].astype(F32)
    return ref[pl.ds(0, count), :].astype(F32), tail[0:1] + tail[1:2] + tail[2:3]


def write_quarters(idx_ref, state, totals, messages, seq_count):
    low = lax.rem(idx_ref[1], 4)
    for other in range(4):
        quarter = low ^ other
        total = totals[0]
        for one in range(1, seq_count):
            total = jnp.where(quarter * seq_count // 4 >= one, totals[one], total)
        put_message(messages[other], state[quarter], total)


def group_total(reverse, idx_ref, *refs):
    out_ref, kept, held = refs[4], refs[5], refs[6]
    low = lax.rem(idx_ref[1], 4)
    for other in range(4):
        rows, total = get_message(refs[other])
        kept[low ^ other] = rows
        held[low ^ other] = total
    order = (3, 2, 1, 0) if reverse else (0, 1, 2, 3)
    rows, total = kept[order[0]], held[order[0]]
    for one in order[1:]:
        rows = held[one] * rows + kept[one]
        total = total * held[one]
    put_message(out_ref, rows, total)


def group_entering(reverse, far_count, idx_ref, *refs):
    far, near = refs[:far_count], refs[far_count : far_count + 4]
    outs = refs[far_count + 4 : far_count + 8]
    kept, held, entering = refs[far_count + 8 :]
    low = lax.rem(idx_ref[1], 4)
    for other in range(4):
        rows, total = get_message(near[other])
        kept[low ^ other] = rows
        held[low ^ other] = total
    rows = jnp.zeros(kept.shape[1:], F32)
    for one in far[::-1]:
        part, total = get_message(one)
        rows = total * rows + part
    for one in (3, 2, 1, 0) if reverse else (0, 1, 2, 3):
        entering[one] = rows
        rows = held[one] * rows + kept[one]
    for other in range(4):
        outs[other][...] = entering[low ^ other].astype(BF16)


def load_state(idx_ref, pieces, state):
    low = lax.rem(idx_ref[1], 4)
    for other in range(4):
        state[low ^ other] = pieces[other][...]


def pack_kernel(idx_ref, li_ref, lo_ref, g1_ref, g2_ref, b_ref, hg_ref, out_ref):
    rank = li_ref.shape[1]
    high = li_ref.shape[0]
    out_ref[0:high, :] = jnp.concatenate(
        [li_ref[...], jnp.zeros((high, 128 - rank), BF16)], axis=1
    )
    at = high
    for tile in range(lo_ref.shape[1] // 128):
        out_ref[at : at + rank, :] = lo_ref[:, tile * 128 : (tile + 1) * 128]
        at += rank
    lines = []
    for ref in (g1_ref, g2_ref, b_ref, hg_ref):
        row = ref[...].astype(F32)
        lines += [row[:, tile * 128 : (tile + 1) * 128] for tile in range(row.shape[1] // 128)]
    lines.append(jnp.zeros((out_ref.shape[0] - at - len(lines), 128), F32))
    out_ref[at:, :] = jnp.concatenate(lines, axis=0).astype(BF16)


def packed_factors(pack_ref, rank, part):
    high = pack_ref.shape[0] - 16 - rank * part // 128
    first = pack_ref[0:high, :][:, 0:rank]
    second = [pack_ref[high + t * rank : high + (t + 1) * rank, :] for t in range(part // 128)]
    return first, jnp.concatenate(second, axis=1)


def packed_row(pack_ref, first, count):
    lines = pack_ref[pack_ref.shape[0] - 16 :, :].astype(F32)
    return jnp.concatenate([lines[t : t + 1, :] for t in range(first, first + count)], axis=1)


def packed_places(half, part, gain):
    g1, b, hg = half // 128, part // 128, gain // 128
    return (0, g1), (g1, g1), (2 * g1, b), (2 * g1 + b, hg)


def keys_kernel(dims, idx_ref, x_ref, cot_ref, g1_own, wk_own, wk_oth, wv_own, wv_oth, li_own, lo_own, b_own, pack_ref,
                nm_ref, no_ref, k_ref, v_ref, lr_ref, lg_ref, kd_ref, tot_ref, e_ref,
                m0, m1, m2, m3, state):
    seqs, span = dims
    half = g1_own.shape[1]
    rank, part = lo_own.shape
    place_g1, _, place_b, _ = packed_places(half, part, 0)
    li_oth, lo_oth = packed_factors(pack_ref, rank, part)
    g1_oth = packed_row(pack_ref, *place_g1)
    b_oth = packed_row(pack_ref, *place_b)
    for s in range(seqs):
        at = slice(s * span, (s + 1) * span)
        places = lax.broadcasted_iota(jnp.int32, (span, cot_ref.shape[1]), 0) + idx_ref[1] * span
        e_ref[at, :] = jnp.where(places < idx_ref[2 + s], cot_ref[at, :].astype(F32), 0.0).astype(BF16)
    xm = x_ref[:, mine_at(idx_ref, half)].astype(F32)
    xo = x_ref[:, theirs_at(idx_ref, half)].astype(F32)
    square = jnp.sum(xm * xm, axis=1, keepdims=True) + jnp.sum(xo * xo, axis=1, keepdims=True)
    root = lax.rsqrt(square / (2 * half) + 1e-6)
    nm = (xm * root * g1_own[...].astype(F32)).astype(BF16)
    no = (xo * root * g1_oth).astype(BF16)
    nm_ref[...] = nm
    no_ref[...] = no
    lr = (dot(nm, li_own[...]) + dot(no, li_oth)).astype(BF16)
    lr_ref[...] = lr
    lg_ref[:, mine_at(idx_ref, part)] = dot(lr, lo_own[...]) + b_own[...].astype(F32)
    lg_ref[:, theirs_at(idx_ref, part)] = dot(lr, lo_oth) + b_oth
    keys = (dot(nm, wk_own[...]) + dot(no, wk_oth[...])).astype(BF16)
    k_ref[...] = keys
    values = (dot(nm, wv_own[...]) + dot(no, wv_oth[...])).astype(BF16)
    v_ref[...] = values
    row, col = pair_iota(span)
    later = (col > row).astype(F32).astype(BF16)
    wide = keys.shape[1] // HEADS
    tall = values.shape[1] // HEADS
    quarter = state.shape[1]
    totals = []
    for s in range(seqs):
        at = slice(s * span, (s + 1) * span)
        logits = lg_ref[at, :]
        decays = (jnp.minimum(logits, 0.0) - jnp.log1p(jnp.exp(-jnp.abs(logits)))) / 16.0
        ahead = mask_dot(later, decays)
        totals.append(jnp.exp(jnp.sum(decays, axis=0, keepdims=True)))
        tot_ref[pl.ds(s, 1), :] = totals[s]
        faded = (keys[at].astype(F32) * jnp.exp(ahead)).astype(BF16)
        kd_ref[at, :] = faded
        for h in range(HEADS):
            part = t_dot(values[at, h * tall : (h + 1) * tall], faded[:, h * wide : (h + 1) * wide])
            per = tall // quarter
            for q in range(per):
                state[s * per + q, :, h * wide : (h + 1) * wide] = part[q * quarter : (q + 1) * quarter]
    write_quarters(idx_ref, state, totals, (m0, m1, m2, m3), seqs)


def inner_kernel(dims, idx_ref, nm_ref, no_ref, wq_own, wq_oth, wg_own, wg_oth, k_ref, v_ref, lg_ref,
                 q_ref, og_ref, mix_ref, a_ref, qb_ref):
    seqs, span = dims
    nm, no = nm_ref[...], no_ref[...]
    queries = (dot(nm, wq_own[...]) + dot(no, wq_oth[...])).astype(BF16)
    q_ref[...] = queries
    og_ref[...] = dot(nm, wg_own[...]) + dot(no, wg_oth[...])
    row, col = pair_iota(span)
    upto = (col <= row).astype(F32).astype(BF16)
    diagonal = row == col
    levels = level_masks(span)
    wide = queries.shape[1] // HEADS
    tall = v_ref.shape[1] // HEADS
    for s in range(seqs):
        at = slice(s * span, (s + 1) * span)
        logits = lg_ref[at, :]
        decays = (jnp.minimum(logits, 0.0) - jnp.log1p(jnp.exp(-jnp.abs(logits)))) / 16.0
        high, rest = two_part(decays)
        qs, ks = queries[at], k_ref[at, :]
        qs32, ks32 = qs.astype(F32), ks.astype(F32)
        qb_ref[at, :] = (qs32 * jnp.exp(dot(upto, high) + dot(upto, rest))).astype(BF16)
        scores = []
        for h in range(HEADS):
            hs = slice(h * wide, (h + 1) * wide)
            scores.append(jnp.where(diagonal, dot_t(qs[:, hs], ks[:, hs]), 0.0))
        for sums, pairs, _, half in levels:
            fade = jnp.exp(dot(sums, high) + dot(sums, rest))
            side = (jnp.where(upper_rows(half, qs.shape[1], span), qs32, ks32) * fade).astype(BF16)
            for h in range(HEADS):
                part = side[:, h * wide : (h + 1) * wide]
                scores[h] = scores[h] + jnp.where(pairs, dot_t(part, part), 0.0)
        for h in range(HEADS):
            low = scores[h].astype(BF16)
            a_ref[s * HEADS + h] = low
            vs = slice(h * tall, (h + 1) * tall)
            mix_ref[at, vs] = dot(low, v_ref[at, vs])


def hidden_kernel(dims, idx_ref, mix_ref, qb_ref, e0, e1, e2, e3, og_ref, hg_own, x_ref, wo_own, wo_oth,
                  g2_own, pack_ref, mixture_ref, gm_ref, go_ref, hid_ref, sm_ref, so_ref, st_ref,
                  gain, gated):
    seqs, span = dims
    load_state(idx_ref, (e0, e1, e2, e3), st_ref)
    _, place_g2, _, place_hg = packed_places(g2_own.shape[1], qb_ref.shape[1] // 2, hg_own.shape[1])
    gain[:, mine_at(idx_ref, hg_own.shape[1])] = hg_own[...].astype(F32)
    gain[:, theirs_at(idx_ref, hg_own.shape[1])] = packed_row(pack_ref, *place_hg)
    wide = qb_ref.shape[1] // HEADS
    tall = mix_ref.shape[1] // HEADS
    factor = wide ** (-0.5)
    quarter = st_ref.shape[1]
    per = tall // quarter
    head_gain = gain[...]
    for s in range(seqs):
        at = slice(s * span, (s + 1) * span)
        for h in range(HEADS):
            hs = slice(h * wide, (h + 1) * wide)
            for q in range(per):
                vs = slice(h * tall + q * quarter, h * tall + (q + 1) * quarter)
                carried = dot_t(qb_ref[at, hs], st_ref[s * per + q, :, hs])
                mixture_ref[at, vs] = (mix_ref[at, vs] + carried) * factor
            vs = slice(h * tall, (h + 1) * tall)
            mixture = mixture_ref[at, vs]
            root = lax.rsqrt(jnp.mean(mixture * mixture, axis=1, keepdims=True) + 1e-5)
            opened = og_ref[at, vs]
            gated[at, vs] = (mixture * root * head_gain * (opened * sigmoid(opened))).astype(BF16)
    half = wo_own.shape[0]
    gm = gated[:, mine_at(idx_ref, half)]
    go = gated[:, theirs_at(idx_ref, half)]
    gm_ref[...] = gm
    go_ref[...] = go
    hid_ref[...] = x_ref[...].astype(F32) + dot(gm, wo_own[...]) + dot(go, wo_oth[...])
    half = g2_own.shape[1]
    hm = hid_ref[:, mine_at(idx_ref, half)]
    ho = hid_ref[:, theirs_at(idx_ref, half)]
    square = jnp.sum(hm * hm, axis=1, keepdims=True) + jnp.sum(ho * ho, axis=1, keepdims=True)
    root = lax.rsqrt(square / (2 * half) + 1e-6)
    sm_ref[...] = (hm * root * g2_own[...].astype(F32)).astype(BF16)
    so_ref[...] = (ho * root * packed_row(pack_ref, *place_g2)).astype(BF16)


def ffn_kernel(dims, idx_ref, sm_ref, so_ref, hid_ref, e_ref, wg_own, wg_oth, wu_own, wu_oth, wd_own, wd_oth,
               out_ref, am_ref, ao_ref, g_ref, dm_ref, do_ref, gates_in, ups_in, downs_in, sems):
    seqs, span = dims
    rows, width = hid_ref.shape
    half = wd_own.shape[0]
    spots = (mine_at(idx_ref, half), theirs_at(idx_ref, half))
    copies = []
    for step in range(2):
        now = []
        for to, sources in ((gates_in, (wg_own, wg_oth)), (ups_in, (wu_own, wu_oth))):
            for which in range(2):
                now.append((sources[which].at[:, spots[step]], to.at[step, which]))
        now.append(((wd_own, wd_oth)[step], downs_in.at[step]))
        copies.append(
            [pltpu.make_async_copy(src, dst, sems.at[step, i]) for i, (src, dst) in enumerate(now)]
        )
    for step in copies:
        for one in step:
            one.start()
    sm, so, cots = sm_ref[...], so_ref[...], e_ref[...]
    for step in range(2):
        at = spots[step]
        act_ref = (am_ref, ao_ref)[step]
        for one in copies[step]:
            one.wait()
        gates = dot(sm, gates_in[step, 0]) + dot(so, gates_in[step, 1])
        ups = dot(sm, ups_in[step, 0]) + dot(so, ups_in[step, 1])
        sig = sigmoid(gates)
        opened = gates * sig
        act = (opened * ups).astype(BF16)
        act_ref[...] = act
        grads = dot_t(cots, downs_in[step])
        gate_grad = (grads * ups * sig * (1.0 + gates * (1.0 - sig))).astype(BF16)
        up_grad = (grads * opened).astype(BF16)
        g_ref[:, at] = gate_grad
        g_ref[:, pl.ds(pl.multiple_of(at.start + 2 * half, 128), half)] = up_grad
        more = dot(act, downs_in[step])
        dm = dot_t(gate_grad, gates_in[step, 0]) + dot_t(up_grad, ups_in[step, 0])
        do = dot_t(gate_grad, gates_in[step, 1]) + dot_t(up_grad, ups_in[step, 1])
        if step == 0:
            out_ref[...] = hid_ref[...] + more
            dm_ref[...] = dm
            do_ref[...] = do
        else:
            out_ref[...] += more
            dm_ref[...] += dm
            do_ref[...] += do
    for s in range(seqs):
        at = slice(s * span, (s + 1) * span)
        places = lax.broadcasted_iota(jnp.int32, (span, width), 0) + idx_ref[1] * span
        out_ref[at, :] = jnp.where(places < idx_ref[2 + s], out_ref[at, :], 0.0)


def gate_back_kernel(dims, idx_ref, hid_ref, dm_ref, do_ref, g2_own, e_ref, wo_own, wo_oth, mixture_ref,
                     og_ref, hg_own, qb_ref, tot_ref, pack_ref,
                     hg_ref, hl_ref, mg_ref, ol_ref, g2m_ref, g2o_ref, hgm_ref, hgo_ref, m0, m1, m2, m3,
                     gain, gated, gain_sum, state):
    seqs, span = dims
    half = g2_own.shape[1]
    _, place_g2, _, place_hg = packed_places(half, qb_ref.shape[1] // 2, hg_own.shape[1])
    mine, theirs = mine_at(idx_ref, half), theirs_at(idx_ref, half)
    hm, ho = hid_ref[:, mine], hid_ref[:, theirs]
    square = jnp.sum(hm * hm, axis=1, keepdims=True) + jnp.sum(ho * ho, axis=1, keepdims=True)
    root = lax.rsqrt(square / (2 * half) + 1e-6)
    dm, do = dm_ref[...], do_ref[...]
    g2m_ref[...] = jnp.sum(dm * hm * root, axis=0, keepdims=True)
    g2o_ref[...] = jnp.sum(do * ho * root, axis=0, keepdims=True)
    dm = dm * g2_own[...].astype(F32)
    do = do * packed_row(pack_ref, *place_g2)
    along = jnp.sum(dm * hm, axis=1, keepdims=True) + jnp.sum(do * ho, axis=1, keepdims=True)
    along = along * (root * root * root) / (2 * half)
    hg_ref[:, mine] = e_ref[:, mine].astype(F32) + dm * root - hm * along
    hg_ref[:, theirs] = e_ref[:, theirs].astype(F32) + do * root - ho * along
    low = hg_ref[...].astype(BF16)
    hl_ref[...] = low
    half = wo_own.shape[0]
    gated[:, mine_at(idx_ref, half)] = dot_t(low, wo_own[...])
    gated[:, theirs_at(idx_ref, half)] = dot_t(low, wo_oth[...])
    gain[:, mine_at(idx_ref, hg_own.shape[1])] = hg_own[...].astype(F32)
    gain[:, theirs_at(idx_ref, hg_own.shape[1])] = packed_row(pack_ref, *place_hg)
    head_gain = gain[...]
    wide = qb_ref.shape[1] // HEADS
    tall = mixture_ref.shape[1] // HEADS
    factor = wide ** (-0.5)
    quarter = state.shape[1]
    per = tall // quarter
    gain_grad = jnp.zeros((1, tall), F32)
    for s in range(seqs):
        at = slice(s * span, (s + 1) * span)
        for h in range(HEADS):
            vs = slice(h * tall, (h + 1) * tall)
            hs = slice(h * wide, (h + 1) * wide)
            mixture, opened, grad = mixture_ref[at, vs], og_ref[at, vs], gated[at, vs]
            root = lax.rsqrt(jnp.mean(mixture * mixture, axis=1, keepdims=True) + 1e-5)
            sig = sigmoid(opened)
            flat = mixture * root
            ol_ref[at, vs] = (grad * flat * head_gain * sig * (1.0 + opened * (1.0 - sig))).astype(BF16)
            grad = grad * (opened * sig)
            gain_grad += jnp.sum(grad * flat, axis=0, keepdims=True)
            grad = grad * head_gain
            along = jnp.mean(grad * flat, axis=1, keepdims=True)
            mixed = (grad - flat * along) * (root * factor)
            mg_ref[at, vs] = mixed
            part = t_dot(mixed.astype(BF16), qb_ref[at, hs])
            for q in range(per):
                state[s * per + q, :, hs] = part[q * quarter : (q + 1) * quarter]
    gain_sum[...] = gain_grad
    hgm_ref[...] = gain_sum[:, mine_at(idx_ref, hg_own.shape[1])]
    hgo_ref[...] = gain_sum[:, theirs_at(idx_ref, hg_own.shape[1])]
    totals = [tot_ref[pl.ds(s, 1), :] for s in range(seqs)]
    write_quarters(idx_ref, state, totals, (m0, m1, m2, m3), seqs)


def inner_back_kernel(dims, idx_ref, q_ref, k_ref, v_ref, lg_ref, a_ref, mg_ref, qb_ref, st_ref,
                      dq_ref, dk_ref, dv_ref, dc_ref):
    seqs, span = dims
    row, col = pair_iota(span)
    upto = (col <= row).astype(F32).astype(BF16)
    diagonal = row == col
    levels = level_masks(span)
    wide = q_ref.shape[1] // HEADS
    tall = v_ref.shape[1] // HEADS
    quarter = st_ref.shape[1]
    per = tall // quarter
    for s in range(seqs):
        at = slice(s * span, (s + 1) * span)
        logits = lg_ref[at, :]
        decays = (jnp.minimum(logits, 0.0) - jnp.log1p(jnp.exp(-jnp.abs(logits)))) / 16.0
        high, rest = two_part(decays)
        qs32, ks32 = q_ref[at, :].astype(F32), k_ref[at, :].astype(F32)
        begun = jnp.exp(dot(upto, high) + dot(upto, rest))
        pair_grads = []
        for h in range(HEADS):
            hs = slice(h * wide, (h + 1) * wide)
            vs = slice(h * tall, (h + 1) * tall)
            mixed, more = two_part(mg_ref[at, vs])
            values = v_ref[at, vs]
            full = dot_t(mixed, values) + dot_t(more, values)
            back = dot_t(values, mixed) + dot_t(values, more)
            pair_grads.append(jnp.where(row >= col, full, back))
            dv_ref[at, vs] = t_dot(a_ref[s * HEADS + h], mixed)
            own = jnp.sum(jnp.where(diagonal, full, 0.0), axis=1, keepdims=True)
            crossed = jnp.zeros((span, wide), F32)
            for q in range(per):
                part = slice(h * tall + q * quarter, h * tall + (q + 1) * quarter)
                crossed += dot(mg_ref[at, part].astype(BF16), st_ref[s * per + q, :, hs])
            dq_ref[at, hs] = own * ks32[:, hs] + begun[:, hs] * crossed
            dk_ref[at, hs] = own * qs32[:, hs]
            dc_ref[at, hs] = qb_ref[at, hs].astype(F32) * crossed
        for sums, _, both, half in levels:
            fade = jnp.exp(dot(sums, high) + dot(sums, rest))
            upper = upper_rows(half, qs32.shape[1], span)
            side = (jnp.where(upper, qs32, ks32) * fade).astype(BF16)
            for h in range(HEADS):
                hs = slice(h * wide, (h + 1) * wide)
                grads = dot(jnp.where(both, pair_grads[h], 0.0).astype(BF16), side[:, hs])
                moved = side[:, hs].astype(F32) * grads
                faded = fade[:, hs] * grads
                over = upper[:, hs]
                dc_ref[at, hs] += jnp.where(over, moved, -moved)
                dq_ref[at, hs] += jnp.where(over, faded, 0.0)
                dk_ref[at, hs] += jnp.where(over, 0.0, faded)


def inputs_back_kernel(dims, idx_ref, dq_ref, dk_ref, dv_ref, dc_ref, ol_ref, kd_ref, v_ref, lg_ref, tot_ref, st_ref,
                       l0, l1, l2, l3, x_ref, hg_ref, g1_own, wq_own, wq_oth, wk_own, wk_oth, wv_own, wv_oth,
                       wg_own, wg_oth, li_own, lo_own, pack_ref, g2o_ref, hgo_ref,
                       tg_ref, ga_ref, llm_ref, g1m_ref, bm_ref, small_ref,
                       leaving, logit, bias):
    seqs, span = dims
    half = g1_own.shape[1]
    rank, part = lo_own.shape
    place_g1, _, _, _ = packed_places(half, part, 0)
    li_oth, lo_oth = packed_factors(pack_ref, rank, part)
    load_state(idx_ref, (l0, l1, l2, l3), leaving)
    row, col = pair_iota(span)
    later = (col > row).astype(F32).astype(BF16)
    since = (col >= row).astype(F32).astype(BF16)
    before = (col < row).astype(F32).astype(BF16)
    keys = kd_ref.shape[1]
    vals = v_ref.shape[1]
    wide, tall = keys // HEADS, vals // HEADS
    quarter = st_ref.shape[1]
    per = tall // quarter
    bias_sum = jnp.zeros((1, keys), F32)
    for s in range(seqs):
        at = slice(s * span, (s + 1) * span)
        logits = lg_ref[at, :]
        decays = (jnp.minimum(logits, 0.0) - jnp.log1p(jnp.exp(-jnp.abs(logits)))) / 16.0
        ahead = jnp.exp(mask_dot(later, decays))
        for h in range(HEADS):
            hs = slice(h * wide, (h + 1) * wide)
            faded = kd_ref[at, hs]
            grads = jnp.zeros((span, wide), F32)
            ends = jnp.zeros((1, wide), F32)
            for q in range(per):
                vs = slice(h * tall + q * quarter, h * tall + (q + 1) * quarter)
                at_v = slice(keys * 2 + vs.start, keys * 2 + vs.stop)
                part = leaving[s * per + q, :, hs]
                ga_ref[at, at_v] = (dv_ref[at, vs] + dot_t(faded, part)).astype(BF16)
                grads += dot(v_ref[at, vs], part)
                ends += jnp.sum(
                    st_ref[s * per + q, :, hs].astype(F32) * part.astype(F32), axis=0, keepdims=True
                )
            moved = faded.astype(F32) * grads
            ga_ref[at, keys + h * wide : keys + (h + 1) * wide] = (
                dk_ref[at, hs] + ahead[:, hs] * grads
            ).astype(BF16)
            decay_grad = (
                mask_dot(since, dc_ref[at, hs])
                + mask_dot(before, moved)
                + tot_ref[pl.ds(s, 1), hs] * ends
            )
            logit_grad = decay_grad * sigmoid(-logits[:, hs]) / 16.0
            bias[:, hs] = jnp.sum(logit_grad, axis=0, keepdims=True)
            logit[at, hs] = logit_grad.astype(BF16)
        bias_sum += bias[...]
    bias[...] = bias_sum
    part = lo_own.shape[1]
    bm_ref[...] = bias[:, mine_at(idx_ref, part)]
    small_ref[:, 2 * half : 2 * half + part] = bias[:, theirs_at(idx_ref, part)]
    small_ref[:, half : 2 * half] = g2o_ref[...]
    small_ref[:, 2 * half + part :] = hgo_ref[...]
    ga_ref[:, 0:keys] = dq_ref[...].astype(BF16)
    ga_ref[:, 2 * keys + vals : 2 * keys + 2 * vals] = ol_ref[...]
    llm, llo = logit[:, mine_at(idx_ref, part)], logit[:, theirs_at(idx_ref, part)]
    llm_ref[...] = llm
    lrg = (dot_t(llm, lo_own[...]) + dot_t(llo, lo_oth)).astype(BF16)
    rest = jnp.zeros((lrg.shape[0], 128 - rank), BF16)
    lanes = 2 * keys + 2 * vals + 128
    ga_ref[:, lanes - 128 : lanes] = jnp.concatenate([lrg, rest], axis=1)
    ga_ref[:, lanes:] = llo
    qg, kg = ga_ref[:, 0:keys], ga_ref[:, keys : 2 * keys]
    vg = ga_ref[:, 2 * keys : 2 * keys + vals]
    og = ga_ref[:, 2 * keys + vals : 2 * keys + 2 * vals]
    dm = dot_t(qg, wq_own[...]) + dot_t(kg, wk_own[...]) + dot_t(vg, wv_own[...])
    dm = dm + dot_t(og, wg_own[...]) + dot_t(lrg, li_own[...])
    do = dot_t(qg, wq_oth[...]) + dot_t(kg, wk_oth[...]) + dot_t(vg, wv_oth[...])
    do = do + dot_t(og, wg_oth[...]) + dot_t(lrg, li_oth)
    mine, theirs = mine_at(idx_ref, half), theirs_at(idx_ref, half)
    xm, xo = x_ref[:, mine].astype(F32), x_ref[:, theirs].astype(F32)
    square = jnp.sum(xm * xm, axis=1, keepdims=True) + jnp.sum(xo * xo, axis=1, keepdims=True)
    root = lax.rsqrt(square / (2 * half) + 1e-6)
    g1m_ref[...] = jnp.sum(dm * xm * root, axis=0, keepdims=True)
    small_ref[:, 0:half] = jnp.sum(do * xo * root, axis=0, keepdims=True)
    dm = dm * g1_own[...].astype(F32)
    do = do * packed_row(pack_ref, *place_g1)
    along = jnp.sum(dm * xm, axis=1, keepdims=True) + jnp.sum(do * xo, axis=1, keepdims=True)
    along = along * (root * root * root) / (2 * half)
    tg_ref[:, mine] = hg_ref[:, mine] + dm * root - xm * along
    tg_ref[:, theirs] = hg_ref[:, theirs] + do * root - xo * along


def block_of(position, order):
    block = 0
    for at, bit in enumerate(order):
        if (position >> (3 - at)) & 1:
            block |= bit
    return block


def deal(position, keep_ref, send_ref):
    return keep_ref.at[position] if position < 8 else send_ref.at[position - 8]


def wide_grad_kernel(orders, idx_ref, lm_ref, lo_ref, gm_ref, go_ref, k0, s0, k1, s1, full):
    place = lax.rem(idx_ref[1], 16)
    width = full.shape[1]
    high = full.shape[0] // 16
    for which, refs in enumerate(((k0, s0), (k1, s1))):
        cols = slice(which * width, (which + 1) * width)
        full[...] = t_dot(lm_ref[...], gm_ref[:, cols]) + t_dot(lo_ref[...], go_ref[:, cols])
        for position in range(16):
            block = block_of(position, orders[which]) ^ place
            rows = full[pl.ds(pl.multiple_of(block * high, high), high), :].astype(BF16)
            to = deal(position, *refs)
            for tile in range(width // 128):
                to[tile * high : (tile + 1) * high, :] = rows[:, tile * 128 : (tile + 1) * 128]


def down_grad_kernel(order, idx_ref, lm_ref, lo_ref, gm_ref, go_ref, keep_ref, send_ref, full):
    place = lax.rem(idx_ref[1], 16)
    full[...] = t_dot(lm_ref[...], gm_ref[...]) + t_dot(lo_ref[...], go_ref[...])
    high = full.shape[0] // 2
    for position in range(16):
        block = block_of(position, order) ^ place
        rows = pl.ds(pl.multiple_of(lax.div(block, 8) * high, 16), high)
        cols = pl.ds(pl.multiple_of(lax.rem(block, 8) * 128, 128), 128)
        deal(position, keep_ref, send_ref)[...] = full[rows, cols].astype(BF16)


def attention_grad_kernel(orders, cuts, idx_ref, nm_ref, no_ref, gm_ref, go_ref, am_ref, ao_ref, hm_ref, ho_ref,
                          lrm_ref, lro_ref, llm_ref, g1_ref, g2_ref, b_ref, hg_ref, small_ref, k0, s0, k1, s1, k2, s2, full, outer, small):
    place = lax.rem(idx_ref[1], 16)
    lanes = full.shape[1]
    full[...] = t_dot(nm_ref[...], gm_ref[:, 0:lanes]) + t_dot(no_ref[...], go_ref[:, 0:lanes])
    outer[...] = t_dot(am_ref[...], hm_ref[...]) + t_dot(ao_ref[...], ho_ref[...])
    low_out = t_dot(lrm_ref[...], llm_ref[...]) + t_dot(lro_ref[...], go_ref[:, lanes:])
    small[...] = jnp.zeros_like(small)
    small[0] = low_out[:, 0:128]
    small[1] = low_out[:, 128:256]
    line = 0
    for ref in (g1_ref, g2_ref, b_ref, hg_ref):
        row = ref[...] + small_ref[:, line * 128 : line * 128 + ref.shape[1]]
        for tile in range(row.shape[1] // 128):
            small[2, line : line + 1, :] = row[:, tile * 128 : (tile + 1) * 128]
            line += 1
    high = full.shape[0] // 16
    tiles = full.shape[1] // 128
    for which, refs in enumerate(((k0, s0), (k1, s1), (k2, s2))):
        first, last = cuts[which], cuts[which + 1]
        for position in range(16):
            block = block_of(position, orders[which]) ^ place
            at = pl.ds(pl.multiple_of(block * high, high), high)
            to = deal(position, *refs)
            for tile in range(first, last):
                if tile < tiles:
                    rows = full[at, tile * 128 : (tile + 1) * 128]
                else:
                    rows = outer[at, (tile - tiles) * 128 : (tile - tiles + 1) * 128]
                to[(tile - first) * high : (tile - first + 1) * high, :] = rows.astype(BF16)
            if which == 2:
                to[(last - first) * high :, :] = small[block].astype(BF16)


def wide_open_kernel(order, idx_ref, own_ref, got_ref, out_ref):
    place = lax.rem(idx_ref[1], 16)
    high = out_ref.shape[0] // 16
    for position in range(16):
        block = block_of(position, order) ^ place
        held = deal(position, own_ref, got_ref)
        at = pl.ds(pl.multiple_of(block * high, high), high)
        for tile in range(out_ref.shape[1] // 128):
            out_ref[at, tile * 128 : (tile + 1) * 128] = held[tile * high : (tile + 1) * high, :].astype(F32)


def down_open_kernel(order, idx_ref, own_ref, got_ref, out_ref):
    place = lax.rem(idx_ref[1], 16)
    high = out_ref.shape[0] // 2
    for position in range(16):
        block = block_of(position, order) ^ place
        rows = pl.ds(pl.multiple_of(lax.div(block, 8) * high, 16), high)
        cols = pl.ds(pl.multiple_of(lax.rem(block, 8) * 128, 128), 128)
        out_ref[rows, cols] = deal(position, own_ref, got_ref)[...].astype(F32)


def attention_open_kernel(orders, cuts, idx_ref, o0, r0, o1, r1, o2, r2, q_ref, k_ref, v_ref, og_ref, li_ref, w_ref,
                          lo_ref, g1_ref, g2_ref, b_ref, hg_ref, small):
    place = lax.rem(idx_ref[1], 16)
    high = q_ref.shape[0] // 16
    homes = []
    for ref in (q_ref, k_ref, v_ref, og_ref):
        homes += [(ref, tile) for tile in range(ref.shape[1] // 128)]
    homes.append((li_ref, None))
    homes += [(w_ref, tile) for tile in range(w_ref.shape[1] // 128)]
    for which, refs in enumerate(((o0, r0), (o1, r1), (o2, r2))):
        first, last = cuts[which], cuts[which + 1]
        for position in range(16):
            block = block_of(position, orders[which]) ^ place
            at = pl.ds(pl.multiple_of(block * high, high), high)
            held = deal(position, *refs)
            for tile in range(first, last):
                rows = held[(tile - first) * high : (tile - first + 1) * high, :].astype(F32)
                ref, column = homes[tile]
                if column is None:
                    ref[at, :] = rows[:, : ref.shape[1]]
                else:
                    ref[at, column * 128 : (column + 1) * 128] = rows
            if which == 2:
                small[block] = held[(last - first) * high :, :].astype(F32)
    lo_ref[:, 0:128] = small[0]
    lo_ref[:, 128:256] = small[1]
    line = 0
    for ref in (g1_ref, g2_ref, b_ref, hg_ref):
        for tile in range(ref.shape[1] // 128):
            ref[:, tile * 128 : (tile + 1) * 128] = small[2, line : line + 1, :]
            line += 1


def across(array):
    return lax.ppermute(array, "fsdp", ((0, 1), (1, 0)))


def swap(array, bit):
    count = lax.axis_size("seq")
    return lax.ppermute(array, "seq", tuple((one, one ^ bit) for one in range(count)))


def ahead(array, step):
    count = lax.axis_size("seq")
    return lax.ppermute(
        array,
        "seq",
        tuple((one, one + step) for one in range(count) if 0 <= one + step < count),
    )


def fence(*groups):
    return lax.optimization_barrier(groups)


class Portions:
    def __init__(self, parts, orders):
        self.kept = [keep for keep, _ in parts]
        self.sent = [send for _, send in parts]
        self.orders = orders

    def move(self, arrays, step):
        if step < 3:
            return [swap(a, order[step]) for a, order in zip(arrays, self.orders)]
        return self.move_all(arrays, self.orders[0][3])

    def move_all(self, arrays, bit):
        got = swap(jnp.concatenate(arrays, axis=1), bit)
        ends = [0]
        for a in arrays:
            ends.append(ends[-1] + a.shape[1])
        return [got[:, first:last] for first, last in zip(ends[:-1], ends[1:])]

    def reduce_start(self, step):
        return self.move(self.sent, step)

    def reduce_end(self, step, got):
        for one, more in enumerate(got):
            if step < 3:
                half = more.shape[0] // 2
                self.sent[one] = self.kept[one][half:] + more[half:]
                self.kept[one] = self.kept[one][:half] + more[:half]
            else:
                self.kept[one] = self.kept[one] + more
        bit = 16
        while step == 3 and bit < lax.axis_size("seq"):
            more = self.move_all(self.kept, bit)
            self.kept = [k + m for k, m in zip(self.kept, more)]
            bit *= 2

    def gather_start(self, step):
        return self.move(self.kept, step)

    def gather_end(self, step, got):
        if step:
            self.kept = [jnp.concatenate([k, more], axis=0) for k, more in zip(self.kept, got)]
        else:
            self.halves = list(zip(self.kept, got))


def scan_near(messages):
    return [messages[0]] + [swap(messages[o], o) for o in (1, 2, 3)]


def scan_scratch(messages):
    rows, lanes = messages[0].shape
    return [((4, rows - 16, lanes), F32), ((4, 1, lanes), F32)]


def scan_total(near, idx, reverse):
    return call("group_total", partial(group_total, reverse), idx, near, [(near[0].shape, BF16)], scan_scratch(near))[0]


def scan_far(total, reverse):
    sign = -4 if reverse else 4
    return [ahead(total, sign * step) for step in range(1, lax.axis_size("seq") // 4)]


def scan_entering(far, near, idx, reverse):
    rows, lanes = near[0].shape
    return call(
        "group_entering", partial(group_entering, reverse, len(far)), idx, list(far) + list(near),
        [((rows - 16, lanes), BF16)] * 4, scan_scratch(near) + [((4, rows - 16, lanes), F32)],
    )


def shards(
    tokens,
    lengths,
    first_gain,
    query_weight,
    key_weight,
    value_weight,
    outgate_weight,
    lowrank_in,
    lowrank_out,
    decay_bias,
    head_gain,
    output_weight,
    second_gain,
    gate_weight,
    up_weight,
    down_weight,
    cotangent,
):
    micro_count, pair_count, span, width = tokens.shape
    seqs = micro_count * pair_count
    rows = seqs * span
    dims = (seqs, span)
    core = lax.axis_index("fsdp")
    place = lax.axis_index("seq")
    own_lengths = lax.dynamic_slice_in_dim(lengths, core * pair_count, pair_count, 1).reshape(-1)
    idx = jnp.concatenate([jnp.stack([core, place]).astype(jnp.int32), own_lengths])
    keys, vals, ff = query_weight.shape[1], value_weight.shape[1], gate_weight.shape[1]
    half = query_weight.shape[0]
    tall = vals // HEADS
    quarter = seqs * tall // 4

    x = tokens.reshape(rows, width)
    cot = cotangent.reshape(rows, width)
    first_gain, decay_bias, head_gain, second_gain = (
        a.reshape(1, -1) for a in (first_gain, decay_bias, head_gain, second_gain)
    )
    lrank = lowrank_in.shape[1]
    pack = call(
        "pack", pack_kernel, idx, [lowrank_in, lowrank_out, first_gain, second_gain, decay_bias, head_gain],
        [((half + lrank * lowrank_out.shape[1] // 128 + 16, 128), BF16)],
    )[0]
    pack2, wk2, wv2, wq2 = (across(a) for a in (pack, key_weight, value_weight, query_weight))

    message = ((quarter + 16, keys), BF16)
    state = ((4, quarter, keys), F32)
    nm, no, k, v, lr, lg, kd, tot, cots, *messages = call(
        "keys", partial(keys_kernel, dims), idx,
        [x, cot, first_gain, key_weight, wk2, value_weight, wv2, lowrank_in, lowrank_out, decay_bias, pack2],
        [((rows, half), BF16), ((rows, half), BF16), ((rows, keys), BF16), ((rows, vals), BF16),
         ((rows, lrank), BF16), ((rows, keys), F32), ((rows, keys), BF16), ((seqs, keys), F32), ((rows, width), BF16)]
        + [message] * 4,
        [state], flops=2 * rows * width * (keys + vals) + 4 * rows * span * keys,
    )
    messages, outgate_send = fence(messages, outgate_weight)
    near = scan_near(messages)
    wg2, cots2 = across(outgate_send), across(cots)
    near, gate_send, up_send = fence(near, gate_weight, up_weight)
    total = scan_total(near, idx, False)
    total, gate_send, up_send = fence(total, gate_send, up_send)
    far = scan_far(total, False)
    wgate2, wup2 = across(gate_send), across(up_send)
    q, og, mix, scores, qb = call(
        "inner", partial(inner_kernel, dims), idx,
        [nm, no, query_weight, wq2, outgate_weight, wg2, k, v, lg],
        [((rows, keys), BF16), ((rows, vals), F32), ((rows, vals), F32), ((seqs * HEADS, span, span), BF16),
         ((rows, keys), BF16)],
        flops=2 * rows * width * (keys + vals) + 60 * rows * span * keys,
    )
    far, mix = fence(far, mix)
    pieces = scan_entering(far, near, idx, False)
    pieces, output_send, down_send = fence(pieces, output_weight, down_weight)
    pieces = [pieces[0]] + [swap(pieces[o], o) for o in (1, 2, 3)]
    wo2, wdown2 = across(output_send), across(down_send)
    mixture, gm, go, hid, sm, so, st = call(
        "hidden", partial(hidden_kernel, dims), idx,
        [mix, qb, *pieces, og, head_gain, x, output_weight, wo2, second_gain, pack2],
        [((rows, vals), F32), ((rows, vals // 2), BF16), ((rows, vals // 2), BF16), ((rows, width), F32),
         ((rows, half), BF16), ((rows, half), BF16), ((4, quarter, keys), BF16)],
        [((1, tall), F32), ((rows, vals), BF16)], flops=2 * rows * vals * width,
    )
    so, no_send, lr_send = fence(so, no, lr)
    so2, no2, go2, lr2 = across(so), across(no_send), across(go), across(lr_send)
    out, am, ao, gu, dm, do = call(
        "ffn", partial(ffn_kernel, dims), idx,
        [sm, so, hid, cots, gate_weight, wgate2, up_weight, wup2, down_weight, wdown2],
        [((rows, width), F32), ((rows, ff // 2), BF16), ((rows, ff // 2), BF16),
         ((rows, 2 * ff), BF16), ((rows, half), F32), ((rows, half), F32)],
        [((2, 2, half, ff // 2), BF16), ((2, 2, half, ff // 2), BF16), ((2, ff // 2, width), BF16),
         pltpu.SemaphoreType.DMA((2, 5))],
        flops=12 * rows * width * ff, limit=52, far=6,
    )
    so2, no2, go2, lr2, gu, dm, ao = fence(so2, no2, go2, lr2, gu, dm, ao)

    orders = ((1, 2, 4, 8), (2, 4, 1, 8), (4, 1, 2, 8))
    ao2, gu2 = across(ao), across(gu)
    hg, hl, mg, ol, g2m, g2o, hgm, hgo, *messages = call(
        "gate_back", partial(gate_back_kernel, dims), idx,
        [hid, dm, do, second_gain, cots, output_weight, wo2, mixture, og, head_gain, qb, tot, pack2],
        [((rows, width), F32), ((rows, width), BF16), ((rows, vals), F32), ((rows, vals), BF16),
         ((1, half), F32), ((1, half), F32), ((1, tall // 2), F32), ((1, tall // 2), F32)] + [message] * 4,
        [((1, tall), F32), ((rows, vals), F32), ((1, tall), F32), state],
        flops=2 * rows * width * vals + 4 * rows * span * keys,
    )
    messages, ao2, gu2 = fence(messages, ao2, gu2)
    near = scan_near(messages)
    portion = ff // 128 * (half // 16)
    flat = [((8, portion, 128), BF16)] * 2
    down_parts = call("down_grad", partial(down_grad_kernel, orders[2]), idx, [am, ao2, cots, cots2], flat,
                      [((ff // 2, width), F32)], flops=2 * rows * ff * width)
    wide_parts = call("wide_grad", partial(wide_grad_kernel, orders), idx, [sm, so2, gu, gu2], flat * 2,
                      [((half, ff), F32)], flops=4 * rows * ff * width, limit=40)
    near, wide_parts = fence(near, wide_parts)
    first = Portions([wide_parts[0:2], wide_parts[2:4], down_parts], orders)

    got = first.reduce_start(0)
    total = scan_total(near, idx, True)
    far = scan_far(total, True)
    dq, dk, dv, dc = call(
        "inner_back", partial(inner_back_kernel, dims), idx, [q, k, v, lg, scores, mg, qb, st],
        [((rows, keys), F32), ((rows, keys), F32), ((rows, vals), F32), ((rows, keys), F32)],
        flops=100 * rows * span * keys,
    )
    far, dq = fence(far, dq)
    pieces = scan_entering(far, near, idx, True)
    pieces = [pieces[0]] + [swap(pieces[o], o) for o in (1, 2, 3)]
    got, pieces = fence(got, pieces)
    first.reduce_end(0, got)
    first.sent, pieces = fence(first.sent, pieces)
    got = first.reduce_start(1)
    lanes = 2 * keys + 2 * vals + 128
    tg, ga, llm, g1m, bm, small = call(
        "inputs_back", partial(inputs_back_kernel, dims), idx,
        [dq, dk, dv, dc, ol, kd, v, lg, tot, st, *pieces, x, hg, first_gain, query_weight, wq2, key_weight, wk2,
         value_weight, wv2, outgate_weight, wg2, lowrank_in, lowrank_out, pack2, g2o, hgo],
        [((rows, width), F32), ((rows, lanes + keys // 2), BF16), ((rows, keys // 2), BF16),
         ((1, half), F32), ((1, keys // 2), F32), ((1, 2 * half + keys // 2 + tall // 2), F32)],
        [((4, quarter, keys), BF16), ((rows, keys), BF16), ((1, keys), F32)],
        flops=2 * rows * width * lanes + 8 * rows * span * keys, limit=40,
    )
    ga2, small2 = across(ga), across(small)
    got, ga2, small2 = fence(got, ga2, small2)
    first.reduce_end(1, got)
    got = first.reduce_start(2)
    hl2 = across(hl)
    tiles = lanes // 128 + width // 128
    cuts = (0, tiles // 3, 2 * tiles // 3, tiles)
    high = half // 16
    shapes = []
    for which in range(3):
        size = (cuts[which + 1] - cuts[which]) * high + (16 if which == 2 else 0)
        shapes += [((8, size, 128), BF16)] * 2
    parts = call(
        "attention_grad", partial(attention_grad_kernel, orders, cuts), idx,
        [nm, no2, ga, ga2, gm, go2, hl, hl2, lr, lr2, llm, g1m, g2m, bm, hgm, small2],
        shapes, [((half, lanes), F32), ((vals // 2, width), F32), ((16, 16, 128), F32)],
        flops=2 * 2 * rows * (half * lanes + width * vals // 2),
    )
    got, parts = fence(got, parts)
    first.reduce_end(2, got)
    second = Portions([parts[0:2], parts[2:4], parts[4:6]], orders)
    got, more = fence(first.reduce_start(3), second.reduce_start(0))
    first.reduce_end(3, got)
    second.reduce_end(0, more)
    got, more = fence(first.gather_start(3), second.reduce_start(1))
    first.gather_end(3, got)
    second.reduce_end(1, more)
    got, more = fence(first.gather_start(2), second.reduce_start(2))
    first.gather_end(2, got)
    second.reduce_end(2, more)
    got, more = fence(first.gather_start(1), second.reduce_start(3))
    first.gather_end(1, got)
    second.reduce_end(3, more)
    got, more = fence(first.gather_start(0), second.gather_start(3))
    first.gather_end(0, got)
    second.gather_end(3, more)
    gate_halves, up_halves, down_halves = first.halves
    more = second.gather_start(2)
    gate_out = call("gate_open", partial(wide_open_kernel, orders[0]), idx, gate_halves, [((half, ff), F32)])[0]
    more, gate_out = fence(more, gate_out)
    second.gather_end(2, more)
    more = second.gather_start(1)
    up_out = call("up_open", partial(wide_open_kernel, orders[1]), idx, up_halves, [((half, ff), F32)])[0]
    more, up_out = fence(more, up_out)
    second.gather_end(1, more)
    more = second.gather_start(0)
    down_out = call("down_open", partial(down_open_kernel, orders[2]), idx, down_halves, [((ff // 2, width), F32)])[0]
    more, down_out = fence(more, down_out)
    second.gather_end(0, more)
    opened = call(
        "attention_open", partial(attention_open_kernel, orders, cuts), idx, [a for pair in second.halves for a in pair],
        [((half, keys), F32), ((half, keys), F32), ((half, vals), F32), ((half, vals), F32),
         ((half, lrank), F32), ((vals // 2, width), F32), ((lrank, keys // 2), F32),
         ((1, half), F32), ((1, half), F32), ((1, keys // 2), F32), ((1, tall // 2), F32)],
        [((16, 16, 128), F32)],
    )
    q_out, k_out, v_out, og_out, li_out, w_out, lo_out, g1_out, g2_out, b_out, hg_out = opened
    return (
        out.reshape(tokens.shape),
        tg.reshape(tokens.shape),
        g1_out.reshape(-1),
        q_out,
        k_out,
        v_out,
        og_out,
        li_out,
        lo_out,
        b_out.reshape(-1),
        hg_out.reshape(-1),
        w_out,
        g2_out.reshape(-1),
        gate_out,
        up_out,
        down_out,
    )


def solution(mesh):
    shard, column = P("fsdp", None), P(None, "fsdp")
    stream, line = P(None, "fsdp", "seq", None), P("fsdp")
    weights = (line, shard, shard, shard, shard, shard, column, line, line, shard, line, shard, shard, shard)
    return jax.shard_map(
        shards,
        mesh=mesh,
        in_specs=(stream, P()) + weights + (stream,),
        out_specs=(stream, stream) + weights,
        check_vma=False,
    )
```

```python
from functools import partial

import jax
import jax.numpy as jnp
from jax import lax
from jax.experimental import pallas as pl
from jax.experimental.pallas import tpu as pltpu
from jax.sharding import PartitionSpec as P

HEADS = 4
RANK = 16
F32 = jnp.float32
BF16 = jnp.bfloat16
MIB = 1024 * 1024


def dot(first_op, second_op):
    return jnp.dot(first_op, second_op, preferred_element_type=F32)


def dot_t(first_op, second_op):
    return lax.dot_general(
        first_op, second_op, (((1,), (1,)), ((), ())), preferred_element_type=F32
    )


def t_dot(first_op, second_op):
    return lax.dot_general(
        first_op, second_op, (((0,), (0,)), ((), ())), preferred_element_type=F32
    )


def two_part(value):
    high = value.astype(BF16)
    return high, (value - high.astype(F32)).astype(BF16)


def mask_dot(mask, value):
    high, rest = two_part(value)
    return dot(mask, high) + dot(mask, rest)


def sigmoid(value):
    return 1.0 / (1.0 + jnp.exp(-value))


def pair_iota(size):
    return (
        lax.broadcasted_iota(jnp.int32, (size, size), 0),
        lax.broadcasted_iota(jnp.int32, (size, size), 1),
    )


def level_masks(size):
    row, col = pair_iota(size)
    out = []
    half = size // 2
    while half >= 1:
        block = 2 * half
        row_block = row // block
        middle = row_block * block + half - 1
        upper = row > middle
        sums = (upper & (col > middle) & (col <= row)) | (
            jnp.logical_not(upper) & (col > row) & (col <= middle)
        )
        same = row_block == col // block
        pairs = same & upper & (col <= middle)
        both = same & (upper != (col > middle))
        out.append((sums.astype(F32).astype(BF16), pairs, both, half))
        half //= 2
    return out


def upper_rows(half, width, size):
    row = lax.broadcasted_iota(jnp.int32, (size, width), 0)
    return row % (2 * half) >= half


def seat(idx_ref):
    return idx_ref[0], idx_ref[1]


def mine_at(idx_ref, width):
    return pl.ds(pl.multiple_of(idx_ref[0] * width, 128), width)


def theirs_at(idx_ref, width):
    return pl.ds(pl.multiple_of((1 - idx_ref[0]) * width, 128), width)


SMEM = pl.BlockSpec(memory_space=pltpu.SMEM)
VMEM = pl.BlockSpec(memory_space=pltpu.VMEM)


def call(name, body, idx, inputs, outs, scratch=(), limit=24, far=0):
    shapes = [jax.ShapeDtypeStruct(s, d) for s, d in outs]
    result = pl.pallas_call(
        body,
        name=name,
        out_shape=shapes,
        in_specs=[SMEM] + [VMEM] * (len(inputs) - far) + [pl.BlockSpec(memory_space=pl.ANY)] * far,
        out_specs=[VMEM] * len(shapes),
        scratch_shapes=[pltpu.VMEM(*s) if isinstance(s, tuple) else s for s in scratch],
        compiler_params=pltpu.CompilerParams(vmem_limit_bytes=limit * MIB),
        cost_estimate=pl.CostEstimate(flops=1, bytes_accessed=1, transcendentals=0),
    )(idx, *inputs)
    return result


def put_message(ref, rows, total):
    count = rows.shape[0]
    ref[pl.ds(0, count), :] = rows.astype(BF16)
    high = total.astype(BF16)
    rest = total - high.astype(F32)
    middle = rest.astype(BF16)
    low = (rest - middle.astype(F32)).astype(BF16)
    tail = jnp.concatenate(
        [high, middle, low, jnp.zeros((13,) + total.shape[1:], BF16)], axis=0
    )
    ref[pl.ds(count, 16), :] = tail


def get_message(ref):
    count = ref.shape[0] - 16
    tail = ref[pl.ds(count, 16), :].astype(F32)
    return ref[pl.ds(0, count), :].astype(F32), tail[0:1] + tail[1:2] + tail[2:3]


def write_quarters(idx_ref, state, totals, messages, seq_count):
    low = lax.rem(idx_ref[1], 4)
    for other in range(4):
        quarter = low ^ other
        total = totals[0]
        for one in range(1, seq_count):
            total = jnp.where(quarter * seq_count // 4 >= one, totals[one], total)
        put_message(messages[other], state[quarter], total)


def group_total(reverse, idx_ref, *refs):
    out_ref, kept, held = refs[4], refs[5], refs[6]
    low = lax.rem(idx_ref[1], 4)
    for other in range(4):
        rows, total = get_message(refs[other])
        kept[low ^ other] = rows
        held[low ^ other] = total
    order = (3, 2, 1, 0) if reverse else (0, 1, 2, 3)
    rows, total = kept[order[0]], held[order[0]]
    for one in order[1:]:
        rows = held[one] * rows + kept[one]
        total = total * held[one]
    put_message(out_ref, rows, total)


def group_entering(reverse, far_count, idx_ref, *refs):
    far, near = refs[:far_count], refs[far_count : far_count + 4]
    outs = refs[far_count + 4 : far_count + 8]
    kept, held, entering = refs[far_count + 8 :]
    low = lax.rem(idx_ref[1], 4)
    for other in range(4):
        rows, total = get_message(near[other])
        kept[low ^ other] = rows
        held[low ^ other] = total
    rows = jnp.zeros(kept.shape[1:], F32)
    for one in far[::-1]:
        part, total = get_message(one)
        rows = total * rows + part
    for one in (3, 2, 1, 0) if reverse else (0, 1, 2, 3):
        entering[one] = rows
        rows = held[one] * rows + kept[one]
    for other in range(4):
        outs[other][...] = entering[low ^ other].astype(BF16)


def load_state(idx_ref, pieces, state):
    low = lax.rem(idx_ref[1], 4)
    for other in range(4):
        state[low ^ other] = pieces[other][...]


def pack_kernel(idx_ref, li_ref, lo_ref, lines_ref, out_ref):
    at = 0
    for ref in (li_ref, lo_ref):
        rank = ref.shape[0]
        for tile in range(ref.shape[1] // 128):
            out_ref[at : at + rank, :] = ref[:, tile * 128 : (tile + 1) * 128]
            at += rank
    out_ref[at:, :] = lines_ref[...]


def packed_factors(pack_ref, half):
    rank = RANK
    high = pack_ref.shape[0] - 16
    tiles = [pack_ref[at : at + rank, :] for at in range(0, high, rank)]
    first = half // 128
    return jnp.concatenate(tiles[:first], axis=1), jnp.concatenate(tiles[first:], axis=1)


def packed_row(pack_ref, first, count):
    lines = pack_ref[pack_ref.shape[0] - 16 :, :].astype(F32)
    return jnp.concatenate([lines[t : t + 1, :] for t in range(first, first + count)], axis=1)


def packed_places(half, part, gain):
    g1, b, hg = half // 128, part // 128, gain // 128
    return (0, g1), (g1, g1), (2 * g1, b), (2 * g1 + b, hg)


def keys_kernel(dims, idx_ref, x_ref, cot_ref, wk_own, wk_oth, wv_own, wv_oth, own_ref, pack_ref,
                nm_ref, no_ref, k_ref, v_ref, lr_ref, lg_ref, kd_ref, tot_ref, e_ref,
                m0, m1, m2, m3, state):
    seqs, span = dims
    half = wk_own.shape[0]
    part = wk_own.shape[1] // 2
    place_g1, _, place_b, _ = packed_places(half, part, 0)
    li_own, lo_own = packed_factors(own_ref, half)
    li_oth, lo_oth = packed_factors(pack_ref, half)
    g1_own, b_own = packed_row(own_ref, *place_g1), packed_row(own_ref, *place_b)
    g1_oth, b_oth = packed_row(pack_ref, *place_g1), packed_row(pack_ref, *place_b)
    for s in range(seqs):
        at = slice(s * span, (s + 1) * span)
        places = lax.broadcasted_iota(jnp.int32, (span, cot_ref.shape[1]), 0) + idx_ref[1] * span
        e_ref[at, :] = jnp.where(places < idx_ref[2 + s], cot_ref[at, :].astype(F32), 0.0).astype(BF16)
    xm = x_ref[:, mine_at(idx_ref, half)].astype(F32)
    xo = x_ref[:, theirs_at(idx_ref, half)].astype(F32)
    square = jnp.sum(xm * xm, axis=1, keepdims=True) + jnp.sum(xo * xo, axis=1, keepdims=True)
    root = lax.rsqrt(square / (2 * half) + 1e-6)
    nm = (xm * root * g1_own).astype(BF16)
    no = (xo * root * g1_oth).astype(BF16)
    nm_ref[...] = nm
    no_ref[...] = no
    lr = (dot_t(nm, li_own) + dot_t(no, li_oth)).astype(BF16)
    lr_ref[...] = lr
    lg_ref[:, mine_at(idx_ref, part)] = dot(lr, lo_own) + b_own
    lg_ref[:, theirs_at(idx_ref, part)] = dot(lr, lo_oth) + b_oth
    keys = (dot(nm, wk_own[...]) + dot(no, wk_oth[...])).astype(BF16)
    k_ref[...] = keys
    values = (dot(nm, wv_own[...]) + dot(no, wv_oth[...])).astype(BF16)
    v_ref[...] = values
    row, col = pair_iota(span)
    later = (col > row).astype(F32).astype(BF16)
    wide = keys.shape[1] // HEADS
    tall = values.shape[1] // HEADS
    quarter = state.shape[1]
    totals = []
    for s in range(seqs):
        at = slice(s * span, (s + 1) * span)
        logits = lg_ref[at, :]
        decays = (jnp.minimum(logits, 0.0) - jnp.log1p(jnp.exp(-jnp.abs(logits)))) / 16.0
        ahead = mask_dot(later, decays)
        totals.append(jnp.exp(jnp.sum(decays, axis=0, keepdims=True)))
        tot_ref[pl.ds(s, 1), :] = totals[s]
        faded = (keys[at].astype(F32) * jnp.exp(ahead)).astype(BF16)
        kd_ref[at, :] = faded
        for h in range(HEADS):
            part = t_dot(values[at, h * tall : (h + 1) * tall], faded[:, h * wide : (h + 1) * wide])
            per = tall // quarter
            for q in range(per):
                state[s * per + q, :, h * wide : (h + 1) * wide] = part[q * quarter : (q + 1) * quarter]
    write_quarters(idx_ref, state, totals, (m0, m1, m2, m3), seqs)


def inner_kernel(dims, idx_ref, nm_ref, no_ref, wq_own, wq_oth, wg_own, wg_oth, k_ref, v_ref, lg_ref,
                 q_ref, og_ref, mix_ref, a_ref, qb_ref):
    seqs, span = dims
    nm, no = nm_ref[...], no_ref[...]
    queries = (dot(nm, wq_own[...]) + dot(no, wq_oth[...])).astype(BF16)
    q_ref[...] = queries
    og_ref[...] = dot(nm, wg_own[...]) + dot(no, wg_oth[...])
    row, col = pair_iota(span)
    upto = (col <= row).astype(F32).astype(BF16)
    diagonal = row == col
    levels = level_masks(span)
    wide = queries.shape[1] // HEADS
    tall = v_ref.shape[1] // HEADS
    for s in range(seqs):
        at = slice(s * span, (s + 1) * span)
        logits = lg_ref[at, :]
        decays = (jnp.minimum(logits, 0.0) - jnp.log1p(jnp.exp(-jnp.abs(logits)))) / 16.0
        high, rest = two_part(decays)
        qs, ks = queries[at], k_ref[at, :]
        qs32, ks32 = qs.astype(F32), ks.astype(F32)
        qb_ref[at, :] = (qs32 * jnp.exp(dot(upto, high) + dot(upto, rest))).astype(BF16)
        scores = []
        for h in range(HEADS):
            hs = slice(h * wide, (h + 1) * wide)
            scores.append(jnp.where(diagonal, dot_t(qs[:, hs], ks[:, hs]), 0.0))
        for sums, pairs, _, half in levels:
            fade = jnp.exp(dot(sums, high) + dot(sums, rest))
            side = (jnp.where(upper_rows(half, qs.shape[1], span), qs32, ks32) * fade).astype(BF16)
            for h in range(HEADS):
                part = side[:, h * wide : (h + 1) * wide]
                scores[h] = scores[h] + jnp.where(pairs, dot_t(part, part), 0.0)
        for h in range(HEADS):
            low = scores[h].astype(BF16)
            a_ref[s * HEADS + h] = low
            vs = slice(h * tall, (h + 1) * tall)
            mix_ref[at, vs] = dot(low, v_ref[at, vs])


def hidden_kernel(dims, idx_ref, mix_ref, qb_ref, e0, e1, e2, e3, og_ref, x_ref, wo_own, wo_oth,
                  own_ref, pack_ref, mixture_ref, gm_ref, go_ref, hid_ref, sm_ref, so_ref, st_ref,
                  gain, gated):
    seqs, span = dims
    load_state(idx_ref, (e0, e1, e2, e3), st_ref)
    half = sm_ref.shape[1]
    gain_half = gain.shape[1] // 2
    _, place_g2, _, place_hg = packed_places(half, qb_ref.shape[1] // 2, gain_half)
    gain[:, mine_at(idx_ref, gain_half)] = packed_row(own_ref, *place_hg)
    gain[:, theirs_at(idx_ref, gain_half)] = packed_row(pack_ref, *place_hg)
    wide = qb_ref.shape[1] // HEADS
    tall = mix_ref.shape[1] // HEADS
    factor = wide ** (-0.5)
    quarter = st_ref.shape[1]
    per = tall // quarter
    head_gain = gain[...]
    for s in range(seqs):
        at = slice(s * span, (s + 1) * span)
        for h in range(HEADS):
            hs = slice(h * wide, (h + 1) * wide)
            for q in range(per):
                vs = slice(h * tall + q * quarter, h * tall + (q + 1) * quarter)
                carried = dot_t(qb_ref[at, hs], st_ref[s * per + q, :, hs])
                mixture_ref[at, vs] = (mix_ref[at, vs] + carried) * factor
            vs = slice(h * tall, (h + 1) * tall)
            mixture = mixture_ref[at, vs]
            root = lax.rsqrt(jnp.mean(mixture * mixture, axis=1, keepdims=True) + 1e-5)
            opened = og_ref[at, vs]
            gated[at, vs] = (mixture * root * head_gain * (opened * sigmoid(opened))).astype(BF16)
    half = wo_own.shape[0]
    gm = gated[:, mine_at(idx_ref, half)]
    go = gated[:, theirs_at(idx_ref, half)]
    gm_ref[...] = gm
    go_ref[...] = go
    hid_ref[...] = x_ref[...].astype(F32) + dot(gm, wo_own[...]) + dot(go, wo_oth[...])
    half = sm_ref.shape[1]
    hm = hid_ref[:, mine_at(idx_ref, half)]
    ho = hid_ref[:, theirs_at(idx_ref, half)]
    square = jnp.sum(hm * hm, axis=1, keepdims=True) + jnp.sum(ho * ho, axis=1, keepdims=True)
    root = lax.rsqrt(square / (2 * half) + 1e-6)
    sm_ref[...] = (hm * root * packed_row(own_ref, *place_g2)).astype(BF16)
    so_ref[...] = (ho * root * packed_row(pack_ref, *place_g2)).astype(BF16)


def ffn_kernel(dims, idx_ref, sm_ref, so_ref, hid_ref, e_ref, wg_own, wg_oth, wu_own, wu_oth, wd_own, wd_oth,
               out_ref, am_ref, ao_ref, g_ref, dm_ref, do_ref, gates_in, ups_in, downs_in, sems):
    seqs, span = dims
    half = wd_own.shape[0]
    spots = (mine_at(idx_ref, half), theirs_at(idx_ref, half))
    cut = half // 256 * 128 + 128
    steps = []
    for side in range(2):
        for first, last in ((0, cut), (cut, half)):
            to_at = pl.ds(first, last - first)
            from_at = pl.ds(pl.multiple_of(spots[side].start + first, 128), last - first)
            now = []
            for to, sources in ((gates_in, (wg_own, wg_oth)), (ups_in, (wu_own, wu_oth))):
                for which in range(2):
                    now.append((sources[which].at[:, from_at], to.at[which, side, :, to_at]))
            now.append(((wd_own, wd_oth)[side].at[to_at, :], downs_in.at[side, to_at, :]))
            copies = [
                pltpu.make_async_copy(src, dst, sems.at[len(steps), i])
                for i, (src, dst) in enumerate(now)
            ]
            for one in copies:
                one.start()
            steps.append((side, first, last, copies))
    sm, so, cots = sm_ref[...], so_ref[...], e_ref[...]
    for side, first, last, copies in steps:
        size = last - first
        for one in copies:
            one.wait()
        g_own, g_oth = gates_in[0, side, :, first:last], gates_in[1, side, :, first:last]
        u_own, u_oth = ups_in[0, side, :, first:last], ups_in[1, side, :, first:last]
        down = downs_in[side, first:last, :]
        gates = dot(sm, g_own) + dot(so, g_oth)
        ups = dot(sm, u_own) + dot(so, u_oth)
        sig = sigmoid(gates)
        opened = gates * sig
        act = (opened * ups).astype(BF16)
        (am_ref, ao_ref)[side][:, first:last] = act
        grads = dot_t(cots, down)
        gate_grad = (grads * ups * sig * (1.0 + gates * (1.0 - sig))).astype(BF16)
        up_grad = (grads * opened).astype(BF16)
        at = spots[side].start + first
        g_ref[:, pl.ds(pl.multiple_of(at, 128), size)] = gate_grad
        g_ref[:, pl.ds(pl.multiple_of(at + 2 * half, 128), size)] = up_grad
        more = dot(act, down)
        dm = dot_t(gate_grad, g_own) + dot_t(up_grad, u_own)
        do = dot_t(gate_grad, g_oth) + dot_t(up_grad, u_oth)
        if side == 0 and first == 0:
            out_ref[...] = hid_ref[...] + more
            dm_ref[...] = dm
            do_ref[...] = do
        else:
            out_ref[...] += more
            dm_ref[...] += dm
            do_ref[...] += do
    width = out_ref.shape[1]
    for s in range(seqs):
        at = slice(s * span, (s + 1) * span)
        places = lax.broadcasted_iota(jnp.int32, (span, width), 0) + idx_ref[1] * span
        out_ref[at, :] = jnp.where(places < idx_ref[2 + s], out_ref[at, :], 0.0)


def gate_back_kernel(dims, idx_ref, hid_ref, dm_ref, do_ref, e_ref, wo_own, wo_oth, mixture_ref,
                     og_ref, qb_ref, tot_ref, own_ref, pack_ref,
                     hg_ref, hl_ref, mg_ref, ol_ref, g2m_ref, g2o_ref, hgm_ref, hgo_ref, m0, m1, m2, m3,
                     gain, gated, gain_sum, state):
    seqs, span = dims
    half = dm_ref.shape[1]
    gain_half = gain.shape[1] // 2
    _, place_g2, _, place_hg = packed_places(half, qb_ref.shape[1] // 2, gain_half)
    mine, theirs = mine_at(idx_ref, half), theirs_at(idx_ref, half)
    hm, ho = hid_ref[:, mine], hid_ref[:, theirs]
    square = jnp.sum(hm * hm, axis=1, keepdims=True) + jnp.sum(ho * ho, axis=1, keepdims=True)
    root = lax.rsqrt(square / (2 * half) + 1e-6)
    dm, do = dm_ref[...], do_ref[...]
    g2m_ref[...] = jnp.sum(dm * hm * root, axis=0, keepdims=True)
    g2o_ref[...] = jnp.sum(do * ho * root, axis=0, keepdims=True)
    dm = dm * packed_row(own_ref, *place_g2)
    do = do * packed_row(pack_ref, *place_g2)
    along = jnp.sum(dm * hm, axis=1, keepdims=True) + jnp.sum(do * ho, axis=1, keepdims=True)
    along = along * (root * root * root) / (2 * half)
    hg_ref[:, mine] = e_ref[:, mine].astype(F32) + dm * root - hm * along
    hg_ref[:, theirs] = e_ref[:, theirs].astype(F32) + do * root - ho * along
    low = hg_ref[...].astype(BF16)
    hl_ref[...] = low
    half = wo_own.shape[0]
    gated[:, mine_at(idx_ref, half)] = dot_t(low, wo_own[...])
    gated[:, theirs_at(idx_ref, half)] = dot_t(low, wo_oth[...])
    gain[:, mine_at(idx_ref, gain_half)] = packed_row(own_ref, *place_hg)
    gain[:, theirs_at(idx_ref, gain_half)] = packed_row(pack_ref, *place_hg)
    head_gain = gain[...]
    wide = qb_ref.shape[1] // HEADS
    tall = mixture_ref.shape[1] // HEADS
    factor = wide ** (-0.5)
    quarter = state.shape[1]
    per = tall // quarter
    gain_grad = jnp.zeros((1, tall), F32)
    for s in range(seqs):
        at = slice(s * span, (s + 1) * span)
        for h in range(HEADS):
            vs = slice(h * tall, (h + 1) * tall)
            hs = slice(h * wide, (h + 1) * wide)
            mixture, opened, grad = mixture_ref[at, vs], og_ref[at, vs], gated[at, vs]
            root = lax.rsqrt(jnp.mean(mixture * mixture, axis=1, keepdims=True) + 1e-5)
            sig = sigmoid(opened)
            flat = mixture * root
            ol_ref[at, vs] = (grad * flat * head_gain * sig * (1.0 + opened * (1.0 - sig))).astype(BF16)
            grad = grad * (opened * sig)
            gain_grad += jnp.sum(grad * flat, axis=0, keepdims=True)
            grad = grad * head_gain
            along = jnp.mean(grad * flat, axis=1, keepdims=True)
            mixed = (grad - flat * along) * (root * factor)
            mg_ref[at, vs] = mixed
            part = t_dot(mixed.astype(BF16), qb_ref[at, hs])
            for q in range(per):
                state[s * per + q, :, hs] = part[q * quarter : (q + 1) * quarter]
    gain_sum[...] = gain_grad
    hgm_ref[...] = gain_sum[:, mine_at(idx_ref, gain_half)]
    hgo_ref[...] = gain_sum[:, theirs_at(idx_ref, gain_half)]
    totals = [tot_ref[pl.ds(s, 1), :] for s in range(seqs)]
    write_quarters(idx_ref, state, totals, (m0, m1, m2, m3), seqs)


def inner_back_kernel(dims, idx_ref, q_ref, k_ref, v_ref, lg_ref, a_ref, mg_ref, qb_ref, st_ref,
                      dq_ref, dk_ref, dv_ref, dc_ref):
    seqs, span = dims
    row, col = pair_iota(span)
    upto = (col <= row).astype(F32).astype(BF16)
    diagonal = row == col
    levels = level_masks(span)
    wide = q_ref.shape[1] // HEADS
    tall = v_ref.shape[1] // HEADS
    quarter = st_ref.shape[1]
    per = tall // quarter
    for s in range(seqs):
        at = slice(s * span, (s + 1) * span)
        logits = lg_ref[at, :]
        decays = (jnp.minimum(logits, 0.0) - jnp.log1p(jnp.exp(-jnp.abs(logits)))) / 16.0
        high, rest = two_part(decays)
        qs32, ks32 = q_ref[at, :].astype(F32), k_ref[at, :].astype(F32)
        begun = jnp.exp(dot(upto, high) + dot(upto, rest))
        pair_grads = []
        for h in range(HEADS):
            hs = slice(h * wide, (h + 1) * wide)
            vs = slice(h * tall, (h + 1) * tall)
            mixed, more = two_part(mg_ref[at, vs])
            values = v_ref[at, vs]
            full = dot_t(mixed, values) + dot_t(more, values)
            back = dot_t(values, mixed) + dot_t(values, more)
            pair_grads.append(jnp.where(row >= col, full, back))
            dv_ref[at, vs] = t_dot(a_ref[s * HEADS + h], mixed)
            own = jnp.sum(jnp.where(diagonal, full, 0.0), axis=1, keepdims=True)
            crossed = jnp.zeros((span, wide), F32)
            for q in range(per):
                part = slice(h * tall + q * quarter, h * tall + (q + 1) * quarter)
                crossed += dot(mg_ref[at, part].astype(BF16), st_ref[s * per + q, :, hs])
            dq_ref[at, hs] = own * ks32[:, hs] + begun[:, hs] * crossed
            dk_ref[at, hs] = own * qs32[:, hs]
            dc_ref[at, hs] = qb_ref[at, hs].astype(F32) * crossed
        for sums, _, both, half in levels:
            fade = jnp.exp(dot(sums, high) + dot(sums, rest))
            upper = upper_rows(half, qs32.shape[1], span)
            side = (jnp.where(upper, qs32, ks32) * fade).astype(BF16)
            for h in range(HEADS):
                hs = slice(h * wide, (h + 1) * wide)
                grads = dot(jnp.where(both, pair_grads[h], 0.0).astype(BF16), side[:, hs])
                moved = side[:, hs].astype(F32) * grads
                faded = fade[:, hs] * grads
                over = upper[:, hs]
                dc_ref[at, hs] += jnp.where(over, moved, -moved)
                dq_ref[at, hs] += jnp.where(over, faded, 0.0)
                dk_ref[at, hs] += jnp.where(over, 0.0, faded)


def inputs_back_kernel(dims, idx_ref, dq_ref, dk_ref, dv_ref, dc_ref, ol_ref, kd_ref, v_ref, lg_ref, tot_ref, st_ref,
                       l0, l1, l2, l3, x_ref, hg_ref, wq_own, wq_oth, wk_own, wk_oth, wv_own, wv_oth,
                       wg_own, wg_oth, own_ref, pack_ref, g2o_ref, hgo_ref,
                       tg_ref, ga_ref, llm_ref, g1m_ref, bm_ref, small_ref,
                       leaving, logit, bias):
    seqs, span = dims
    half = wq_own.shape[0]
    part = wq_own.shape[1] // 2
    place_g1, _, _, _ = packed_places(half, part, 0)
    li_own, lo_own = packed_factors(own_ref, half)
    li_oth, lo_oth = packed_factors(pack_ref, half)
    load_state(idx_ref, (l0, l1, l2, l3), leaving)
    row, col = pair_iota(span)
    later = (col > row).astype(F32).astype(BF16)
    since = (col >= row).astype(F32).astype(BF16)
    before = (col < row).astype(F32).astype(BF16)
    keys = kd_ref.shape[1]
    vals = v_ref.shape[1]
    wide, tall = keys // HEADS, vals // HEADS
    quarter = st_ref.shape[1]
    per = tall // quarter
    bias_sum = jnp.zeros((1, keys), F32)
    for s in range(seqs):
        at = slice(s * span, (s + 1) * span)
        logits = lg_ref[at, :]
        decays = (jnp.minimum(logits, 0.0) - jnp.log1p(jnp.exp(-jnp.abs(logits)))) / 16.0
        ahead = jnp.exp(mask_dot(later, decays))
        for h in range(HEADS):
            hs = slice(h * wide, (h + 1) * wide)
            faded = kd_ref[at, hs]
            grads = jnp.zeros((span, wide), F32)
            ends = jnp.zeros((1, wide), F32)
            for q in range(per):
                vs = slice(h * tall + q * quarter, h * tall + (q + 1) * quarter)
                at_v = slice(keys * 2 + vs.start, keys * 2 + vs.stop)
                part = leaving[s * per + q, :, hs]
                ga_ref[at, at_v] = (dv_ref[at, vs] + dot_t(faded, part)).astype(BF16)
                grads += dot(v_ref[at, vs], part)
                ends += jnp.sum(
                    st_ref[s * per + q, :, hs].astype(F32) * part.astype(F32), axis=0, keepdims=True
                )
            moved = faded.astype(F32) * grads
            ga_ref[at, keys + h * wide : keys + (h + 1) * wide] = (
                dk_ref[at, hs] + ahead[:, hs] * grads
            ).astype(BF16)
            decay_grad = (
                mask_dot(since, dc_ref[at, hs])
                + mask_dot(before, moved)
                + tot_ref[pl.ds(s, 1), hs] * ends
            )
            logit_grad = decay_grad * sigmoid(-logits[:, hs]) / 16.0
            bias[:, hs] = jnp.sum(logit_grad, axis=0, keepdims=True)
            logit[at, hs] = logit_grad.astype(BF16)
        bias_sum += bias[...]
    bias[...] = bias_sum
    part = keys // 2
    bm_ref[...] = bias[:, mine_at(idx_ref, part)]
    small_ref[:, 2 * half : 2 * half + part] = bias[:, theirs_at(idx_ref, part)]
    small_ref[:, half : 2 * half] = g2o_ref[...]
    small_ref[:, 2 * half + part :] = hgo_ref[...]
    ga_ref[:, 0:keys] = dq_ref[...].astype(BF16)
    ga_ref[:, 2 * keys + vals : 2 * keys + 2 * vals] = ol_ref[...]
    llm, llo = logit[:, mine_at(idx_ref, part)], logit[:, theirs_at(idx_ref, part)]
    llm_ref[...] = llm
    lrg = (dot_t(llm, lo_own) + dot_t(llo, lo_oth)).astype(BF16)
    rest = jnp.zeros((lrg.shape[0], 128 - RANK), BF16)
    lanes = 2 * keys + 2 * vals + 128
    ga_ref[:, lanes - 128 : lanes] = jnp.concatenate([lrg, rest], axis=1)
    ga_ref[:, lanes:] = llo
    qg, kg = ga_ref[:, 0:keys], ga_ref[:, keys : 2 * keys]
    vg = ga_ref[:, 2 * keys : 2 * keys + vals]
    og = ga_ref[:, 2 * keys + vals : 2 * keys + 2 * vals]
    dm = dot_t(qg, wq_own[...]) + dot_t(kg, wk_own[...]) + dot_t(vg, wv_own[...])
    dm = dm + dot_t(og, wg_own[...]) + dot(lrg, li_own)
    do = dot_t(qg, wq_oth[...]) + dot_t(kg, wk_oth[...]) + dot_t(vg, wv_oth[...])
    do = do + dot_t(og, wg_oth[...]) + dot(lrg, li_oth)
    mine, theirs = mine_at(idx_ref, half), theirs_at(idx_ref, half)
    xm, xo = x_ref[:, mine].astype(F32), x_ref[:, theirs].astype(F32)
    square = jnp.sum(xm * xm, axis=1, keepdims=True) + jnp.sum(xo * xo, axis=1, keepdims=True)
    root = lax.rsqrt(square / (2 * half) + 1e-6)
    g1m_ref[...] = jnp.sum(dm * xm * root, axis=0, keepdims=True)
    small_ref[:, 0:half] = jnp.sum(do * xo * root, axis=0, keepdims=True)
    dm = dm * packed_row(own_ref, *place_g1)
    do = do * packed_row(pack_ref, *place_g1)
    along = jnp.sum(dm * xm, axis=1, keepdims=True) + jnp.sum(do * xo, axis=1, keepdims=True)
    along = along * (root * root * root) / (2 * half)
    tg_ref[:, mine] = hg_ref[:, mine] + dm * root - xm * along
    tg_ref[:, theirs] = hg_ref[:, theirs] + do * root - xo * along


def block_of(position, order):
    block = 0
    for at, bit in enumerate(order):
        if (position >> (3 - at)) & 1:
            block |= bit
    return block


def deal(position, keep_ref, send_ref):
    return keep_ref.at[position] if position < 8 else send_ref.at[position - 8]


def wide_grad_kernel(orders, idx_ref, lm_ref, lo_ref, gm_ref, go_ref, k0, s0, k1, s1, full):
    place = lax.rem(idx_ref[1], 16)
    width = full.shape[1]
    high = full.shape[0] // 16
    for which, refs in enumerate(((k0, s0), (k1, s1))):
        cols = slice(which * width, (which + 1) * width)
        full[...] = t_dot(lm_ref[...], gm_ref[:, cols]) + t_dot(lo_ref[...], go_ref[:, cols])
        for position in range(16):
            block = block_of(position, orders[which]) ^ place
            rows = full[pl.ds(pl.multiple_of(block * high, high), high), :].astype(BF16)
            to = deal(position, *refs)
            for tile in range(width // 128):
                to[tile * high : (tile + 1) * high, :] = rows[:, tile * 128 : (tile + 1) * 128]


def down_grad_kernel(order, idx_ref, lm_ref, lo_ref, gm_ref, go_ref, keep_ref, send_ref, full):
    place = lax.rem(idx_ref[1], 16)
    full[...] = t_dot(lm_ref[...], gm_ref[...]) + t_dot(lo_ref[...], go_ref[...])
    high = full.shape[0] // 2
    for position in range(16):
        block = block_of(position, order) ^ place
        rows = pl.ds(pl.multiple_of(lax.div(block, 8) * high, 16), high)
        cols = pl.ds(pl.multiple_of(lax.rem(block, 8) * 128, 128), 128)
        deal(position, keep_ref, send_ref)[...] = full[rows, cols].astype(BF16)


def attention_grad_kernel(orders, cuts, idx_ref, nm_ref, no_ref, gm_ref, go_ref, am_ref, ao_ref, hm_ref, ho_ref,
                          lrm_ref, lro_ref, llm_ref, g1_ref, g2_ref, b_ref, hg_ref, small_ref, k0, s0, k1, s1, k2, s2, full, outer, small):
    place = lax.rem(idx_ref[1], 16)
    lanes = full.shape[1]
    full[...] = t_dot(nm_ref[...], gm_ref[:, 0:lanes]) + t_dot(no_ref[...], go_ref[:, 0:lanes])
    outer[...] = t_dot(am_ref[...], hm_ref[...]) + t_dot(ao_ref[...], ho_ref[...])
    low_out = t_dot(lrm_ref[...], llm_ref[...]) + t_dot(lro_ref[...], go_ref[:, lanes:])
    small[...] = jnp.zeros_like(small)
    small[0] = low_out[:, 0:128]
    small[1] = low_out[:, 128:256]
    line = 0
    for ref in (g1_ref, g2_ref, b_ref, hg_ref):
        row = ref[...] + small_ref[:, line * 128 : line * 128 + ref.shape[1]]
        for tile in range(row.shape[1] // 128):
            small[2, line : line + 1, :] = row[:, tile * 128 : (tile + 1) * 128]
            line += 1
    high = full.shape[0] // 16
    tiles = full.shape[1] // 128
    for which, refs in enumerate(((k0, s0), (k1, s1), (k2, s2))):
        first, last = cuts[which], cuts[which + 1]
        for position in range(16):
            block = block_of(position, orders[which]) ^ place
            at = pl.ds(pl.multiple_of(block * high, high), high)
            to = deal(position, *refs)
            for tile in range(first, last):
                if tile < tiles:
                    rows = full[at, tile * 128 : (tile + 1) * 128]
                else:
                    rows = outer[at, (tile - tiles) * 128 : (tile - tiles + 1) * 128]
                to[(tile - first) * high : (tile - first + 1) * high, :] = rows.astype(BF16)
            if which == 2:
                to[(last - first) * high :, :] = small[block].astype(BF16)


def wide_open_kernel(order, idx_ref, own_ref, got_ref, out_ref):
    place = lax.rem(idx_ref[1], 16)
    high = out_ref.shape[0] // 16
    for position in range(16):
        block = block_of(position, order) ^ place
        held = deal(position, own_ref, got_ref)
        at = pl.ds(pl.multiple_of(block * high, high), high)
        for tile in range(out_ref.shape[1] // 128):
            out_ref[at, tile * 128 : (tile + 1) * 128] = held[tile * high : (tile + 1) * high, :].astype(F32)


def down_open_kernel(order, idx_ref, own_ref, got_ref, out_ref):
    place = lax.rem(idx_ref[1], 16)
    high = out_ref.shape[0] // 2
    for position in range(16):
        block = block_of(position, order) ^ place
        rows = pl.ds(pl.multiple_of(lax.div(block, 8) * high, 16), high)
        cols = pl.ds(pl.multiple_of(lax.rem(block, 8) * 128, 128), 128)
        out_ref[rows, cols] = deal(position, own_ref, got_ref)[...].astype(F32)


def attention_open_kernel(orders, cuts, idx_ref, o0, r0, o1, r1, o2, r2, q_ref, k_ref, v_ref, og_ref, li_ref, w_ref,
                          lo_ref, g1_ref, g2_ref, b_ref, hg_ref, small, first_factor):
    place = lax.rem(idx_ref[1], 16)
    high = q_ref.shape[0] // 16
    homes = []
    for ref in (q_ref, k_ref, v_ref, og_ref):
        homes += [(ref, tile) for tile in range(ref.shape[1] // 128)]
    homes.append((first_factor, 0))
    homes += [(w_ref, tile) for tile in range(w_ref.shape[1] // 128)]
    for which, refs in enumerate(((o0, r0), (o1, r1), (o2, r2))):
        first, last = cuts[which], cuts[which + 1]
        for position in range(16):
            block = block_of(position, orders[which]) ^ place
            at = pl.ds(pl.multiple_of(block * high, high), high)
            held = deal(position, *refs)
            for tile in range(first, last):
                rows = held[(tile - first) * high : (tile - first + 1) * high, :].astype(F32)
                ref, column = homes[tile]
                ref[at, column * 128 : (column + 1) * 128] = rows
            if which == 2:
                small[block] = held[(last - first) * high :, :].astype(F32)
    li_ref[...] = first_factor[...].T[0 : li_ref.shape[0], :]
    lo_ref[:, 0:128] = small[0]
    lo_ref[:, 128:256] = small[1]
    line = 0
    for ref in (g1_ref, g2_ref, b_ref, hg_ref):
        for tile in range(ref.shape[1] // 128):
            ref[:, tile * 128 : (tile + 1) * 128] = small[2, line : line + 1, :]
            line += 1


def across(array):
    return lax.ppermute(array, "fsdp", ((0, 1), (1, 0)))


def swap(array, bit):
    count = lax.axis_size("seq")
    return lax.ppermute(array, "seq", tuple((one, one ^ bit) for one in range(count)))


def ahead(array, step):
    count = lax.axis_size("seq")
    return lax.ppermute(
        array,
        "seq",
        tuple((one, one + step) for one in range(count) if 0 <= one + step < count),
    )


def fence(*groups):
    return lax.optimization_barrier(groups)


class Portions:
    def __init__(self, parts, orders):
        self.kept = [keep for keep, _ in parts]
        self.sent = [send for _, send in parts]
        self.orders = orders

    def move(self, arrays, step):
        if step < 3:
            return [swap(a, order[step]) for a, order in zip(arrays, self.orders)]
        return self.move_all(arrays, self.orders[0][3])

    def move_all(self, arrays, bit):
        got = swap(jnp.concatenate(arrays, axis=1), bit)
        ends = [0]
        for a in arrays:
            ends.append(ends[-1] + a.shape[1])
        return [got[:, first:last] for first, last in zip(ends[:-1], ends[1:])]

    def reduce_start(self, step):
        return self.move(self.sent, step)

    def reduce_end(self, step, got):
        for one, more in enumerate(got):
            if step < 3:
                half = more.shape[0] // 2
                self.sent[one] = self.kept[one][half:] + more[half:]
                self.kept[one] = self.kept[one][:half] + more[:half]
            else:
                self.kept[one] = self.kept[one] + more
        bit = 16
        while step == 3 and bit < lax.axis_size("seq"):
            more = self.move_all(self.kept, bit)
            self.kept = [k + m for k, m in zip(self.kept, more)]
            bit *= 2

    def gather_start(self, step):
        return self.move(self.kept, step)

    def gather_end(self, step, got):
        if step:
            self.kept = [jnp.concatenate([k, more], axis=0) for k, more in zip(self.kept, got)]
        else:
            self.halves = list(zip(self.kept, got))


def scan_near(messages):
    return [messages[0]] + [swap(messages[o], o) for o in (1, 2, 3)]


def scan_scratch(messages):
    rows, lanes = messages[0].shape
    return [((4, rows - 16, lanes), F32), ((4, 1, lanes), F32)]


def scan_total(near, idx, reverse):
    return call("group_total", partial(group_total, reverse), idx, near, [(near[0].shape, BF16)], scan_scratch(near))[0]


def scan_far(total, reverse):
    sign = -4 if reverse else 4
    return [ahead(total, sign * step) for step in range(1, lax.axis_size("seq") // 4)]


def scan_entering(far, near, idx, reverse):
    rows, lanes = near[0].shape
    return call(
        "group_entering", partial(group_entering, reverse, len(far)), idx, list(far) + list(near),
        [((rows - 16, lanes), BF16)] * 4, scan_scratch(near) + [((4, rows - 16, lanes), F32)],
    )


def shards(
    tokens,
    lengths,
    first_gain,
    query_weight,
    key_weight,
    value_weight,
    outgate_weight,
    lowrank_in,
    lowrank_out,
    decay_bias,
    head_gain,
    output_weight,
    second_gain,
    gate_weight,
    up_weight,
    down_weight,
    cotangent,
):
    micro_count, pair_count, span, width = tokens.shape
    seqs = micro_count * pair_count
    rows = seqs * span
    dims = (seqs, span)
    core = lax.axis_index("fsdp")
    place = lax.axis_index("seq")
    own_lengths = lax.dynamic_slice_in_dim(lengths, core * pair_count, pair_count, 1).reshape(-1)
    idx = jnp.concatenate([jnp.stack([core, place]).astype(jnp.int32), own_lengths])
    keys, vals, ff = query_weight.shape[1], value_weight.shape[1], gate_weight.shape[1]
    half = query_weight.shape[0]
    tall = vals // HEADS
    quarter = seqs * tall // 4

    x = tokens.reshape(rows, width)
    cot = cotangent.reshape(rows, width)
    lrank = lowrank_in.shape[1]
    lines, at = 0, 0
    for a in (first_gain, second_gain, decay_bias, head_gain):
        lines = lines + jnp.pad(a, (at, 16 * 128 - at - a.size))
        at += a.size
    lines = lines.reshape(16, 128)
    pack = call(
        "pack", pack_kernel, idx, [lowrank_in.T, lowrank_out, lines],
        [((lrank * (half + lowrank_out.shape[1]) // 128 + 16, 128), BF16)],
    )[0]
    pack2, wk2, wv2 = (across(a) for a in (pack, key_weight, value_weight))

    message = ((quarter + 16, keys), BF16)
    state = ((4, quarter, keys), F32)
    nm, no, k, v, lr, lg, kd, tot, cots, *messages = call(
        "keys", partial(keys_kernel, dims), idx,
        [x, cot, key_weight, wk2, value_weight, wv2, pack, pack2],
        [((rows, half), BF16), ((rows, half), BF16), ((rows, keys), BF16), ((rows, vals), BF16),
         ((rows, lrank), BF16), ((rows, keys), F32), ((rows, keys), BF16), ((seqs, keys), F32), ((rows, width), BF16)]
        + [message] * 4,
        [state], limit=56,
    )
    messages, outgate_send, query_send = fence(messages, outgate_weight, query_weight)
    near = scan_near(messages)
    wg2, wq2 = across(outgate_send), across(query_send)
    near, wg2, wq2, gate_send, up_send = fence(near, wg2, wq2, gate_weight, up_weight)
    total = scan_total(near, idx, False)
    total, gate_send, up_send = fence(total, gate_send, up_send)
    far = scan_far(total, False)
    wgate2, wup2 = across(gate_send), across(up_send)
    q, og, mix, scores, qb = call(
        "inner", partial(inner_kernel, dims), idx,
        [nm, no, query_weight, wq2, outgate_weight, wg2, k, v, lg],
        [((rows, keys), BF16), ((rows, vals), F32), ((rows, vals), F32), ((seqs * HEADS, span, span), BF16),
         ((rows, keys), BF16)],
    )
    far, mix, wgate2, wup2 = fence(far, mix, wgate2, wup2)
    pieces = scan_entering(far, near, idx, False)
    pieces, output_send, down_send = fence(pieces, output_weight, down_weight)
    pieces = [pieces[0]] + [swap(pieces[o], o) for o in (1, 2, 3)]
    wo2, wdown2 = across(output_send), across(down_send)
    mixture, gm, go, hid, sm, so, st = call(
        "hidden", partial(hidden_kernel, dims), idx,
        [mix, qb, *pieces, og, x, output_weight, wo2, pack, pack2],
        [((rows, vals), F32), ((rows, vals // 2), BF16), ((rows, vals // 2), BF16), ((rows, width), F32),
         ((rows, half), BF16), ((rows, half), BF16), ((4, quarter, keys), BF16)],
        [((1, tall), F32), ((rows, vals), BF16)],
    )
    so, no_send, lr_send, cots_send = fence(so, no, lr, cots)
    so2, no2, go2, lr2, cots2 = (across(a) for a in (so, no_send, go, lr_send, cots_send))
    out, am, ao, gu, dm, do = call(
        "ffn", partial(ffn_kernel, dims), idx,
        [sm, so, hid, cots, gate_weight, wgate2, up_weight, wup2, down_weight, wdown2],
        [((rows, width), F32), ((rows, ff // 2), BF16), ((rows, ff // 2), BF16),
         ((rows, 2 * ff), BF16), ((rows, half), F32), ((rows, half), F32)],
        [((2, 2, half, ff // 2), BF16), ((2, 2, half, ff // 2), BF16), ((2, ff // 2, width), BF16),
         pltpu.SemaphoreType.DMA((4, 5))], limit=42, far=6,
    )
    so2, no2, go2, lr2, cots2, gu, dm, ao = fence(so2, no2, go2, lr2, cots2, gu, dm, ao)

    orders = ((1, 2, 4, 8), (2, 4, 1, 8), (4, 1, 2, 8))
    hg, hl, mg, ol, g2m, g2o, hgm, hgo, *messages = call(
        "gate_back", partial(gate_back_kernel, dims), idx,
        [hid, dm, do, cots, output_weight, wo2, mixture, og, qb, tot, pack, pack2],
        [((rows, width), F32), ((rows, width), BF16), ((rows, vals), F32), ((rows, vals), BF16),
         ((1, half), F32), ((1, half), F32), ((1, tall // 2), F32), ((1, tall // 2), F32)] + [message] * 4,
        [((1, tall), F32), ((rows, vals), F32), ((1, tall), F32), state],
    )
    messages, ao, gu_send = fence(messages, ao, gu)
    near = scan_near(messages)
    ao2, gu2 = across(ao), across(gu_send)
    portion = ff // 128 * (half // 16)
    flat = [((8, portion, 128), BF16)] * 2
    down_parts = call("down_grad", partial(down_grad_kernel, orders[2]), idx, [am, ao2, cots, cots2], flat,
                      [((ff // 2, width), F32)])
    near, down_parts, gu2 = fence(near, down_parts, gu2)
    total = scan_total(near, idx, True)
    total, gu2 = fence(total, gu2)
    far = scan_far(total, True)
    wide_parts = call("wide_grad", partial(wide_grad_kernel, orders), idx, [sm, so2, gu, gu2], flat * 2,
                      [((half, ff), F32)], limit=32)

    far, wide_parts = fence(far, wide_parts)
    pieces = scan_entering(far, near, idx, True)
    pieces = [pieces[0]] + [swap(pieces[o], o) for o in (1, 2, 3)]
    pieces, wide_parts, hl, mg = fence(pieces, wide_parts, hl, mg)
    first = Portions([wide_parts[0:2], wide_parts[2:4], down_parts], orders)
    got = first.reduce_start(0)
    hl2 = across(hl)
    dq, dk, dv, dc = call(
        "inner_back", partial(inner_back_kernel, dims), idx, [q, k, v, lg, scores, mg, qb, st],
        [((rows, keys), F32), ((rows, keys), F32), ((rows, vals), F32), ((rows, keys), F32)],
    )
    pieces, dq = fence(pieces, dq)
    lanes = 2 * keys + 2 * vals + 128
    tg, ga, llm, g1m, bm, small = call(
        "inputs_back", partial(inputs_back_kernel, dims), idx,
        [dq, dk, dv, dc, ol, kd, v, lg, tot, st, *pieces, x, hg, query_weight, wq2, key_weight, wk2,
         value_weight, wv2, outgate_weight, wg2, pack, pack2, g2o, hgo],
        [((rows, width), F32), ((rows, lanes + keys // 2), BF16), ((rows, keys // 2), BF16),
         ((1, half), F32), ((1, keys // 2), F32), ((1, 2 * half + keys // 2 + tall // 2), F32)],
        [((4, quarter, keys), BF16), ((rows, keys), BF16), ((1, keys), F32)], limit=32,
    )
    got, ga, small, hl2 = fence(got, ga, small, hl2)
    first.reduce_end(0, got)
    got = first.reduce_start(1)
    ga2, small2 = across(ga), across(small)
    got, ga2, small2 = fence(got, ga2, small2)
    first.reduce_end(1, got)
    first.sent, ga2 = fence(first.sent, ga2)
    got = first.reduce_start(2)
    tiles = lanes // 128 + width // 128
    cuts = (0, tiles // 3, 2 * tiles // 3, tiles)
    high = half // 16
    shapes = []
    for which in range(3):
        size = (cuts[which + 1] - cuts[which]) * high + (16 if which == 2 else 0)
        shapes += [((8, size, 128), BF16)] * 2
    parts = call(
        "attention_grad", partial(attention_grad_kernel, orders, cuts), idx,
        [nm, no2, ga, ga2, gm, go2, hl, hl2, lr, lr2, llm, g1m, g2m, bm, hgm, small2],
        shapes, [((half, lanes), F32), ((vals // 2, width), F32), ((16, 16, 128), F32)], limit=32,
    )
    got, parts = fence(got, parts)
    first.reduce_end(2, got)
    second = Portions([parts[0:2], parts[2:4], parts[4:6]], orders)
    got, more = fence(first.reduce_start(3), second.reduce_start(0))
    first.reduce_end(3, got)
    second.reduce_end(0, more)
    got, more = fence(first.gather_start(3), second.reduce_start(1))
    first.gather_end(3, got)
    second.reduce_end(1, more)
    both = [jnp.concatenate([k, a], axis=1) for k, a in zip(first.kept, second.sent)]
    both = fence(*[swap(a, order[2]) for a, order in zip(both, orders)])
    got = [a[:, : k.shape[1]] for a, k in zip(both, first.kept)]
    more = [a[:, k.shape[1] :] for a, k in zip(both, first.kept)]
    first.gather_end(2, got)
    second.reduce_end(2, more)
    got, more = fence(first.gather_start(1), second.reduce_start(3))
    first.gather_end(1, got)
    second.reduce_end(3, more)
    got, more = fence(first.gather_start(0), second.gather_start(3))
    first.gather_end(0, got)
    second.gather_end(3, more)
    gate_halves, up_halves, down_halves = first.halves
    more = second.gather_start(2)
    gate_out = call("gate_open", partial(wide_open_kernel, orders[0]), idx, gate_halves, [((half, ff), F32)])[0]
    more, gate_out = fence(more, gate_out)
    second.gather_end(2, more)
    more = second.gather_start(1)
    up_out = call("up_open", partial(wide_open_kernel, orders[1]), idx, up_halves, [((half, ff), F32)])[0]
    more, up_out = fence(more, up_out)
    second.gather_end(1, more)
    more = second.gather_start(0)
    down_out = call("down_open", partial(down_open_kernel, orders[2]), idx, down_halves, [((ff // 2, width), F32)])[0]
    more, down_out = fence(more, down_out)
    second.gather_end(0, more)
    opened = call(
        "attention_open", partial(attention_open_kernel, orders, cuts), idx, [a for pair in second.halves for a in pair],
        [((half, keys), F32), ((half, keys), F32), ((half, vals), F32), ((half, vals), F32),
         ((lrank, half), F32), ((vals // 2, width), F32), ((lrank, keys // 2), F32),
         ((1, half), F32), ((1, half), F32), ((1, keys // 2), F32), ((1, tall // 2), F32)],
        [((16, 16, 128), F32), ((half, 128), F32)],
    )
    q_out, k_out, v_out, og_out, li_out, w_out, lo_out, g1_out, g2_out, b_out, hg_out = opened
    return (
        out.reshape(tokens.shape),
        tg.reshape(tokens.shape),
        g1_out.reshape(-1),
        q_out,
        k_out,
        v_out,
        og_out,
        li_out.T,
        lo_out,
        b_out.reshape(-1),
        hg_out.reshape(-1),
        w_out,
        g2_out.reshape(-1),
        gate_out,
        up_out,
        down_out,
    )


def solution(mesh):
    shard, column = P("fsdp", None), P(None, "fsdp")
    stream, line = P(None, "fsdp", "seq", None), P("fsdp")
    weights = (line, shard, shard, shard, shard, shard, column, line, line, shard, line, shard, shard, shard)
    return jax.shard_map(
        shards,
        mesh=mesh,
        in_specs=(stream, P()) + weights + (stream,),
        out_specs=(stream, stream) + weights,
        check_vma=False,
    )
```

```python
from functools import partial

import jax
import jax.numpy as jnp
from jax import lax
from jax.experimental import pallas as pl
from jax.experimental.pallas import tpu as pltpu
from jax.sharding import PartitionSpec as P

HEADS = 4
RANK = 16
F32 = jnp.float32
BF16 = jnp.bfloat16
MIB = 1024 * 1024


def dot(first_op, second_op):
    return jnp.dot(first_op, second_op, preferred_element_type=F32)


def dot_t(first_op, second_op):
    return lax.dot_general(
        first_op, second_op, (((1,), (1,)), ((), ())), preferred_element_type=F32
    )


def t_dot(first_op, second_op):
    return lax.dot_general(
        first_op, second_op, (((0,), (0,)), ((), ())), preferred_element_type=F32
    )


def two_part(value):
    high = value.astype(BF16)
    return high, (value - high.astype(F32)).astype(BF16)


def mask_dot(mask, value):
    high, rest = two_part(value)
    return dot(mask, high) + dot(mask, rest)


def sigmoid(value):
    return 1.0 / (1.0 + jnp.exp(-value))


def pair_iota(size):
    return (
        lax.broadcasted_iota(jnp.int32, (size, size), 0),
        lax.broadcasted_iota(jnp.int32, (size, size), 1),
    )


def level_masks(size):
    row, col = pair_iota(size)
    out = []
    half = size // 2
    while half >= 1:
        block = 2 * half
        row_block = row // block
        middle = row_block * block + half - 1
        upper = row > middle
        sums = (upper & (col > middle) & (col <= row)) | (
            jnp.logical_not(upper) & (col > row) & (col <= middle)
        )
        same = row_block == col // block
        pairs = same & upper & (col <= middle)
        both = same & (upper != (col > middle))
        out.append((sums.astype(F32).astype(BF16), pairs, both, half))
        half //= 2
    return out


def upper_rows(half, width, size):
    row = lax.broadcasted_iota(jnp.int32, (size, width), 0)
    return row % (2 * half) >= half


def seat(idx_ref):
    return idx_ref[0], idx_ref[1]


def mine_at(idx_ref, width):
    return pl.ds(pl.multiple_of(idx_ref[0] * width, 128), width)


def theirs_at(idx_ref, width):
    return pl.ds(pl.multiple_of((1 - idx_ref[0]) * width, 128), width)


SMEM = pl.BlockSpec(memory_space=pltpu.SMEM)
VMEM = pl.BlockSpec(memory_space=pltpu.VMEM)


def call(name, body, idx, inputs, outs, scratch=(), limit=24, far=0):
    shapes = [jax.ShapeDtypeStruct(s, d) for s, d in outs]
    result = pl.pallas_call(
        body,
        name=name,
        out_shape=shapes,
        in_specs=[SMEM] + [VMEM] * (len(inputs) - far) + [pl.BlockSpec(memory_space=pl.ANY)] * far,
        out_specs=[VMEM] * len(shapes),
        scratch_shapes=[pltpu.VMEM(*s) if isinstance(s, tuple) else s for s in scratch],
        compiler_params=pltpu.CompilerParams(vmem_limit_bytes=limit * MIB),
        cost_estimate=pl.CostEstimate(flops=1, bytes_accessed=1, transcendentals=0),
    )(idx, *inputs)
    return result


def put_message(ref, rows, total):
    count = rows.shape[0]
    ref[pl.ds(0, count), :] = rows.astype(BF16)
    high = total.astype(BF16)
    rest = total - high.astype(F32)
    middle = rest.astype(BF16)
    low = (rest - middle.astype(F32)).astype(BF16)
    tail = jnp.concatenate(
        [high, middle, low, jnp.zeros((13,) + total.shape[1:], BF16)], axis=0
    )
    ref[pl.ds(count, 16), :] = tail


def get_message(ref):
    count = ref.shape[0] - 16
    tail = ref[pl.ds(count, 16), :].astype(F32)
    return ref[pl.ds(0, count), :].astype(F32), tail[0:1] + tail[1:2] + tail[2:3]


def write_quarters(idx_ref, state, totals, messages, seq_count):
    low = lax.rem(idx_ref[1], 4)
    for other in range(4):
        quarter = low ^ other
        total = totals[0]
        for one in range(1, seq_count):
            total = jnp.where(quarter * seq_count // 4 >= one, totals[one], total)
        put_message(messages[other], state[quarter], total)


def group_total(reverse, idx_ref, *refs):
    out_ref, kept, held = refs[4], refs[5], refs[6]
    low = lax.rem(idx_ref[1], 4)
    for other in range(4):
        rows, total = get_message(refs[other])
        kept[low ^ other] = rows
        held[low ^ other] = total
    order = (3, 2, 1, 0) if reverse else (0, 1, 2, 3)
    rows, total = kept[order[0]], held[order[0]]
    for one in order[1:]:
        rows = held[one] * rows + kept[one]
        total = total * held[one]
    put_message(out_ref, rows, total)


def group_entering(reverse, far_count, idx_ref, *refs):
    far, near = refs[:far_count], refs[far_count : far_count + 4]
    outs = refs[far_count + 4 : far_count + 8]
    kept, held, entering = refs[far_count + 8 :]
    low = lax.rem(idx_ref[1], 4)
    for other in range(4):
        rows, total = get_message(near[other])
        kept[low ^ other] = rows
        held[low ^ other] = total
    rows = jnp.zeros(kept.shape[1:], F32)
    for one in far[::-1]:
        part, total = get_message(one)
        rows = total * rows + part
    for one in (3, 2, 1, 0) if reverse else (0, 1, 2, 3):
        entering[one] = rows
        rows = held[one] * rows + kept[one]
    for other in range(4):
        outs[other][...] = entering[low ^ other].astype(BF16)


def load_state(idx_ref, pieces, state):
    low = lax.rem(idx_ref[1], 4)
    for other in range(4):
        state[low ^ other] = pieces[other][...]


def pack_kernel(idx_ref, li_ref, lo_ref, lines_ref, out_ref):
    at = 0
    for ref in (li_ref, lo_ref):
        rank = ref.shape[0]
        for tile in range(ref.shape[1] // 128):
            out_ref[at : at + rank, :] = ref[:, tile * 128 : (tile + 1) * 128]
            at += rank
    out_ref[at:, :] = lines_ref[...]


def packed_factors(pack_ref, half):
    rank = RANK
    high = pack_ref.shape[0] - 16
    tiles = [pack_ref[at : at + rank, :] for at in range(0, high, rank)]
    first = half // 128
    return jnp.concatenate(tiles[:first], axis=1), jnp.concatenate(tiles[first:], axis=1)


def packed_row(pack_ref, first, count):
    lines = pack_ref[pack_ref.shape[0] - 16 :, :].astype(F32)
    return jnp.concatenate([lines[t : t + 1, :] for t in range(first, first + count)], axis=1)


def packed_places(half, part, gain):
    g1, b, hg = half // 128, part // 128, gain // 128
    return (0, g1), (g1, g1), (2 * g1, b), (2 * g1 + b, hg)


def keys_kernel(dims, idx_ref, x_ref, wk_own, wk_oth, wv_own, wv_oth, own_ref, pack_ref,
                nm_ref, no_ref, k_ref, v_ref, lr_ref, lg_ref, kd_ref, tot_ref,
                m0, m1, m2, m3, state):
    seqs, span = dims
    half = wk_own.shape[0]
    part = wk_own.shape[1] // 2
    place_g1, _, place_b, _ = packed_places(half, part, 0)
    li_own, lo_own = packed_factors(own_ref, half)
    li_oth, lo_oth = packed_factors(pack_ref, half)
    g1_own, b_own = packed_row(own_ref, *place_g1), packed_row(own_ref, *place_b)
    g1_oth, b_oth = packed_row(pack_ref, *place_g1), packed_row(pack_ref, *place_b)
    xm = x_ref[:, mine_at(idx_ref, half)].astype(F32)
    xo = x_ref[:, theirs_at(idx_ref, half)].astype(F32)
    square = jnp.sum(xm * xm, axis=1, keepdims=True) + jnp.sum(xo * xo, axis=1, keepdims=True)
    root = lax.rsqrt(square / (2 * half) + 1e-6)
    nm = (xm * root * g1_own).astype(BF16)
    no = (xo * root * g1_oth).astype(BF16)
    nm_ref[...] = nm
    no_ref[...] = no
    lr = (dot_t(nm, li_own) + dot_t(no, li_oth)).astype(BF16)
    lr_ref[...] = lr
    lg_ref[:, mine_at(idx_ref, part)] = dot(lr, lo_own) + b_own
    lg_ref[:, theirs_at(idx_ref, part)] = dot(lr, lo_oth) + b_oth
    keys = (dot(nm, wk_own[...]) + dot(no, wk_oth[...])).astype(BF16)
    k_ref[...] = keys
    values = (dot(nm, wv_own[...]) + dot(no, wv_oth[...])).astype(BF16)
    v_ref[...] = values
    row, col = pair_iota(span)
    later = (col > row).astype(F32).astype(BF16)
    wide = keys.shape[1] // HEADS
    tall = values.shape[1] // HEADS
    quarter = state.shape[1]
    totals = []
    for s in range(seqs):
        at = slice(s * span, (s + 1) * span)
        logits = lg_ref[at, :]
        decays = (jnp.minimum(logits, 0.0) - jnp.log1p(jnp.exp(-jnp.abs(logits)))) / 16.0
        ahead = mask_dot(later, decays)
        totals.append(jnp.exp(jnp.sum(decays, axis=0, keepdims=True)))
        tot_ref[pl.ds(s, 1), :] = totals[s]
        faded = (keys[at].astype(F32) * jnp.exp(ahead)).astype(BF16)
        kd_ref[at, :] = faded
        for h in range(HEADS):
            part = t_dot(values[at, h * tall : (h + 1) * tall], faded[:, h * wide : (h + 1) * wide])
            per = tall // quarter
            for q in range(per):
                state[s * per + q, :, h * wide : (h + 1) * wide] = part[q * quarter : (q + 1) * quarter]
    write_quarters(idx_ref, state, totals, (m0, m1, m2, m3), seqs)


def inner_kernel(dims, idx_ref, nm_ref, no_ref, wq_own, wq_oth, wg_own, wg_oth, k_ref, v_ref, lg_ref, cot_ref,
                 q_ref, og_ref, mix_ref, a_ref, qb_ref, e_ref):
    seqs, span = dims
    for s in range(seqs):
        at = slice(s * span, (s + 1) * span)
        places = lax.broadcasted_iota(jnp.int32, (span, cot_ref.shape[1]), 0) + idx_ref[1] * span
        e_ref[at, :] = jnp.where(places < idx_ref[2 + s], cot_ref[at, :].astype(F32), 0.0).astype(BF16)
    nm, no = nm_ref[...], no_ref[...]
    queries = (dot(nm, wq_own[...]) + dot(no, wq_oth[...])).astype(BF16)
    q_ref[...] = queries
    og_ref[...] = dot(nm, wg_own[...]) + dot(no, wg_oth[...])
    row, col = pair_iota(span)
    upto = (col <= row).astype(F32).astype(BF16)
    diagonal = row == col
    levels = level_masks(span)
    wide = queries.shape[1] // HEADS
    tall = v_ref.shape[1] // HEADS
    for s in range(seqs):
        at = slice(s * span, (s + 1) * span)
        logits = lg_ref[at, :]
        decays = (jnp.minimum(logits, 0.0) - jnp.log1p(jnp.exp(-jnp.abs(logits)))) / 16.0
        high, rest = two_part(decays)
        qs, ks = queries[at], k_ref[at, :]
        qs32, ks32 = qs.astype(F32), ks.astype(F32)
        qb_ref[at, :] = (qs32 * jnp.exp(dot(upto, high) + dot(upto, rest))).astype(BF16)
        scores = []
        for h in range(HEADS):
            hs = slice(h * wide, (h + 1) * wide)
            scores.append(jnp.where(diagonal, dot_t(qs[:, hs], ks[:, hs]), 0.0))
        for sums, pairs, _, half in levels:
            fade = jnp.exp(dot(sums, high) + dot(sums, rest))
            side = (jnp.where(upper_rows(half, qs.shape[1], span), qs32, ks32) * fade).astype(BF16)
            for h in range(HEADS):
                part = side[:, h * wide : (h + 1) * wide]
                scores[h] = scores[h] + jnp.where(pairs, dot_t(part, part), 0.0)
        for h in range(HEADS):
            low = scores[h].astype(BF16)
            a_ref[s * HEADS + h] = low
            vs = slice(h * tall, (h + 1) * tall)
            mix_ref[at, vs] = dot(low, v_ref[at, vs])


def hidden_kernel(dims, idx_ref, mix_ref, qb_ref, e0, e1, e2, e3, og_ref, x_ref, wo_own, wo_oth,
                  own_ref, pack_ref, mixture_ref, gm_ref, go_ref, hid_ref, sm_ref, so_ref, st_ref,
                  gain, gated):
    seqs, span = dims
    load_state(idx_ref, (e0, e1, e2, e3), st_ref)
    half = sm_ref.shape[1]
    gain_half = gain.shape[1] // 2
    _, place_g2, _, place_hg = packed_places(half, qb_ref.shape[1] // 2, gain_half)
    gain[:, mine_at(idx_ref, gain_half)] = packed_row(own_ref, *place_hg)
    gain[:, theirs_at(idx_ref, gain_half)] = packed_row(pack_ref, *place_hg)
    wide = qb_ref.shape[1] // HEADS
    tall = mix_ref.shape[1] // HEADS
    factor = wide ** (-0.5)
    quarter = st_ref.shape[1]
    per = tall // quarter
    head_gain = gain[...]
    for s in range(seqs):
        at = slice(s * span, (s + 1) * span)
        for h in range(HEADS):
            hs = slice(h * wide, (h + 1) * wide)
            for q in range(per):
                vs = slice(h * tall + q * quarter, h * tall + (q + 1) * quarter)
                carried = dot_t(qb_ref[at, hs], st_ref[s * per + q, :, hs])
                mixture_ref[at, vs] = (mix_ref[at, vs] + carried) * factor
            vs = slice(h * tall, (h + 1) * tall)
            mixture = mixture_ref[at, vs]
            root = lax.rsqrt(jnp.mean(mixture * mixture, axis=1, keepdims=True) + 1e-5)
            opened = og_ref[at, vs]
            gated[at, vs] = (mixture * root * head_gain * (opened * sigmoid(opened))).astype(BF16)
    half = wo_own.shape[0]
    gm = gated[:, mine_at(idx_ref, half)]
    go = gated[:, theirs_at(idx_ref, half)]
    gm_ref[...] = gm
    go_ref[...] = go
    hid_ref[...] = x_ref[...].astype(F32) + dot(gm, wo_own[...]) + dot(go, wo_oth[...])
    half = sm_ref.shape[1]
    hm = hid_ref[:, mine_at(idx_ref, half)]
    ho = hid_ref[:, theirs_at(idx_ref, half)]
    square = jnp.sum(hm * hm, axis=1, keepdims=True) + jnp.sum(ho * ho, axis=1, keepdims=True)
    root = lax.rsqrt(square / (2 * half) + 1e-6)
    sm_ref[...] = (hm * root * packed_row(own_ref, *place_g2)).astype(BF16)
    so_ref[...] = (ho * root * packed_row(pack_ref, *place_g2)).astype(BF16)


def ffn_kernel(dims, idx_ref, sm_ref, so_ref, hid_ref, e_ref, wg_own, wg_oth, wu_own, wu_oth, wd_own, wd_oth,
               out_ref, am_ref, g_ref, dm_ref, do_ref, gates_in, ups_in, downs_in, sems):
    seqs, span = dims
    half = wd_own.shape[0]
    spots = (mine_at(idx_ref, half), theirs_at(idx_ref, half))
    cut = half // 256 * 128 + 128
    steps = []
    for side in range(2):
        for first, last in ((0, cut), (cut, half)):
            to_at = pl.ds(first, last - first)
            from_at = pl.ds(pl.multiple_of(spots[side].start + first, 128), last - first)
            now = []
            for to, sources in ((gates_in, (wg_own, wg_oth)), (ups_in, (wu_own, wu_oth))):
                for which in range(2):
                    now.append((sources[which].at[:, from_at], to.at[which, side, :, to_at]))
            now.append(((wd_own, wd_oth)[side].at[to_at, :], downs_in.at[side, to_at, :]))
            copies = [
                pltpu.make_async_copy(src, dst, sems.at[len(steps), i])
                for i, (src, dst) in enumerate(now)
            ]
            for one in copies:
                one.start()
            steps.append((side, first, last, copies))
    sm, so, cots = sm_ref[...], so_ref[...], e_ref[...]
    for side, first, last, copies in steps:
        size = last - first
        for one in copies:
            one.wait()
        g_own, g_oth = gates_in[0, side, :, first:last], gates_in[1, side, :, first:last]
        u_own, u_oth = ups_in[0, side, :, first:last], ups_in[1, side, :, first:last]
        down = downs_in[side, first:last, :]
        gates = dot(sm, g_own) + dot(so, g_oth)
        ups = dot(sm, u_own) + dot(so, u_oth)
        sig = sigmoid(gates)
        opened = gates * sig
        act = (opened * ups).astype(BF16)
        if side == 0:
            am_ref[:, first:last] = act
        else:
            g_ref[:, 4 * half + first : 4 * half + last] = act
        grads = dot_t(cots, down)
        gate_grad = (grads * ups * sig * (1.0 + gates * (1.0 - sig))).astype(BF16)
        up_grad = (grads * opened).astype(BF16)
        at = spots[side].start + first
        g_ref[:, pl.ds(pl.multiple_of(at, 128), size)] = gate_grad
        g_ref[:, pl.ds(pl.multiple_of(at + 2 * half, 128), size)] = up_grad
        more = dot(act, down)
        dm = dot_t(gate_grad, g_own) + dot_t(up_grad, u_own)
        do = dot_t(gate_grad, g_oth) + dot_t(up_grad, u_oth)
        if side == 0 and first == 0:
            out_ref[...] = hid_ref[...] + more
            dm_ref[...] = dm
            do_ref[...] = do
        else:
            out_ref[...] += more
            dm_ref[...] += dm
            do_ref[...] += do
    width = out_ref.shape[1]
    for s in range(seqs):
        at = slice(s * span, (s + 1) * span)
        places = lax.broadcasted_iota(jnp.int32, (span, width), 0) + idx_ref[1] * span
        out_ref[at, :] = jnp.where(places < idx_ref[2 + s], out_ref[at, :], 0.0)


def gate_back_kernel(dims, idx_ref, hid_ref, dm_ref, do_ref, e_ref, wo_own, wo_oth, mixture_ref,
                     og_ref, qb_ref, tot_ref, own_ref, pack_ref,
                     hg_ref, hl_ref, mg_ref, ol_ref, g2m_ref, g2o_ref, hgm_ref, hgo_ref, m0, m1, m2, m3,
                     gain, gated, gain_sum, state):
    seqs, span = dims
    half = dm_ref.shape[1]
    gain_half = gain.shape[1] // 2
    _, place_g2, _, place_hg = packed_places(half, qb_ref.shape[1] // 2, gain_half)
    mine, theirs = mine_at(idx_ref, half), theirs_at(idx_ref, half)
    hm, ho = hid_ref[:, mine], hid_ref[:, theirs]
    square = jnp.sum(hm * hm, axis=1, keepdims=True) + jnp.sum(ho * ho, axis=1, keepdims=True)
    root = lax.rsqrt(square / (2 * half) + 1e-6)
    dm, do = dm_ref[...], do_ref[...]
    g2m_ref[...] = jnp.sum(dm * hm * root, axis=0, keepdims=True)
    g2o_ref[...] = jnp.sum(do * ho * root, axis=0, keepdims=True)
    dm = dm * packed_row(own_ref, *place_g2)
    do = do * packed_row(pack_ref, *place_g2)
    along = jnp.sum(dm * hm, axis=1, keepdims=True) + jnp.sum(do * ho, axis=1, keepdims=True)
    along = along * (root * root * root) / (2 * half)
    hg_ref[:, mine] = e_ref[:, mine].astype(F32) + dm * root - hm * along
    hg_ref[:, theirs] = e_ref[:, theirs].astype(F32) + do * root - ho * along
    low = hg_ref[...].astype(BF16)
    hl_ref[...] = low
    half = wo_own.shape[0]
    gated[:, mine_at(idx_ref, half)] = dot_t(low, wo_own[...])
    gated[:, theirs_at(idx_ref, half)] = dot_t(low, wo_oth[...])
    gain[:, mine_at(idx_ref, gain_half)] = packed_row(own_ref, *place_hg)
    gain[:, theirs_at(idx_ref, gain_half)] = packed_row(pack_ref, *place_hg)
    head_gain = gain[...]
    wide = qb_ref.shape[1] // HEADS
    tall = mixture_ref.shape[1] // HEADS
    factor = wide ** (-0.5)
    quarter = state.shape[1]
    per = tall // quarter
    gain_grad = jnp.zeros((1, tall), F32)
    for s in range(seqs):
        at = slice(s * span, (s + 1) * span)
        for h in range(HEADS):
            vs = slice(h * tall, (h + 1) * tall)
            hs = slice(h * wide, (h + 1) * wide)
            mixture, opened, grad = mixture_ref[at, vs], og_ref[at, vs], gated[at, vs]
            root = lax.rsqrt(jnp.mean(mixture * mixture, axis=1, keepdims=True) + 1e-5)
            sig = sigmoid(opened)
            flat = mixture * root
            ol_ref[at, vs] = (grad * flat * head_gain * sig * (1.0 + opened * (1.0 - sig))).astype(BF16)
            grad = grad * (opened * sig)
            gain_grad += jnp.sum(grad * flat, axis=0, keepdims=True)
            grad = grad * head_gain
            along = jnp.mean(grad * flat, axis=1, keepdims=True)
            mixed = (grad - flat * along) * (root * factor)
            mg_ref[at, vs] = mixed
            part = t_dot(mixed.astype(BF16), qb_ref[at, hs])
            for q in range(per):
                state[s * per + q, :, hs] = part[q * quarter : (q + 1) * quarter]
    gain_sum[...] = gain_grad
    hgm_ref[...] = gain_sum[:, mine_at(idx_ref, gain_half)]
    hgo_ref[...] = gain_sum[:, theirs_at(idx_ref, gain_half)]
    totals = [tot_ref[pl.ds(s, 1), :] for s in range(seqs)]
    write_quarters(idx_ref, state, totals, (m0, m1, m2, m3), seqs)


def inner_back_kernel(dims, idx_ref, q_ref, k_ref, v_ref, lg_ref, a_ref, mg_ref, qb_ref, st_ref,
                      dq_ref, dk_ref, dv_ref, dc_ref):
    seqs, span = dims
    row, col = pair_iota(span)
    upto = (col <= row).astype(F32).astype(BF16)
    diagonal = row == col
    levels = level_masks(span)
    wide = q_ref.shape[1] // HEADS
    tall = v_ref.shape[1] // HEADS
    quarter = st_ref.shape[1]
    per = tall // quarter
    for s in range(seqs):
        at = slice(s * span, (s + 1) * span)
        logits = lg_ref[at, :]
        decays = (jnp.minimum(logits, 0.0) - jnp.log1p(jnp.exp(-jnp.abs(logits)))) / 16.0
        high, rest = two_part(decays)
        qs32, ks32 = q_ref[at, :].astype(F32), k_ref[at, :].astype(F32)
        begun = jnp.exp(dot(upto, high) + dot(upto, rest))
        pair_grads = []
        for h in range(HEADS):
            hs = slice(h * wide, (h + 1) * wide)
            vs = slice(h * tall, (h + 1) * tall)
            mixed, more = two_part(mg_ref[at, vs])
            values = v_ref[at, vs]
            full = dot_t(mixed, values) + dot_t(more, values)
            back = dot_t(values, mixed) + dot_t(values, more)
            pair_grads.append(jnp.where(row >= col, full, back))
            dv_ref[at, vs] = t_dot(a_ref[s * HEADS + h], mixed)
            own = jnp.sum(jnp.where(diagonal, full, 0.0), axis=1, keepdims=True)
            crossed = jnp.zeros((span, wide), F32)
            for q in range(per):
                part = slice(h * tall + q * quarter, h * tall + (q + 1) * quarter)
                crossed += dot(mg_ref[at, part].astype(BF16), st_ref[s * per + q, :, hs])
            dq_ref[at, hs] = own * ks32[:, hs] + begun[:, hs] * crossed
            dk_ref[at, hs] = own * qs32[:, hs]
            dc_ref[at, hs] = qb_ref[at, hs].astype(F32) * crossed
        for sums, _, both, half in levels:
            fade = jnp.exp(dot(sums, high) + dot(sums, rest))
            upper = upper_rows(half, qs32.shape[1], span)
            side = (jnp.where(upper, qs32, ks32) * fade).astype(BF16)
            for h in range(HEADS):
                hs = slice(h * wide, (h + 1) * wide)
                grads = dot(jnp.where(both, pair_grads[h], 0.0).astype(BF16), side[:, hs])
                moved = side[:, hs].astype(F32) * grads
                faded = fade[:, hs] * grads
                over = upper[:, hs]
                dc_ref[at, hs] += jnp.where(over, moved, -moved)
                dq_ref[at, hs] += jnp.where(over, faded, 0.0)
                dk_ref[at, hs] += jnp.where(over, 0.0, faded)


def inputs_back_kernel(dims, idx_ref, dq_ref, dk_ref, dv_ref, dc_ref, ol_ref, kd_ref, v_ref, lg_ref, tot_ref, st_ref,
                       l0, l1, l2, l3, x_ref, hg_ref, wq_own, wq_oth, wk_own, wk_oth, wv_own, wv_oth,
                       wg_own, wg_oth, own_ref, pack_ref, g2o_ref, hgo_ref,
                       tg_ref, ga_ref, llm_ref, g1m_ref, bm_ref, small_ref,
                       leaving, logit, bias):
    seqs, span = dims
    half = wq_own.shape[0]
    part = wq_own.shape[1] // 2
    place_g1, _, _, _ = packed_places(half, part, 0)
    li_own, lo_own = packed_factors(own_ref, half)
    li_oth, lo_oth = packed_factors(pack_ref, half)
    load_state(idx_ref, (l0, l1, l2, l3), leaving)
    row, col = pair_iota(span)
    later = (col > row).astype(F32).astype(BF16)
    since = (col >= row).astype(F32).astype(BF16)
    before = (col < row).astype(F32).astype(BF16)
    keys = kd_ref.shape[1]
    vals = v_ref.shape[1]
    wide, tall = keys // HEADS, vals // HEADS
    quarter = st_ref.shape[1]
    per = tall // quarter
    bias_sum = jnp.zeros((1, keys), F32)
    for s in range(seqs):
        at = slice(s * span, (s + 1) * span)
        logits = lg_ref[at, :]
        decays = (jnp.minimum(logits, 0.0) - jnp.log1p(jnp.exp(-jnp.abs(logits)))) / 16.0
        ahead = jnp.exp(mask_dot(later, decays))
        for h in range(HEADS):
            hs = slice(h * wide, (h + 1) * wide)
            faded = kd_ref[at, hs]
            grads = jnp.zeros((span, wide), F32)
            ends = jnp.zeros((1, wide), F32)
            for q in range(per):
                vs = slice(h * tall + q * quarter, h * tall + (q + 1) * quarter)
                at_v = slice(keys * 2 + vs.start, keys * 2 + vs.stop)
                part = leaving[s * per + q, :, hs]
                ga_ref[at, at_v] = (dv_ref[at, vs] + dot_t(faded, part)).astype(BF16)
                grads += dot(v_ref[at, vs], part)
                ends += jnp.sum(
                    st_ref[s * per + q, :, hs].astype(F32) * part.astype(F32), axis=0, keepdims=True
                )
            moved = faded.astype(F32) * grads
            ga_ref[at, keys + h * wide : keys + (h + 1) * wide] = (
                dk_ref[at, hs] + ahead[:, hs] * grads
            ).astype(BF16)
            decay_grad = (
                mask_dot(since, dc_ref[at, hs])
                + mask_dot(before, moved)
                + tot_ref[pl.ds(s, 1), hs] * ends
            )
            logit_grad = decay_grad * sigmoid(-logits[:, hs]) / 16.0
            bias[:, hs] = jnp.sum(logit_grad, axis=0, keepdims=True)
            logit[at, hs] = logit_grad.astype(BF16)
        bias_sum += bias[...]
    bias[...] = bias_sum
    part = keys // 2
    bm_ref[...] = bias[:, mine_at(idx_ref, part)]
    small_ref[:, 2 * half : 2 * half + part] = bias[:, theirs_at(idx_ref, part)]
    small_ref[:, half : 2 * half] = g2o_ref[...]
    small_ref[:, 2 * half + part :] = hgo_ref[...]
    ga_ref[:, 0:keys] = dq_ref[...].astype(BF16)
    ga_ref[:, 2 * keys + vals : 2 * keys + 2 * vals] = ol_ref[...]
    llm, llo = logit[:, mine_at(idx_ref, part)], logit[:, theirs_at(idx_ref, part)]
    llm_ref[...] = llm
    lrg = (dot_t(llm, lo_own) + dot_t(llo, lo_oth)).astype(BF16)
    rest = jnp.zeros((lrg.shape[0], 128 - RANK), BF16)
    lanes = 2 * keys + 2 * vals + 128
    ga_ref[:, lanes - 128 : lanes] = jnp.concatenate([lrg, rest], axis=1)
    ga_ref[:, lanes:] = llo
    qg, kg = ga_ref[:, 0:keys], ga_ref[:, keys : 2 * keys]
    vg = ga_ref[:, 2 * keys : 2 * keys + vals]
    og = ga_ref[:, 2 * keys + vals : 2 * keys + 2 * vals]
    dm = dot_t(qg, wq_own[...]) + dot_t(kg, wk_own[...]) + dot_t(vg, wv_own[...])
    dm = dm + dot_t(og, wg_own[...]) + dot(lrg, li_own)
    do = dot_t(qg, wq_oth[...]) + dot_t(kg, wk_oth[...]) + dot_t(vg, wv_oth[...])
    do = do + dot_t(og, wg_oth[...]) + dot(lrg, li_oth)
    mine, theirs = mine_at(idx_ref, half), theirs_at(idx_ref, half)
    xm, xo = x_ref[:, mine].astype(F32), x_ref[:, theirs].astype(F32)
    square = jnp.sum(xm * xm, axis=1, keepdims=True) + jnp.sum(xo * xo, axis=1, keepdims=True)
    root = lax.rsqrt(square / (2 * half) + 1e-6)
    g1m_ref[...] = jnp.sum(dm * xm * root, axis=0, keepdims=True)
    small_ref[:, 0:half] = jnp.sum(do * xo * root, axis=0, keepdims=True)
    dm = dm * packed_row(own_ref, *place_g1)
    do = do * packed_row(pack_ref, *place_g1)
    along = jnp.sum(dm * xm, axis=1, keepdims=True) + jnp.sum(do * xo, axis=1, keepdims=True)
    along = along * (root * root * root) / (2 * half)
    tg_ref[:, mine] = hg_ref[:, mine] + dm * root - xm * along
    tg_ref[:, theirs] = hg_ref[:, theirs] + do * root - xo * along


def block_of(position, order):
    block = 0
    for at, bit in enumerate(order):
        if (position >> (3 - at)) & 1:
            block |= bit
    return block


def deal(position, keep_ref, send_ref):
    return keep_ref.at[position] if position < 8 else send_ref.at[position - 8]


def wide_grad_kernel(orders, idx_ref, sm_ref, so_ref, gm_ref, go_ref, k0, s0, k1, s1, full):
    place = lax.rem(idx_ref[1], 16)
    width = full.shape[1]
    high = full.shape[0] // 16
    for which, refs in enumerate(((k0, s0), (k1, s1))):
        cols = slice(which * width, (which + 1) * width)
        full[...] = t_dot(sm_ref[...], gm_ref[:, cols]) + t_dot(so_ref[...], go_ref[:, cols])
        for position in range(16):
            block = block_of(position, orders[which]) ^ place
            rows = full[pl.ds(pl.multiple_of(block * high, high), high), :].astype(BF16)
            to = deal(position, *refs)
            for tile in range(width // 128):
                to[tile * high : (tile + 1) * high, :] = rows[:, tile * 128 : (tile + 1) * 128]


def down_grad_kernel(order, idx_ref, am_ref, go_ref, em_ref, eo_ref, keep_ref, send_ref, full):
    place = lax.rem(idx_ref[1], 16)
    first = go_ref.shape[1] - am_ref.shape[1]
    full[...] = t_dot(am_ref[...], em_ref[...]) + t_dot(go_ref[:, first:], eo_ref[...])
    high = full.shape[0] // 2
    for position in range(16):
        block = block_of(position, order) ^ place
        rows = pl.ds(pl.multiple_of(lax.div(block, 8) * high, 16), high)
        cols = pl.ds(pl.multiple_of(lax.rem(block, 8) * 128, 128), 128)
        deal(position, keep_ref, send_ref)[...] = full[rows, cols].astype(BF16)


def attention_grad_kernel(orders, cuts, idx_ref, nm_ref, no_ref, gm_ref, go_ref, am_ref, ao_ref, hm_ref, ho_ref,
                          lrm_ref, lro_ref, llm_ref, g1_ref, g2_ref, b_ref, hg_ref, small_ref, k0, s0, k1, s1, k2, s2, full, outer, small):
    place = lax.rem(idx_ref[1], 16)
    lanes = full.shape[1]
    full[...] = t_dot(nm_ref[...], gm_ref[:, 0:lanes]) + t_dot(no_ref[...], go_ref[:, 0:lanes])
    outer[...] = t_dot(am_ref[...], hm_ref[...]) + t_dot(ao_ref[...], ho_ref[...])
    low_out = t_dot(lrm_ref[...], llm_ref[...]) + t_dot(lro_ref[...], go_ref[:, lanes:])
    small[...] = jnp.zeros_like(small)
    small[0] = low_out[:, 0:128]
    small[1] = low_out[:, 128:256]
    line = 0
    for ref in (g1_ref, g2_ref, b_ref, hg_ref):
        row = ref[...] + small_ref[:, line * 128 : line * 128 + ref.shape[1]]
        for tile in range(row.shape[1] // 128):
            small[2, line : line + 1, :] = row[:, tile * 128 : (tile + 1) * 128]
            line += 1
    high = full.shape[0] // 16
    tiles = full.shape[1] // 128
    for which, refs in enumerate(((k0, s0), (k1, s1), (k2, s2))):
        first, last = cuts[which], cuts[which + 1]
        for position in range(16):
            block = block_of(position, orders[which]) ^ place
            at = pl.ds(pl.multiple_of(block * high, high), high)
            to = deal(position, *refs)
            for tile in range(first, last):
                if tile < tiles:
                    rows = full[at, tile * 128 : (tile + 1) * 128]
                else:
                    rows = outer[at, (tile - tiles) * 128 : (tile - tiles + 1) * 128]
                to[(tile - first) * high : (tile - first + 1) * high, :] = rows.astype(BF16)
            if which == 2:
                to[(last - first) * high :, :] = small[block].astype(BF16)


def wide_open_kernel(order, idx_ref, own_ref, got_ref, out_ref):
    place = lax.rem(idx_ref[1], 16)
    high = out_ref.shape[0] // 16
    for position in range(16):
        block = block_of(position, order) ^ place
        held = deal(position, own_ref, got_ref)
        at = pl.ds(pl.multiple_of(block * high, high), high)
        for tile in range(out_ref.shape[1] // 128):
            out_ref[at, tile * 128 : (tile + 1) * 128] = held[tile * high : (tile + 1) * high, :].astype(F32)


def down_open_kernel(order, idx_ref, own_ref, got_ref, out_ref):
    place = lax.rem(idx_ref[1], 16)
    high = out_ref.shape[0] // 2
    for position in range(16):
        block = block_of(position, order) ^ place
        rows = pl.ds(pl.multiple_of(lax.div(block, 8) * high, 16), high)
        cols = pl.ds(pl.multiple_of(lax.rem(block, 8) * 128, 128), 128)
        out_ref[rows, cols] = deal(position, own_ref, got_ref)[...].astype(F32)


def attention_open_kernel(orders, cuts, idx_ref, o0, r0, o1, r1, o2, r2, q_ref, k_ref, v_ref, og_ref, li_ref, w_ref,
                          lo_ref, g1_ref, g2_ref, b_ref, hg_ref, small, first_factor):
    place = lax.rem(idx_ref[1], 16)
    high = q_ref.shape[0] // 16
    homes = []
    for ref in (q_ref, k_ref, v_ref, og_ref):
        homes += [(ref, tile) for tile in range(ref.shape[1] // 128)]
    homes.append((first_factor, 0))
    homes += [(w_ref, tile) for tile in range(w_ref.shape[1] // 128)]
    for which, refs in enumerate(((o0, r0), (o1, r1), (o2, r2))):
        first, last = cuts[which], cuts[which + 1]
        for position in range(16):
            block = block_of(position, orders[which]) ^ place
            at = pl.ds(pl.multiple_of(block * high, high), high)
            held = deal(position, *refs)
            for tile in range(first, last):
                rows = held[(tile - first) * high : (tile - first + 1) * high, :].astype(F32)
                ref, column = homes[tile]
                ref[at, column * 128 : (column + 1) * 128] = rows
            if which == 2:
                small[block] = held[(last - first) * high :, :].astype(F32)
    li_ref[...] = first_factor[...].T[0 : li_ref.shape[0], :]
    lo_ref[:, 0:128] = small[0]
    lo_ref[:, 128:256] = small[1]
    line = 0
    for ref in (g1_ref, g2_ref, b_ref, hg_ref):
        for tile in range(ref.shape[1] // 128):
            ref[:, tile * 128 : (tile + 1) * 128] = small[2, line : line + 1, :]
            line += 1


def across(array):
    return lax.ppermute(array, "fsdp", ((0, 1), (1, 0)))


def swap(array, bit):
    count = lax.axis_size("seq")
    return lax.ppermute(array, "seq", tuple((one, one ^ bit) for one in range(count)))


def ahead(array, step):
    count = lax.axis_size("seq")
    return lax.ppermute(
        array,
        "seq",
        tuple((one, one + step) for one in range(count) if 0 <= one + step < count),
    )


def fence(*groups):
    return lax.optimization_barrier(groups)


class Portions:
    def __init__(self, parts, orders):
        self.kept = [keep for keep, _ in parts]
        self.sent = [send for _, send in parts]
        self.orders = orders

    def move(self, arrays, step):
        if step < 3:
            return [swap(a, order[step]) for a, order in zip(arrays, self.orders)]
        return self.move_all(arrays, self.orders[0][3])

    def move_all(self, arrays, bit):
        got = swap(jnp.concatenate(arrays, axis=1), bit)
        ends = [0]
        for a in arrays:
            ends.append(ends[-1] + a.shape[1])
        return [got[:, first:last] for first, last in zip(ends[:-1], ends[1:])]

    def reduce_start(self, step):
        return self.move(self.sent, step)

    def reduce_end(self, step, got):
        for one, more in enumerate(got):
            if step < 3:
                half = more.shape[0] // 2
                self.sent[one] = self.kept[one][half:] + more[half:]
                self.kept[one] = self.kept[one][:half] + more[:half]
            else:
                self.kept[one] = self.kept[one] + more
        bit = 16
        while step == 3 and bit < lax.axis_size("seq"):
            more = self.move_all(self.kept, bit)
            self.kept = [k + m for k, m in zip(self.kept, more)]
            bit *= 2

    def gather_start(self, step):
        return self.move(self.kept, step)

    def gather_end(self, step, got):
        if step:
            self.kept = [jnp.concatenate([k, more], axis=0) for k, more in zip(self.kept, got)]
        else:
            self.halves = list(zip(self.kept, got))


def scan_near(messages):
    return [messages[0]] + [swap(messages[o], o) for o in (1, 2, 3)]


def scan_scratch(messages):
    rows, lanes = messages[0].shape
    return [((4, rows - 16, lanes), F32), ((4, 1, lanes), F32)]


def scan_total(near, idx, reverse):
    return call("group_total", partial(group_total, reverse), idx, near, [(near[0].shape, BF16)], scan_scratch(near))[0]


def scan_far(total, reverse):
    sign = -4 if reverse else 4
    return [ahead(total, sign * step) for step in range(1, lax.axis_size("seq") // 4)]


def scan_entering(far, near, idx, reverse):
    rows, lanes = near[0].shape
    return call(
        "group_entering", partial(group_entering, reverse, len(far)), idx, list(far) + list(near),
        [((rows - 16, lanes), BF16)] * 4, scan_scratch(near) + [((4, rows - 16, lanes), F32)],
    )


def shards(
    tokens,
    lengths,
    first_gain,
    query_weight,
    key_weight,
    value_weight,
    outgate_weight,
    lowrank_in,
    lowrank_out,
    decay_bias,
    head_gain,
    output_weight,
    second_gain,
    gate_weight,
    up_weight,
    down_weight,
    cotangent,
):
    micro_count, pair_count, span, width = tokens.shape
    seqs = micro_count * pair_count
    rows = seqs * span
    dims = (seqs, span)
    core = lax.axis_index("fsdp")
    place = lax.axis_index("seq")
    own_lengths = lax.dynamic_slice_in_dim(lengths, core * pair_count, pair_count, 1).reshape(-1)
    idx = jnp.concatenate([jnp.stack([core, place]).astype(jnp.int32), own_lengths])
    keys, vals, ff = query_weight.shape[1], value_weight.shape[1], gate_weight.shape[1]
    half = query_weight.shape[0]
    tall = vals // HEADS
    quarter = seqs * tall // 4

    x = tokens.reshape(rows, width)
    cot = cotangent.reshape(rows, width)
    lrank = lowrank_in.shape[1]
    lines, at = 0, 0
    for a in (first_gain, second_gain, decay_bias, head_gain):
        lines = lines + jnp.pad(a, (at, 16 * 128 - at - a.size))
        at += a.size
    lines = lines.reshape(16, 128)
    pack = call(
        "pack", pack_kernel, idx, [lowrank_in.T, lowrank_out, lines],
        [((lrank * (half + lowrank_out.shape[1]) // 128 + 16, 128), BF16)],
    )[0]
    pack2, wk2, wv2 = (across(a) for a in (pack, key_weight, value_weight))

    message = ((quarter + 16, keys), BF16)
    state = ((4, quarter, keys), F32)
    nm, no, k, v, lr, lg, kd, tot, *messages = call(
        "keys", partial(keys_kernel, dims), idx,
        [x, key_weight, wk2, value_weight, wv2, pack, pack2],
        [((rows, half), BF16), ((rows, half), BF16), ((rows, keys), BF16), ((rows, vals), BF16),
         ((rows, lrank), BF16), ((rows, keys), F32), ((rows, keys), BF16), ((seqs, keys), F32)]
        + [message] * 4,
        [state],
    )
    messages, outgate_send, query_send = fence(messages, outgate_weight, query_weight)
    near = scan_near(messages)
    wg2, wq2 = across(outgate_send), across(query_send)
    q, og, mix, scores, qb, cots = call(
        "inner", partial(inner_kernel, dims), idx,
        [nm, no, query_weight, wq2, outgate_weight, wg2, k, v, lg, cot],
        [((rows, keys), BF16), ((rows, vals), F32), ((rows, vals), F32), ((seqs * HEADS, span, span), BF16),
         ((rows, keys), BF16), ((rows, width), BF16)],
    )
    near, mix, gate_send, up_send = fence(near, mix, gate_weight, up_weight)
    total = scan_total(near, idx, False)
    total, gate_send, up_send = fence(total, gate_send, up_send)
    far = scan_far(total, False)
    wgate2, wup2 = across(gate_send), across(up_send)
    far, wgate2, wup2 = fence(far, wgate2, wup2)
    pieces = scan_entering(far, near, idx, False)
    pieces, output_send, down_send = fence(pieces, output_weight, down_weight)
    pieces = [pieces[0]] + [swap(pieces[o], o) for o in (1, 2, 3)]
    wo2, wdown2 = across(output_send), across(down_send)
    mixture, gm, go, hid, sm, so, st = call(
        "hidden", partial(hidden_kernel, dims), idx,
        [mix, qb, *pieces, og, x, output_weight, wo2, pack, pack2],
        [((rows, vals), F32), ((rows, vals // 2), BF16), ((rows, vals // 2), BF16), ((rows, width), F32),
         ((rows, half), BF16), ((rows, half), BF16), ((4, quarter, keys), BF16)],
        [((1, tall), F32), ((rows, vals), BF16)],
    )
    so, no_send, lr_send, cots_send = fence(so, no, lr, cots)
    so2, no2, go2, lr2, cots2 = (across(a) for a in (so, no_send, go, lr_send, cots_send))
    out, am, gu, dm, do = call(
        "ffn", partial(ffn_kernel, dims), idx,
        [sm, so, hid, cots, gate_weight, wgate2, up_weight, wup2, down_weight, wdown2],
        [((rows, width), F32), ((rows, ff // 2), BF16), ((rows, 5 * ff // 2), BF16),
         ((rows, half), F32), ((rows, half), F32)],
        [((2, 2, half, ff // 2), BF16), ((2, 2, half, ff // 2), BF16), ((2, ff // 2, width), BF16),
         pltpu.SemaphoreType.DMA((4, 5))], limit=42, far=6,
    )
    so2, no2, go2, lr2, cots2, gu, dm = fence(so2, no2, go2, lr2, cots2, gu, dm)

    orders = ((1, 2, 4, 8), (2, 4, 1, 8), (4, 1, 2, 8))
    hg, hl, mg, ol, g2m, g2o, hgm, hgo, *messages = call(
        "gate_back", partial(gate_back_kernel, dims), idx,
        [hid, dm, do, cots, output_weight, wo2, mixture, og, qb, tot, pack, pack2],
        [((rows, width), F32), ((rows, width), BF16), ((rows, vals), F32), ((rows, vals), BF16),
         ((1, half), F32), ((1, half), F32), ((1, tall // 2), F32), ((1, tall // 2), F32)] + [message] * 4,
        [((1, tall), F32), ((rows, vals), F32), ((1, tall), F32), state],
    )
    messages, gu_send, mg = fence(messages, gu, mg)
    near = scan_near(messages)
    gu2 = across(gu_send)
    dq, dk, dv, dc = call(
        "inner_back", partial(inner_back_kernel, dims), idx, [q, k, v, lg, scores, mg, qb, st],
        [((rows, keys), F32), ((rows, keys), F32), ((rows, vals), F32), ((rows, keys), F32)],
    )
    near, gu2, dq = fence(near, gu2, dq)
    total = scan_total(near, idx, True)
    total, gu2 = fence(total, gu2)
    far = scan_far(total, True)
    portion = ff // 128 * (half // 16)
    flat = [((8, portion, 128), BF16)] * 2
    wide_parts = call("wide_grad", partial(wide_grad_kernel, orders), idx, [sm, so2, gu, gu2], flat * 2,
                      [((half, ff), F32)], limit=32)
    am, wide_parts = fence(am, wide_parts)
    down_parts = call("down_grad", partial(down_grad_kernel, orders[2]), idx, [am, gu2, cots, cots2], flat,
                      [((ff // 2, width), F32)])
    far, down_parts = fence(far, down_parts)
    first = Portions([wide_parts[0:2], wide_parts[2:4], down_parts], orders)
    got = first.reduce_start(0)
    pieces = scan_entering(far, near, idx, True)
    pieces = [pieces[0]] + [swap(pieces[o], o) for o in (1, 2, 3)]
    got, pieces = fence(got, pieces)
    first.reduce_end(0, got)
    first.sent, pieces = fence(first.sent, pieces)
    got = first.reduce_start(1)
    lanes = 2 * keys + 2 * vals + 128
    tg, ga, llm, g1m, bm, small = call(
        "inputs_back", partial(inputs_back_kernel, dims), idx,
        [dq, dk, dv, dc, ol, kd, v, lg, tot, st, *pieces, x, hg, query_weight, wq2, key_weight, wk2,
         value_weight, wv2, outgate_weight, wg2, pack, pack2, g2o, hgo],
        [((rows, width), F32), ((rows, lanes + keys // 2), BF16), ((rows, keys // 2), BF16),
         ((1, half), F32), ((1, keys // 2), F32), ((1, 2 * half + keys // 2 + tall // 2), F32)],
        [((4, quarter, keys), BF16), ((rows, keys), BF16), ((1, keys), F32)], limit=32,
    )
    got, ga, small = fence(got, ga, small)
    first.reduce_end(1, got)
    got = first.reduce_start(2)
    ga2, small2, hl2 = across(ga), across(small), across(hl)
    tiles = lanes // 128 + width // 128
    cuts = (0, tiles // 3, 2 * tiles // 3, tiles)
    high = half // 16
    shapes = []
    for which in range(3):
        size = (cuts[which + 1] - cuts[which]) * high + (16 if which == 2 else 0)
        shapes += [((8, size, 128), BF16)] * 2
    parts = call(
        "attention_grad", partial(attention_grad_kernel, orders, cuts), idx,
        [nm, no2, ga, ga2, gm, go2, hl, hl2, lr, lr2, llm, g1m, g2m, bm, hgm, small2],
        shapes, [((half, lanes), F32), ((vals // 2, width), F32), ((16, 16, 128), F32)], limit=32,
    )
    got, parts = fence(got, parts)
    first.reduce_end(2, got)
    second = Portions([parts[0:2], parts[2:4], parts[4:6]], orders)
    got, more = fence(first.reduce_start(3), second.reduce_start(0))
    first.reduce_end(3, got)
    second.reduce_end(0, more)
    got, more = fence(first.gather_start(3), second.reduce_start(1))
    first.gather_end(3, got)
    second.reduce_end(1, more)
    both = [jnp.concatenate([k, a], axis=1) for k, a in zip(first.kept, second.sent)]
    both = fence(*[swap(a, order[2]) for a, order in zip(both, orders)])
    got = [a[:, : k.shape[1]] for a, k in zip(both, first.kept)]
    more = [a[:, k.shape[1] :] for a, k in zip(both, first.kept)]
    first.gather_end(2, got)
    second.reduce_end(2, more)
    got, more = fence(first.gather_start(1), second.reduce_start(3))
    first.gather_end(1, got)
    second.reduce_end(3, more)
    got, more = fence(first.gather_start(0), second.gather_start(3))
    first.gather_end(0, got)
    second.gather_end(3, more)
    gate_halves, up_halves, down_halves = first.halves
    more = second.gather_start(2)
    gate_out = call("gate_open", partial(wide_open_kernel, orders[0]), idx, gate_halves, [((half, ff), F32)])[0]
    more, gate_out = fence(more, gate_out)
    second.gather_end(2, more)
    more = second.gather_start(1)
    up_out = call("up_open", partial(wide_open_kernel, orders[1]), idx, up_halves, [((half, ff), F32)])[0]
    more, up_out = fence(more, up_out)
    second.gather_end(1, more)
    more = second.gather_start(0)
    down_out = call("down_open", partial(down_open_kernel, orders[2]), idx, down_halves, [((ff // 2, width), F32)])[0]
    more, down_out = fence(more, down_out)
    second.gather_end(0, more)
    opened = call(
        "attention_open", partial(attention_open_kernel, orders, cuts), idx, [a for pair in second.halves for a in pair],
        [((half, keys), F32), ((half, keys), F32), ((half, vals), F32), ((half, vals), F32),
         ((lrank, half), F32), ((vals // 2, width), F32), ((lrank, keys // 2), F32),
         ((1, half), F32), ((1, half), F32), ((1, keys // 2), F32), ((1, tall // 2), F32)],
        [((16, 16, 128), F32), ((half, 128), F32)],
    )
    q_out, k_out, v_out, og_out, li_out, w_out, lo_out, g1_out, g2_out, b_out, hg_out = opened
    return (
        out.reshape(tokens.shape),
        tg.reshape(tokens.shape),
        g1_out.reshape(-1),
        q_out,
        k_out,
        v_out,
        og_out,
        li_out.T,
        lo_out,
        b_out.reshape(-1),
        hg_out.reshape(-1),
        w_out,
        g2_out.reshape(-1),
        gate_out,
        up_out,
        down_out,
    )


def solution(mesh):
    shard, column = P("fsdp", None), P(None, "fsdp")
    stream, line = P(None, "fsdp", "seq", None), P("fsdp")
    weights = (line, shard, shard, shard, shard, shard, column, line, line, shard, line, shard, shard, shard)
    return jax.shard_map(
        shards,
        mesh=mesh,
        in_specs=(stream, P()) + weights + (stream,),
        out_specs=(stream, stream) + weights,
        check_vma=False,
    )
```

```python
from functools import partial

import jax
import jax.numpy as jnp
from jax import lax
from jax.experimental import pallas as pl
from jax.experimental.pallas import tpu as pltpu
from jax.sharding import PartitionSpec as P

HEADS = 4
RANK = 16
F32 = jnp.float32
BF16 = jnp.bfloat16
MIB = 1024 * 1024


def dot(first_op, second_op):
    return jnp.dot(first_op, second_op, preferred_element_type=F32)


def dot_t(first_op, second_op):
    return lax.dot_general(
        first_op, second_op, (((1,), (1,)), ((), ())), preferred_element_type=F32
    )


def t_dot(first_op, second_op):
    return lax.dot_general(
        first_op, second_op, (((0,), (0,)), ((), ())), preferred_element_type=F32
    )


def two_part(value):
    high = value.astype(BF16)
    return high, (value - high.astype(F32)).astype(BF16)


def mask_dot(mask, value):
    high, rest = two_part(value)
    return dot(mask, high) + dot(mask, rest)


def sigmoid(value):
    return 1.0 / (1.0 + jnp.exp(-value))


def pair_iota(size):
    return (
        lax.broadcasted_iota(jnp.int32, (size, size), 0),
        lax.broadcasted_iota(jnp.int32, (size, size), 1),
    )


def level_masks(size):
    row, col = pair_iota(size)
    out = []
    half = size // 2
    while half >= 1:
        block = 2 * half
        row_block = row // block
        middle = row_block * block + half - 1
        upper = row > middle
        sums = (upper & (col > middle) & (col <= row)) | (
            jnp.logical_not(upper) & (col > row) & (col <= middle)
        )
        same = row_block == col // block
        pairs = same & upper & (col <= middle)
        both = same & (upper != (col > middle))
        out.append((sums.astype(F32).astype(BF16), pairs, both, half))
        half //= 2
    return out


def upper_rows(half, width, size):
    row = lax.broadcasted_iota(jnp.int32, (size, width), 0)
    return row % (2 * half) >= half


def seat(idx_ref):
    return idx_ref[0], idx_ref[1]


def mine_at(idx_ref, width):
    return pl.ds(pl.multiple_of(idx_ref[0] * width, 128), width)


def theirs_at(idx_ref, width):
    return pl.ds(pl.multiple_of((1 - idx_ref[0]) * width, 128), width)


SMEM = pl.BlockSpec(memory_space=pltpu.SMEM)
VMEM = pl.BlockSpec(memory_space=pltpu.VMEM)


def call(name, body, idx, inputs, outs, scratch=(), limit=24, far=0):
    shapes = [jax.ShapeDtypeStruct(s, d) for s, d in outs]
    result = pl.pallas_call(
        body,
        name=name,
        out_shape=shapes,
        in_specs=[SMEM] + [VMEM] * (len(inputs) - far) + [pl.BlockSpec(memory_space=pl.ANY)] * far,
        out_specs=[VMEM] * len(shapes),
        scratch_shapes=[pltpu.VMEM(*s) if isinstance(s, tuple) else s for s in scratch],
        compiler_params=pltpu.CompilerParams(vmem_limit_bytes=limit * MIB),
        cost_estimate=pl.CostEstimate(flops=1, bytes_accessed=1, transcendentals=0),
    )(idx, *inputs)
    return result


def put_message(ref, rows, total):
    count = rows.shape[0]
    ref[pl.ds(0, count), :] = rows.astype(BF16)
    high = total.astype(BF16)
    rest = total - high.astype(F32)
    middle = rest.astype(BF16)
    low = (rest - middle.astype(F32)).astype(BF16)
    tail = jnp.concatenate(
        [high, middle, low, jnp.zeros((13,) + total.shape[1:], BF16)], axis=0
    )
    ref[pl.ds(count, 16), :] = tail


def get_message(ref):
    count = ref.shape[0] - 16
    tail = ref[pl.ds(count, 16), :].astype(F32)
    return ref[pl.ds(0, count), :].astype(F32), tail[0:1] + tail[1:2] + tail[2:3]


def write_quarters(idx_ref, state, totals, messages, seq_count):
    low = lax.rem(idx_ref[1], 4)
    for other in range(4):
        quarter = low ^ other
        total = totals[0]
        for one in range(1, seq_count):
            total = jnp.where(quarter * seq_count // 4 >= one, totals[one], total)
        put_message(messages[other], state[quarter], total)


def group_total(reverse, idx_ref, *refs):
    out_ref, kept, held = refs[4], refs[5], refs[6]
    low = lax.rem(idx_ref[1], 4)
    for other in range(4):
        rows, total = get_message(refs[other])
        kept[low ^ other] = rows
        held[low ^ other] = total
    order = (3, 2, 1, 0) if reverse else (0, 1, 2, 3)
    rows, total = kept[order[0]], held[order[0]]
    for one in order[1:]:
        rows = held[one] * rows + kept[one]
        total = total * held[one]
    put_message(out_ref, rows, total)


def group_entering(reverse, far_count, idx_ref, *refs):
    far, near = refs[:far_count], refs[far_count : far_count + 4]
    outs = refs[far_count + 4 : far_count + 8]
    kept, held, entering = refs[far_count + 8 :]
    low = lax.rem(idx_ref[1], 4)
    for other in range(4):
        rows, total = get_message(near[other])
        kept[low ^ other] = rows
        held[low ^ other] = total
    rows = jnp.zeros(kept.shape[1:], F32)
    for one in far[::-1]:
        part, total = get_message(one)
        rows = total * rows + part
    for one in (3, 2, 1, 0) if reverse else (0, 1, 2, 3):
        entering[one] = rows
        rows = held[one] * rows + kept[one]
    for other in range(4):
        outs[other][...] = entering[low ^ other].astype(BF16)


def load_state(idx_ref, pieces, state):
    low = lax.rem(idx_ref[1], 4)
    for other in range(4):
        state[low ^ other] = pieces[other][...]


def pack_kernel(idx_ref, li_ref, lo_ref, lines_ref, out_ref):
    at = 0
    for ref in (li_ref, lo_ref):
        rank = ref.shape[0]
        for tile in range(ref.shape[1] // 128):
            out_ref[at : at + rank, :] = ref[:, tile * 128 : (tile + 1) * 128]
            at += rank
    out_ref[at:, :] = lines_ref[...]


def packed_factors(pack_ref, half):
    rank = RANK
    high = pack_ref.shape[0] - 16
    tiles = [pack_ref[at : at + rank, :] for at in range(0, high, rank)]
    first = half // 128
    return jnp.concatenate(tiles[:first], axis=1), jnp.concatenate(tiles[first:], axis=1)


def packed_row(pack_ref, first, count):
    lines = pack_ref[pack_ref.shape[0] - 16 :, :].astype(F32)
    return jnp.concatenate([lines[t : t + 1, :] for t in range(first, first + count)], axis=1)


def packed_places(half, part, gain):
    g1, b, hg = half // 128, part // 128, gain // 128
    return (0, g1), (g1, g1), (2 * g1, b), (2 * g1 + b, hg)


def keys_kernel(dims, idx_ref, x_ref, wk_own, wk_oth, wv_own, wv_oth, own_ref, pack_ref,
                nm_ref, no_ref, k_ref, v_ref, lr_ref, lg_ref, kd_ref, tot_ref,
                m0, m1, m2, m3, state):
    seqs, span = dims
    half = wk_own.shape[0]
    part = wk_own.shape[1] // 2
    place_g1, _, place_b, _ = packed_places(half, part, 0)
    li_own, lo_own = packed_factors(own_ref, half)
    li_oth, lo_oth = packed_factors(pack_ref, half)
    g1_own, b_own = packed_row(own_ref, *place_g1), packed_row(own_ref, *place_b)
    g1_oth, b_oth = packed_row(pack_ref, *place_g1), packed_row(pack_ref, *place_b)
    xm = x_ref[:, mine_at(idx_ref, half)].astype(F32)
    xo = x_ref[:, theirs_at(idx_ref, half)].astype(F32)
    square = jnp.sum(xm * xm, axis=1, keepdims=True) + jnp.sum(xo * xo, axis=1, keepdims=True)
    root = lax.rsqrt(square / (2 * half) + 1e-6)
    nm = (xm * root * g1_own).astype(BF16)
    no = (xo * root * g1_oth).astype(BF16)
    nm_ref[...] = nm
    no_ref[...] = no
    lr = (dot_t(nm, li_own) + dot_t(no, li_oth)).astype(BF16)
    lr_ref[...] = lr
    lg_ref[:, mine_at(idx_ref, part)] = dot(lr, lo_own) + b_own
    lg_ref[:, theirs_at(idx_ref, part)] = dot(lr, lo_oth) + b_oth
    keys = (dot(nm, wk_own[...]) + dot(no, wk_oth[...])).astype(BF16)
    k_ref[...] = keys
    values = (dot(nm, wv_own[...]) + dot(no, wv_oth[...])).astype(BF16)
    v_ref[...] = values
    row, col = pair_iota(span)
    later = (col > row).astype(F32).astype(BF16)
    wide = keys.shape[1] // HEADS
    tall = values.shape[1] // HEADS
    quarter = state.shape[1]
    totals = []
    for s in range(seqs):
        at = slice(s * span, (s + 1) * span)
        logits = lg_ref[at, :]
        decays = (jnp.minimum(logits, 0.0) - jnp.log1p(jnp.exp(-jnp.abs(logits)))) / 16.0
        ahead = mask_dot(later, decays)
        totals.append(jnp.exp(jnp.sum(decays, axis=0, keepdims=True)))
        tot_ref[pl.ds(s, 1), :] = totals[s]
        faded = (keys[at].astype(F32) * jnp.exp(ahead)).astype(BF16)
        kd_ref[at, :] = faded
        for h in range(HEADS):
            part = t_dot(values[at, h * tall : (h + 1) * tall], faded[:, h * wide : (h + 1) * wide])
            per = tall // quarter
            for q in range(per):
                state[s * per + q, :, h * wide : (h + 1) * wide] = part[q * quarter : (q + 1) * quarter]
    write_quarters(idx_ref, state, totals, (m0, m1, m2, m3), seqs)


def inner_kernel(dims, idx_ref, nm_ref, no_ref, wq_own, wq_oth, wg_own, wg_oth, k_ref, v_ref, lg_ref, cot_ref,
                 q_ref, og_ref, mix_ref, a_ref, qb_ref, e_ref):
    seqs, span = dims
    for s in range(seqs):
        at = slice(s * span, (s + 1) * span)
        places = lax.broadcasted_iota(jnp.int32, (span, cot_ref.shape[1]), 0) + idx_ref[1] * span
        e_ref[at, :] = jnp.where(places < idx_ref[2 + s], cot_ref[at, :].astype(F32), 0.0).astype(BF16)
    nm, no = nm_ref[...], no_ref[...]
    queries = (dot(nm, wq_own[...]) + dot(no, wq_oth[...])).astype(BF16)
    q_ref[...] = queries
    og_ref[...] = dot(nm, wg_own[...]) + dot(no, wg_oth[...])
    row, col = pair_iota(span)
    upto = (col <= row).astype(F32).astype(BF16)
    diagonal = row == col
    levels = level_masks(span)
    wide = queries.shape[1] // HEADS
    tall = v_ref.shape[1] // HEADS
    def one_sequence(s, carry):
        at = pl.ds(pl.multiple_of(s * span, span), span)
        logits = lg_ref[at, :]
        decays = (jnp.minimum(logits, 0.0) - jnp.log1p(jnp.exp(-jnp.abs(logits)))) / 16.0
        high, rest = two_part(decays)
        qs, ks = q_ref[at, :], k_ref[at, :]
        qs32, ks32 = qs.astype(F32), ks.astype(F32)
        qb_ref[at, :] = (qs32 * jnp.exp(dot(upto, high) + dot(upto, rest))).astype(BF16)
        scores = []
        for h in range(HEADS):
            hs = slice(h * wide, (h + 1) * wide)
            scores.append(jnp.where(diagonal, dot_t(qs[:, hs], ks[:, hs]), 0.0))
        for sums, pairs, _, half in levels:
            fade = jnp.exp(dot(sums, high) + dot(sums, rest))
            side = (jnp.where(upper_rows(half, qs.shape[1], span), qs32, ks32) * fade).astype(BF16)
            for h in range(HEADS):
                part = side[:, h * wide : (h + 1) * wide]
                scores[h] = scores[h] + jnp.where(pairs, dot_t(part, part), 0.0)
        for h in range(HEADS):
            low = scores[h].astype(BF16)
            a_ref[s * HEADS + h] = low
            vs = slice(h * tall, (h + 1) * tall)
            mix_ref[at, vs] = dot(low, v_ref[at, vs])
        return carry

    lax.fori_loop(0, seqs, one_sequence, 0)


def hidden_kernel(dims, idx_ref, mix_ref, qb_ref, e0, e1, e2, e3, og_ref, x_ref, wo_own, wo_oth,
                  own_ref, pack_ref, mixture_ref, gm_ref, go_ref, hid_ref, sm_ref, so_ref, st_ref,
                  gain, gated):
    seqs, span = dims
    load_state(idx_ref, (e0, e1, e2, e3), st_ref)
    half = sm_ref.shape[1]
    gain_half = gain.shape[1] // 2
    _, place_g2, _, place_hg = packed_places(half, qb_ref.shape[1] // 2, gain_half)
    gain[:, mine_at(idx_ref, gain_half)] = packed_row(own_ref, *place_hg)
    gain[:, theirs_at(idx_ref, gain_half)] = packed_row(pack_ref, *place_hg)
    wide = qb_ref.shape[1] // HEADS
    tall = mix_ref.shape[1] // HEADS
    factor = wide ** (-0.5)
    quarter = st_ref.shape[1]
    per = tall // quarter
    head_gain = gain[...]
    for s in range(seqs):
        at = slice(s * span, (s + 1) * span)
        for h in range(HEADS):
            hs = slice(h * wide, (h + 1) * wide)
            for q in range(per):
                vs = slice(h * tall + q * quarter, h * tall + (q + 1) * quarter)
                carried = dot_t(qb_ref[at, hs], st_ref[s * per + q, :, hs])
                mixture_ref[at, vs] = (mix_ref[at, vs] + carried) * factor
            vs = slice(h * tall, (h + 1) * tall)
            mixture = mixture_ref[at, vs]
            root = lax.rsqrt(jnp.mean(mixture * mixture, axis=1, keepdims=True) + 1e-5)
            opened = og_ref[at, vs]
            gated[at, vs] = (mixture * root * head_gain * (opened * sigmoid(opened))).astype(BF16)
    half = wo_own.shape[0]
    gm = gated[:, mine_at(idx_ref, half)]
    go = gated[:, theirs_at(idx_ref, half)]
    gm_ref[...] = gm
    go_ref[...] = go
    hid_ref[...] = x_ref[...].astype(F32) + dot(gm, wo_own[...]) + dot(go, wo_oth[...])
    half = sm_ref.shape[1]
    hm = hid_ref[:, mine_at(idx_ref, half)]
    ho = hid_ref[:, theirs_at(idx_ref, half)]
    square = jnp.sum(hm * hm, axis=1, keepdims=True) + jnp.sum(ho * ho, axis=1, keepdims=True)
    root = lax.rsqrt(square / (2 * half) + 1e-6)
    sm_ref[...] = (hm * root * packed_row(own_ref, *place_g2)).astype(BF16)
    so_ref[...] = (ho * root * packed_row(pack_ref, *place_g2)).astype(BF16)


def ffn_kernel(dims, idx_ref, sm_ref, so_ref, hid_ref, e_ref, wg_own, wg_oth, wu_own, wu_oth, wd_own, wd_oth,
               out_ref, am_ref, g_ref, dm_ref, do_ref, gates_in, ups_in, downs_in, acts, sems):
    seqs, span = dims
    half = wd_own.shape[0]
    spots = (mine_at(idx_ref, half), theirs_at(idx_ref, half))
    cut = half // 256 * 128 + 128
    steps = []
    for side in range(2):
        for first, last in ((0, cut), (cut, half)):
            to_at = pl.ds(first, last - first)
            from_at = pl.ds(pl.multiple_of(spots[side].start + first, 128), last - first)
            now = []
            for to, sources in ((gates_in, (wg_own, wg_oth)), (ups_in, (wu_own, wu_oth))):
                for which in range(2):
                    now.append((sources[which].at[:, from_at], to.at[which, side, :, to_at]))
            now.append(((wd_own, wd_oth)[side].at[to_at, :], downs_in.at[side, to_at, :]))
            copies = [
                pltpu.make_async_copy(src, dst, sems.at[len(steps), i])
                for i, (src, dst) in enumerate(now)
            ]
            for one in copies:
                one.start()
            steps.append(copies)
    out_ref[...] = hid_ref[...]
    dm_ref[...] = jnp.zeros_like(dm_ref)
    do_ref[...] = jnp.zeros_like(do_ref)

    def one_side(side, carry):
        sm, so, cots = sm_ref[...], so_ref[...], e_ref[...]
        at = lax.rem(idx_ref[0] + side, 2) * half
        for part, (first, last) in enumerate(((0, cut), (cut, half))):
            for now in range(2):

                @pl.when(side == now)
                def _():
                    for one in steps[2 * now + part]:
                        one.wait()

            size = last - first
            g_own, g_oth = gates_in[0, side, :, first:last], gates_in[1, side, :, first:last]
            u_own, u_oth = ups_in[0, side, :, first:last], ups_in[1, side, :, first:last]
            down = downs_in[side, first:last, :]
            gates = dot(sm, g_own) + dot(so, g_oth)
            ups = dot(sm, u_own) + dot(so, u_oth)
            sig = sigmoid(gates)
            opened = gates * sig
            act = (opened * ups).astype(BF16)
            acts[side, :, first:last] = act
            grads = dot_t(cots, down)
            gate_grad = (grads * ups * sig * (1.0 + gates * (1.0 - sig))).astype(BF16)
            up_grad = (grads * opened).astype(BF16)
            g_ref[:, pl.ds(pl.multiple_of(at + first, 128), size)] = gate_grad
            g_ref[:, pl.ds(pl.multiple_of(at + first + 2 * half, 128), size)] = up_grad
            out_ref[...] += dot(act, down)
            dm_ref[...] += dot_t(gate_grad, g_own) + dot_t(up_grad, u_own)
            do_ref[...] += dot_t(gate_grad, g_oth) + dot_t(up_grad, u_oth)
        return carry

    lax.fori_loop(0, 2, one_side, 0)
    am_ref[...] = acts[0]
    g_ref[:, 4 * half :] = acts[1]
    width = out_ref.shape[1]
    for s in range(seqs):
        at = slice(s * span, (s + 1) * span)
        places = lax.broadcasted_iota(jnp.int32, (span, width), 0) + idx_ref[1] * span
        out_ref[at, :] = jnp.where(places < idx_ref[2 + s], out_ref[at, :], 0.0)


def gate_back_kernel(dims, idx_ref, hid_ref, dm_ref, do_ref, e_ref, wo_own, wo_oth, mixture_ref,
                     og_ref, qb_ref, tot_ref, own_ref, pack_ref,
                     hg_ref, hl_ref, mg_ref, ol_ref, g2m_ref, g2o_ref, hgm_ref, hgo_ref, m0, m1, m2, m3,
                     gain, gated, gain_sum, state):
    seqs, span = dims
    half = dm_ref.shape[1]
    gain_half = gain.shape[1] // 2
    _, place_g2, _, place_hg = packed_places(half, qb_ref.shape[1] // 2, gain_half)
    mine, theirs = mine_at(idx_ref, half), theirs_at(idx_ref, half)
    hm, ho = hid_ref[:, mine], hid_ref[:, theirs]
    square = jnp.sum(hm * hm, axis=1, keepdims=True) + jnp.sum(ho * ho, axis=1, keepdims=True)
    root = lax.rsqrt(square / (2 * half) + 1e-6)
    dm, do = dm_ref[...], do_ref[...]
    g2m_ref[...] = jnp.sum(dm * hm * root, axis=0, keepdims=True)
    g2o_ref[...] = jnp.sum(do * ho * root, axis=0, keepdims=True)
    dm = dm * packed_row(own_ref, *place_g2)
    do = do * packed_row(pack_ref, *place_g2)
    along = jnp.sum(dm * hm, axis=1, keepdims=True) + jnp.sum(do * ho, axis=1, keepdims=True)
    along = along * (root * root * root) / (2 * half)
    hg_ref[:, mine] = e_ref[:, mine].astype(F32) + dm * root - hm * along
    hg_ref[:, theirs] = e_ref[:, theirs].astype(F32) + do * root - ho * along
    low = hg_ref[...].astype(BF16)
    hl_ref[...] = low
    half = wo_own.shape[0]
    gated[:, mine_at(idx_ref, half)] = dot_t(low, wo_own[...])
    gated[:, theirs_at(idx_ref, half)] = dot_t(low, wo_oth[...])
    gain[:, mine_at(idx_ref, gain_half)] = packed_row(own_ref, *place_hg)
    gain[:, theirs_at(idx_ref, gain_half)] = packed_row(pack_ref, *place_hg)
    head_gain = gain[...]
    wide = qb_ref.shape[1] // HEADS
    tall = mixture_ref.shape[1] // HEADS
    factor = wide ** (-0.5)
    quarter = state.shape[1]
    per = tall // quarter
    gain_grad = jnp.zeros((1, tall), F32)
    for s in range(seqs):
        at = slice(s * span, (s + 1) * span)
        for h in range(HEADS):
            vs = slice(h * tall, (h + 1) * tall)
            hs = slice(h * wide, (h + 1) * wide)
            mixture, opened, grad = mixture_ref[at, vs], og_ref[at, vs], gated[at, vs]
            root = lax.rsqrt(jnp.mean(mixture * mixture, axis=1, keepdims=True) + 1e-5)
            sig = sigmoid(opened)
            flat = mixture * root
            ol_ref[at, vs] = (grad * flat * head_gain * sig * (1.0 + opened * (1.0 - sig))).astype(BF16)
            grad = grad * (opened * sig)
            gain_grad += jnp.sum(grad * flat, axis=0, keepdims=True)
            grad = grad * head_gain
            along = jnp.mean(grad * flat, axis=1, keepdims=True)
            mixed = (grad - flat * along) * (root * factor)
            mg_ref[at, vs] = mixed
            part = t_dot(mixed.astype(BF16), qb_ref[at, hs])
            for q in range(per):
                state[s * per + q, :, hs] = part[q * quarter : (q + 1) * quarter]
    gain_sum[...] = gain_grad
    hgm_ref[...] = gain_sum[:, mine_at(idx_ref, gain_half)]
    hgo_ref[...] = gain_sum[:, theirs_at(idx_ref, gain_half)]
    totals = [tot_ref[pl.ds(s, 1), :] for s in range(seqs)]
    write_quarters(idx_ref, state, totals, (m0, m1, m2, m3), seqs)


def inner_back_kernel(dims, idx_ref, q_ref, k_ref, v_ref, lg_ref, a_ref, mg_ref, qb_ref, st_ref,
                      dq_ref, dk_ref, dv_ref, dc_ref):
    seqs, span = dims
    row, col = pair_iota(span)
    upto = (col <= row).astype(F32).astype(BF16)
    diagonal = row == col
    levels = level_masks(span)
    wide = q_ref.shape[1] // HEADS
    tall = v_ref.shape[1] // HEADS
    quarter = st_ref.shape[1]
    per = tall // quarter
    def one_sequence(s, carry):
        at = pl.ds(pl.multiple_of(s * span, span), span)
        logits = lg_ref[at, :]
        decays = (jnp.minimum(logits, 0.0) - jnp.log1p(jnp.exp(-jnp.abs(logits)))) / 16.0
        high, rest = two_part(decays)
        qs32, ks32 = q_ref[at, :].astype(F32), k_ref[at, :].astype(F32)
        begun = jnp.exp(dot(upto, high) + dot(upto, rest))
        pair_grads = []
        for h in range(HEADS):
            hs = slice(h * wide, (h + 1) * wide)
            vs = slice(h * tall, (h + 1) * tall)
            mixed, more = two_part(mg_ref[at, vs])
            values = v_ref[at, vs]
            full = dot_t(mixed, values) + dot_t(more, values)
            back = dot_t(values, mixed) + dot_t(values, more)
            pair_grads.append(jnp.where(row >= col, full, back))
            dv_ref[at, vs] = t_dot(a_ref[s * HEADS + h], mixed)
            own = jnp.sum(jnp.where(diagonal, full, 0.0), axis=1, keepdims=True)
            crossed = jnp.zeros((span, wide), F32)
            for q in range(per):
                part = slice(h * tall + q * quarter, h * tall + (q + 1) * quarter)
                crossed += dot(mg_ref[at, part].astype(BF16), st_ref[s * per + q, :, hs])
            dq_ref[at, hs] = own * ks32[:, hs] + begun[:, hs] * crossed
            dk_ref[at, hs] = own * qs32[:, hs]
            dc_ref[at, hs] = qb_ref[at, hs].astype(F32) * crossed
        for sums, _, both, half in levels:
            fade = jnp.exp(dot(sums, high) + dot(sums, rest))
            upper = upper_rows(half, qs32.shape[1], span)
            side = (jnp.where(upper, qs32, ks32) * fade).astype(BF16)
            for h in range(HEADS):
                hs = slice(h * wide, (h + 1) * wide)
                grads = dot(jnp.where(both, pair_grads[h], 0.0).astype(BF16), side[:, hs])
                moved = side[:, hs].astype(F32) * grads
                faded = fade[:, hs] * grads
                over = upper[:, hs]
                dc_ref[at, hs] += jnp.where(over, moved, -moved)
                dq_ref[at, hs] += jnp.where(over, faded, 0.0)
                dk_ref[at, hs] += jnp.where(over, 0.0, faded)
        return carry

    lax.fori_loop(0, seqs, one_sequence, 0)


def inputs_back_kernel(dims, idx_ref, dq_ref, dk_ref, dv_ref, dc_ref, ol_ref, kd_ref, v_ref, lg_ref, tot_ref, st_ref,
                       l0, l1, l2, l3, x_ref, hg_ref, wq_own, wq_oth, wk_own, wk_oth, wv_own, wv_oth,
                       wg_own, wg_oth, own_ref, pack_ref, g2o_ref, hgo_ref,
                       tg_ref, ga_ref, llm_ref, g1m_ref, bm_ref, small_ref,
                       leaving, logit, bias):
    seqs, span = dims
    half = wq_own.shape[0]
    part = wq_own.shape[1] // 2
    place_g1, _, _, _ = packed_places(half, part, 0)
    li_own, lo_own = packed_factors(own_ref, half)
    li_oth, lo_oth = packed_factors(pack_ref, half)
    load_state(idx_ref, (l0, l1, l2, l3), leaving)
    row, col = pair_iota(span)
    later = (col > row).astype(F32).astype(BF16)
    since = (col >= row).astype(F32).astype(BF16)
    before = (col < row).astype(F32).astype(BF16)
    keys = kd_ref.shape[1]
    vals = v_ref.shape[1]
    wide, tall = keys // HEADS, vals // HEADS
    quarter = st_ref.shape[1]
    per = tall // quarter
    bias_sum = jnp.zeros((1, keys), F32)
    for s in range(seqs):
        at = slice(s * span, (s + 1) * span)
        logits = lg_ref[at, :]
        decays = (jnp.minimum(logits, 0.0) - jnp.log1p(jnp.exp(-jnp.abs(logits)))) / 16.0
        ahead = jnp.exp(mask_dot(later, decays))
        for h in range(HEADS):
            hs = slice(h * wide, (h + 1) * wide)
            faded = kd_ref[at, hs]
            grads = jnp.zeros((span, wide), F32)
            ends = jnp.zeros((1, wide), F32)
            for q in range(per):
                vs = slice(h * tall + q * quarter, h * tall + (q + 1) * quarter)
                at_v = slice(keys * 2 + vs.start, keys * 2 + vs.stop)
                part = leaving[s * per + q, :, hs]
                ga_ref[at, at_v] = (dv_ref[at, vs] + dot_t(faded, part)).astype(BF16)
                grads += dot(v_ref[at, vs], part)
                ends += jnp.sum(
                    st_ref[s * per + q, :, hs].astype(F32) * part.astype(F32), axis=0, keepdims=True
                )
            moved = faded.astype(F32) * grads
            ga_ref[at, keys + h * wide : keys + (h + 1) * wide] = (
                dk_ref[at, hs] + ahead[:, hs] * grads
            ).astype(BF16)
            decay_grad = (
                mask_dot(since, dc_ref[at, hs])
                + mask_dot(before, moved)
                + tot_ref[pl.ds(s, 1), hs] * ends
            )
            logit_grad = decay_grad * sigmoid(-logits[:, hs]) / 16.0
            bias[:, hs] = jnp.sum(logit_grad, axis=0, keepdims=True)
            logit[at, hs] = logit_grad.astype(BF16)
        bias_sum += bias[...]
    bias[...] = bias_sum
    part = keys // 2
    bm_ref[...] = bias[:, mine_at(idx_ref, part)]
    small_ref[:, 2 * half : 2 * half + part] = bias[:, theirs_at(idx_ref, part)]
    small_ref[:, half : 2 * half] = g2o_ref[...]
    small_ref[:, 2 * half + part :] = hgo_ref[...]
    ga_ref[:, 0:keys] = dq_ref[...].astype(BF16)
    ga_ref[:, 2 * keys + vals : 2 * keys + 2 * vals] = ol_ref[...]
    llm, llo = logit[:, mine_at(idx_ref, part)], logit[:, theirs_at(idx_ref, part)]
    llm_ref[...] = llm
    lrg = (dot_t(llm, lo_own) + dot_t(llo, lo_oth)).astype(BF16)
    rest = jnp.zeros((lrg.shape[0], 128 - RANK), BF16)
    lanes = 2 * keys + 2 * vals + 128
    ga_ref[:, lanes - 128 : lanes] = jnp.concatenate([lrg, rest], axis=1)
    ga_ref[:, lanes:] = llo
    qg, kg = ga_ref[:, 0:keys], ga_ref[:, keys : 2 * keys]
    vg = ga_ref[:, 2 * keys : 2 * keys + vals]
    og = ga_ref[:, 2 * keys + vals : 2 * keys + 2 * vals]
    dm = dot_t(qg, wq_own[...]) + dot_t(kg, wk_own[...]) + dot_t(vg, wv_own[...])
    dm = dm + dot_t(og, wg_own[...]) + dot(lrg, li_own)
    do = dot_t(qg, wq_oth[...]) + dot_t(kg, wk_oth[...]) + dot_t(vg, wv_oth[...])
    do = do + dot_t(og, wg_oth[...]) + dot(lrg, li_oth)
    mine, theirs = mine_at(idx_ref, half), theirs_at(idx_ref, half)
    xm, xo = x_ref[:, mine].astype(F32), x_ref[:, theirs].astype(F32)
    square = jnp.sum(xm * xm, axis=1, keepdims=True) + jnp.sum(xo * xo, axis=1, keepdims=True)
    root = lax.rsqrt(square / (2 * half) + 1e-6)
    g1m_ref[...] = jnp.sum(dm * xm * root, axis=0, keepdims=True)
    small_ref[:, 0:half] = jnp.sum(do * xo * root, axis=0, keepdims=True)
    dm = dm * packed_row(own_ref, *place_g1)
    do = do * packed_row(pack_ref, *place_g1)
    along = jnp.sum(dm * xm, axis=1, keepdims=True) + jnp.sum(do * xo, axis=1, keepdims=True)
    along = along * (root * root * root) / (2 * half)
    tg_ref[:, mine] = hg_ref[:, mine] + dm * root - xm * along
    tg_ref[:, theirs] = hg_ref[:, theirs] + do * root - xo * along


def block_of(position, order):
    block = 0
    for at, bit in enumerate(order):
        if (position >> (3 - at)) & 1:
            block |= bit
    return block


def deal(position, keep_ref, send_ref):
    return keep_ref.at[position] if position < 8 else send_ref.at[position - 8]


def wide_grad_kernel(orders, idx_ref, sm_ref, so_ref, gm_ref, go_ref, k0, s0, k1, s1, full):
    place = lax.rem(idx_ref[1], 16)
    width = full.shape[1]
    high = full.shape[0] // 16
    for which, refs in enumerate(((k0, s0), (k1, s1))):
        cols = slice(which * width, (which + 1) * width)
        full[...] = t_dot(sm_ref[...], gm_ref[:, cols]) + t_dot(so_ref[...], go_ref[:, cols])
        for position in range(16):
            block = block_of(position, orders[which]) ^ place
            rows = full[pl.ds(pl.multiple_of(block * high, high), high), :].astype(BF16)
            to = deal(position, *refs)
            for tile in range(width // 128):
                to[tile * high : (tile + 1) * high, :] = rows[:, tile * 128 : (tile + 1) * 128]


def down_grad_kernel(order, idx_ref, am_ref, go_ref, em_ref, eo_ref, keep_ref, send_ref, full):
    place = lax.rem(idx_ref[1], 16)
    first = go_ref.shape[1] - am_ref.shape[1]
    full[...] = t_dot(am_ref[...], em_ref[...]) + t_dot(go_ref[:, first:], eo_ref[...])
    high = full.shape[0] // 2
    for position in range(16):
        block = block_of(position, order) ^ place
        rows = pl.ds(pl.multiple_of(lax.div(block, 8) * high, 16), high)
        cols = pl.ds(pl.multiple_of(lax.rem(block, 8) * 128, 128), 128)
        deal(position, keep_ref, send_ref)[...] = full[rows, cols].astype(BF16)


def attention_grad_kernel(orders, cuts, idx_ref, nm_ref, no_ref, gm_ref, go_ref, am_ref, ao_ref, hm_ref, ho_ref,
                          lrm_ref, lro_ref, llm_ref, g1_ref, g2_ref, b_ref, hg_ref, small_ref, k0, s0, k1, s1, k2, s2, full, outer, small):
    place = lax.rem(idx_ref[1], 16)
    lanes = full.shape[1]
    full[...] = t_dot(nm_ref[...], gm_ref[:, 0:lanes]) + t_dot(no_ref[...], go_ref[:, 0:lanes])
    outer[...] = t_dot(am_ref[...], hm_ref[...]) + t_dot(ao_ref[...], ho_ref[...])
    low_out = t_dot(lrm_ref[...], llm_ref[...]) + t_dot(lro_ref[...], go_ref[:, lanes:])
    small[...] = jnp.zeros_like(small)
    small[0] = low_out[:, 0:128]
    small[1] = low_out[:, 128:256]
    line = 0
    for ref in (g1_ref, g2_ref, b_ref, hg_ref):
        row = ref[...] + small_ref[:, line * 128 : line * 128 + ref.shape[1]]
        for tile in range(row.shape[1] // 128):
            small[2, line : line + 1, :] = row[:, tile * 128 : (tile + 1) * 128]
            line += 1
    high = full.shape[0] // 16
    tiles = full.shape[1] // 128
    for which, refs in enumerate(((k0, s0), (k1, s1), (k2, s2))):
        first, last = cuts[which], cuts[which + 1]
        for position in range(16):
            block = block_of(position, orders[which]) ^ place
            at = pl.ds(pl.multiple_of(block * high, high), high)
            to = deal(position, *refs)
            for tile in range(first, last):
                if tile < tiles:
                    rows = full[at, tile * 128 : (tile + 1) * 128]
                else:
                    rows = outer[at, (tile - tiles) * 128 : (tile - tiles + 1) * 128]
                to[(tile - first) * high : (tile - first + 1) * high, :] = rows.astype(BF16)
            if which == 2:
                to[(last - first) * high :, :] = small[block].astype(BF16)


def wide_open_kernel(order, idx_ref, own_ref, got_ref, out_ref):
    place = lax.rem(idx_ref[1], 16)
    high = out_ref.shape[0] // 16
    for position in range(16):
        block = block_of(position, order) ^ place
        held = deal(position, own_ref, got_ref)
        at = pl.ds(pl.multiple_of(block * high, high), high)
        for tile in range(out_ref.shape[1] // 128):
            out_ref[at, tile * 128 : (tile + 1) * 128] = held[tile * high : (tile + 1) * high, :].astype(F32)


def down_open_kernel(order, idx_ref, own_ref, got_ref, out_ref):
    place = lax.rem(idx_ref[1], 16)
    high = out_ref.shape[0] // 2
    for position in range(16):
        block = block_of(position, order) ^ place
        rows = pl.ds(pl.multiple_of(lax.div(block, 8) * high, 16), high)
        cols = pl.ds(pl.multiple_of(lax.rem(block, 8) * 128, 128), 128)
        out_ref[rows, cols] = deal(position, own_ref, got_ref)[...].astype(F32)


def attention_open_kernel(orders, cuts, idx_ref, o0, r0, o1, r1, o2, r2, q_ref, k_ref, v_ref, og_ref, li_ref, w_ref,
                          lo_ref, g1_ref, g2_ref, b_ref, hg_ref, small, first_factor):
    place = lax.rem(idx_ref[1], 16)
    high = q_ref.shape[0] // 16
    homes = []
    for ref in (q_ref, k_ref, v_ref, og_ref):
        homes += [(ref, tile) for tile in range(ref.shape[1] // 128)]
    homes.append((first_factor, 0))
    homes += [(w_ref, tile) for tile in range(w_ref.shape[1] // 128)]
    for which, refs in enumerate(((o0, r0), (o1, r1), (o2, r2))):
        first, last = cuts[which], cuts[which + 1]
        for position in range(16):
            block = block_of(position, orders[which]) ^ place
            at = pl.ds(pl.multiple_of(block * high, high), high)
            held = deal(position, *refs)
            for tile in range(first, last):
                rows = held[(tile - first) * high : (tile - first + 1) * high, :].astype(F32)
                ref, column = homes[tile]
                ref[at, column * 128 : (column + 1) * 128] = rows
            if which == 2:
                small[block] = held[(last - first) * high :, :].astype(F32)
    li_ref[...] = first_factor[...].T[0 : li_ref.shape[0], :]
    lo_ref[:, 0:128] = small[0]
    lo_ref[:, 128:256] = small[1]
    line = 0
    for ref in (g1_ref, g2_ref, b_ref, hg_ref):
        for tile in range(ref.shape[1] // 128):
            ref[:, tile * 128 : (tile + 1) * 128] = small[2, line : line + 1, :]
            line += 1


def across(array):
    return lax.ppermute(array, "fsdp", ((0, 1), (1, 0)))


def swap(array, bit):
    count = lax.axis_size("seq")
    return lax.ppermute(array, "seq", tuple((one, one ^ bit) for one in range(count)))


def ahead(array, step):
    count = lax.axis_size("seq")
    return lax.ppermute(
        array,
        "seq",
        tuple((one, one + step) for one in range(count) if 0 <= one + step < count),
    )


def fence(*groups):
    return lax.optimization_barrier(groups)


class Portions:
    def __init__(self, parts, orders):
        self.kept = [keep for keep, _ in parts]
        self.sent = [send for _, send in parts]
        self.orders = orders

    def move(self, arrays, step):
        if step < 3:
            return [swap(a, order[step]) for a, order in zip(arrays, self.orders)]
        return self.move_all(arrays, self.orders[0][3])

    def move_all(self, arrays, bit):
        got = swap(jnp.concatenate(arrays, axis=1), bit)
        ends = [0]
        for a in arrays:
            ends.append(ends[-1] + a.shape[1])
        return [got[:, first:last] for first, last in zip(ends[:-1], ends[1:])]

    def reduce_start(self, step):
        return self.move(self.sent, step)

    def reduce_end(self, step, got):
        for one, more in enumerate(got):
            if step < 3:
                half = more.shape[0] // 2
                self.sent[one] = self.kept[one][half:] + more[half:]
                self.kept[one] = self.kept[one][:half] + more[:half]
            else:
                self.kept[one] = self.kept[one] + more
        bit = 16
        while step == 3 and bit < lax.axis_size("seq"):
            more = self.move_all(self.kept, bit)
            self.kept = [k + m for k, m in zip(self.kept, more)]
            bit *= 2

    def gather_start(self, step):
        return self.move(self.kept, step)

    def gather_end(self, step, got):
        if step:
            self.kept = [jnp.concatenate([k, more], axis=0) for k, more in zip(self.kept, got)]
        else:
            self.halves = list(zip(self.kept, got))


def scan_near(messages):
    return [messages[0]] + [swap(messages[o], o) for o in (1, 2, 3)]


def scan_scratch(messages):
    rows, lanes = messages[0].shape
    return [((4, rows - 16, lanes), F32), ((4, 1, lanes), F32)]


def scan_total(near, idx, reverse):
    return call("group_total", partial(group_total, reverse), idx, near, [(near[0].shape, BF16)], scan_scratch(near))[0]


def scan_far(total, reverse):
    sign = -4 if reverse else 4
    return [ahead(total, sign * step) for step in range(1, lax.axis_size("seq") // 4)]


def scan_entering(far, near, idx, reverse):
    rows, lanes = near[0].shape
    return call(
        "group_entering", partial(group_entering, reverse, len(far)), idx, list(far) + list(near),
        [((rows - 16, lanes), BF16)] * 4, scan_scratch(near) + [((4, rows - 16, lanes), F32)],
    )


def shards(
    tokens,
    lengths,
    first_gain,
    query_weight,
    key_weight,
    value_weight,
    outgate_weight,
    lowrank_in,
    lowrank_out,
    decay_bias,
    head_gain,
    output_weight,
    second_gain,
    gate_weight,
    up_weight,
    down_weight,
    cotangent,
):
    micro_count, pair_count, span, width = tokens.shape
    seqs = micro_count * pair_count
    rows = seqs * span
    dims = (seqs, span)
    core = lax.axis_index("fsdp")
    place = lax.axis_index("seq")
    own_lengths = lax.dynamic_slice_in_dim(lengths, core * pair_count, pair_count, 1).reshape(-1)
    idx = jnp.concatenate([jnp.stack([core, place]).astype(jnp.int32), own_lengths])
    keys, vals, ff = query_weight.shape[1], value_weight.shape[1], gate_weight.shape[1]
    half = query_weight.shape[0]
    tall = vals // HEADS
    quarter = seqs * tall // 4

    x = tokens.reshape(rows, width)
    cot = cotangent.reshape(rows, width)
    lrank = lowrank_in.shape[1]
    lines, at = 0, 0
    for a in (first_gain, second_gain, decay_bias, head_gain):
        lines = lines + jnp.pad(a, (at, 16 * 128 - at - a.size))
        at += a.size
    lines = lines.reshape(16, 128)
    pack = call(
        "pack", pack_kernel, idx, [lowrank_in.T, lowrank_out, lines],
        [((lrank * (half + lowrank_out.shape[1]) // 128 + 16, 128), BF16)],
    )[0]
    pack2, wk2, wv2 = (across(a) for a in (pack, key_weight, value_weight))

    message = ((quarter + 16, keys), BF16)
    state = ((4, quarter, keys), F32)
    nm, no, k, v, lr, lg, kd, tot, *messages = call(
        "keys", partial(keys_kernel, dims), idx,
        [x, key_weight, wk2, value_weight, wv2, pack, pack2],
        [((rows, half), BF16), ((rows, half), BF16), ((rows, keys), BF16), ((rows, vals), BF16),
         ((rows, lrank), BF16), ((rows, keys), F32), ((rows, keys), BF16), ((seqs, keys), F32)]
        + [message] * 4,
        [state],
    )
    messages, outgate_send, query_send = fence(messages, outgate_weight, query_weight)
    near = scan_near(messages)
    wg2, wq2 = across(outgate_send), across(query_send)
    q, og, mix, scores, qb, cots = call(
        "inner", partial(inner_kernel, dims), idx,
        [nm, no, query_weight, wq2, outgate_weight, wg2, k, v, lg, cot],
        [((rows, keys), BF16), ((rows, vals), F32), ((rows, vals), F32), ((seqs * HEADS, span, span), BF16),
         ((rows, keys), BF16), ((rows, width), BF16)],
    )
    near, mix, gate_send, up_send = fence(near, mix, gate_weight, up_weight)
    total = scan_total(near, idx, False)
    total, gate_send, up_send = fence(total, gate_send, up_send)
    far = scan_far(total, False)
    wgate2, wup2 = across(gate_send), across(up_send)
    far, wgate2, wup2 = fence(far, wgate2, wup2)
    pieces = scan_entering(far, near, idx, False)
    pieces, output_send, down_send = fence(pieces, output_weight, down_weight)
    pieces = [pieces[0]] + [swap(pieces[o], o) for o in (1, 2, 3)]
    wo2, wdown2 = across(output_send), across(down_send)
    mixture, gm, go, hid, sm, so, st = call(
        "hidden", partial(hidden_kernel, dims), idx,
        [mix, qb, *pieces, og, x, output_weight, wo2, pack, pack2],
        [((rows, vals), F32), ((rows, vals // 2), BF16), ((rows, vals // 2), BF16), ((rows, width), F32),
         ((rows, half), BF16), ((rows, half), BF16), ((4, quarter, keys), BF16)],
        [((1, tall), F32), ((rows, vals), BF16)],
    )
    so, no_send, lr_send, cots_send = fence(so, no, lr, cots)
    so2, no2, go2, lr2, cots2 = (across(a) for a in (so, no_send, go, lr_send, cots_send))
    out, am, gu, dm, do = call(
        "ffn", partial(ffn_kernel, dims), idx,
        [sm, so, hid, cots, gate_weight, wgate2, up_weight, wup2, down_weight, wdown2],
        [((rows, width), F32), ((rows, ff // 2), BF16), ((rows, 5 * ff // 2), BF16),
         ((rows, half), F32), ((rows, half), F32)],
        [((2, 2, half, ff // 2), BF16), ((2, 2, half, ff // 2), BF16), ((2, ff // 2, width), BF16),
         ((2, rows, ff // 2), BF16), pltpu.SemaphoreType.DMA((4, 5))], limit=42, far=6,
    )
    so2, no2, go2, lr2, cots2, gu, dm = fence(so2, no2, go2, lr2, cots2, gu, dm)

    orders = ((1, 2, 4, 8), (2, 4, 1, 8), (4, 1, 2, 8))
    hg, hl, mg, ol, g2m, g2o, hgm, hgo, *messages = call(
        "gate_back", partial(gate_back_kernel, dims), idx,
        [hid, dm, do, cots, output_weight, wo2, mixture, og, qb, tot, pack, pack2],
        [((rows, width), F32), ((rows, width), BF16), ((rows, vals), F32), ((rows, vals), BF16),
         ((1, half), F32), ((1, half), F32), ((1, tall // 2), F32), ((1, tall // 2), F32)] + [message] * 4,
        [((1, tall), F32), ((rows, vals), F32), ((1, tall), F32), state],
    )
    messages, gu_send, mg = fence(messages, gu, mg)
    near = scan_near(messages)
    gu2 = across(gu_send)
    dq, dk, dv, dc = call(
        "inner_back", partial(inner_back_kernel, dims), idx, [q, k, v, lg, scores, mg, qb, st],
        [((rows, keys), F32), ((rows, keys), F32), ((rows, vals), F32), ((rows, keys), F32)],
    )
    near, gu2, dq = fence(near, gu2, dq)
    total = scan_total(near, idx, True)
    total, gu2 = fence(total, gu2)
    far = scan_far(total, True)
    portion = ff // 128 * (half // 16)
    flat = [((8, portion, 128), BF16)] * 2
    wide_parts = call("wide_grad", partial(wide_grad_kernel, orders), idx, [sm, so2, gu, gu2], flat * 2,
                      [((half, ff), F32)], limit=32)
    am, wide_parts = fence(am, wide_parts)
    down_parts = call("down_grad", partial(down_grad_kernel, orders[2]), idx, [am, gu2, cots, cots2], flat,
                      [((ff // 2, width), F32)])
    far, down_parts = fence(far, down_parts)
    first = Portions([wide_parts[0:2], wide_parts[2:4], down_parts], orders)
    got = first.reduce_start(0)
    pieces = scan_entering(far, near, idx, True)
    pieces = [pieces[0]] + [swap(pieces[o], o) for o in (1, 2, 3)]
    got, pieces = fence(got, pieces)
    first.reduce_end(0, got)
    first.sent, pieces = fence(first.sent, pieces)
    got = first.reduce_start(1)
    lanes = 2 * keys + 2 * vals + 128
    tg, ga, llm, g1m, bm, small = call(
        "inputs_back", partial(inputs_back_kernel, dims), idx,
        [dq, dk, dv, dc, ol, kd, v, lg, tot, st, *pieces, x, hg, query_weight, wq2, key_weight, wk2,
         value_weight, wv2, outgate_weight, wg2, pack, pack2, g2o, hgo],
        [((rows, width), F32), ((rows, lanes + keys // 2), BF16), ((rows, keys // 2), BF16),
         ((1, half), F32), ((1, keys // 2), F32), ((1, 2 * half + keys // 2 + tall // 2), F32)],
        [((4, quarter, keys), BF16), ((rows, keys), BF16), ((1, keys), F32)], limit=32,
    )
    got, ga, small = fence(got, ga, small)
    first.reduce_end(1, got)
    got = first.reduce_start(2)
    ga2, small2, hl2 = across(ga), across(small), across(hl)
    tiles = lanes // 128 + width // 128
    cuts = (0, tiles // 3, 2 * tiles // 3, tiles)
    high = half // 16
    shapes = []
    for which in range(3):
        size = (cuts[which + 1] - cuts[which]) * high + (16 if which == 2 else 0)
        shapes += [((8, size, 128), BF16)] * 2
    parts = call(
        "attention_grad", partial(attention_grad_kernel, orders, cuts), idx,
        [nm, no2, ga, ga2, gm, go2, hl, hl2, lr, lr2, llm, g1m, g2m, bm, hgm, small2],
        shapes, [((half, lanes), F32), ((vals // 2, width), F32), ((16, 16, 128), F32)], limit=32,
    )
    got, parts = fence(got, parts)
    first.reduce_end(2, got)
    second = Portions([parts[0:2], parts[2:4], parts[4:6]], orders)
    got, more = fence(first.reduce_start(3), second.reduce_start(0))
    first.reduce_end(3, got)
    second.reduce_end(0, more)
    got, more = fence(first.gather_start(3), second.reduce_start(1))
    first.gather_end(3, got)
    second.reduce_end(1, more)
    both = [jnp.concatenate([k, a], axis=1) for k, a in zip(first.kept, second.sent)]
    both = fence(*[swap(a, order[2]) for a, order in zip(both, orders)])
    got = [a[:, : k.shape[1]] for a, k in zip(both, first.kept)]
    more = [a[:, k.shape[1] :] for a, k in zip(both, first.kept)]
    first.gather_end(2, got)
    second.reduce_end(2, more)
    got, more = fence(first.gather_start(1), second.reduce_start(3))
    first.gather_end(1, got)
    second.reduce_end(3, more)
    got, more = fence(first.gather_start(0), second.gather_start(3))
    first.gather_end(0, got)
    second.gather_end(3, more)
    gate_halves, up_halves, down_halves = first.halves
    more = second.gather_start(2)
    gate_out = call("gate_open", partial(wide_open_kernel, orders[0]), idx, gate_halves, [((half, ff), F32)])[0]
    more, gate_out = fence(more, gate_out)
    second.gather_end(2, more)
    more = second.gather_start(1)
    up_out = call("up_open", partial(wide_open_kernel, orders[1]), idx, up_halves, [((half, ff), F32)])[0]
    more, up_out = fence(more, up_out)
    second.gather_end(1, more)
    more = second.gather_start(0)
    down_out = call("down_open", partial(down_open_kernel, orders[2]), idx, down_halves, [((ff // 2, width), F32)])[0]
    more, down_out = fence(more, down_out)
    second.gather_end(0, more)
    opened = call(
        "attention_open", partial(attention_open_kernel, orders, cuts), idx, [a for pair in second.halves for a in pair],
        [((half, keys), F32), ((half, keys), F32), ((half, vals), F32), ((half, vals), F32),
         ((lrank, half), F32), ((vals // 2, width), F32), ((lrank, keys // 2), F32),
         ((1, half), F32), ((1, half), F32), ((1, keys // 2), F32), ((1, tall // 2), F32)],
        [((16, 16, 128), F32), ((half, 128), F32)],
    )
    q_out, k_out, v_out, og_out, li_out, w_out, lo_out, g1_out, g2_out, b_out, hg_out = opened
    return (
        out.reshape(tokens.shape),
        tg.reshape(tokens.shape),
        g1_out.reshape(-1),
        q_out,
        k_out,
        v_out,
        og_out,
        li_out.T,
        lo_out,
        b_out.reshape(-1),
        hg_out.reshape(-1),
        w_out,
        g2_out.reshape(-1),
        gate_out,
        up_out,
        down_out,
    )


def solution(mesh):
    shard, column = P("fsdp", None), P(None, "fsdp")
    stream, line = P(None, "fsdp", "seq", None), P("fsdp")
    weights = (line, shard, shard, shard, shard, shard, column, line, line, shard, line, shard, shard, shard)
    return jax.shard_map(
        shards,
        mesh=mesh,
        in_specs=(stream, P()) + weights + (stream,),
        out_specs=(stream, stream) + weights,
        check_vma=False,
    )
```

```python
from functools import partial

import jax
import jax.numpy as jnp
from jax import lax
from jax.experimental import pallas as pl
from jax.experimental.pallas import tpu as pltpu
from jax.sharding import PartitionSpec as P

HEADS = 4
RANK = 16
F32 = jnp.float32
BF16 = jnp.bfloat16
MIB = 1024 * 1024


def dot(first_op, second_op):
    return jnp.dot(first_op, second_op, preferred_element_type=F32)


def dot_t(first_op, second_op):
    return lax.dot_general(
        first_op, second_op, (((1,), (1,)), ((), ())), preferred_element_type=F32
    )


def t_dot(first_op, second_op):
    return lax.dot_general(
        first_op, second_op, (((0,), (0,)), ((), ())), preferred_element_type=F32
    )


def two_part(value):
    high = value.astype(BF16)
    return high, (value - high.astype(F32)).astype(BF16)


def mask_dot(mask, value):
    high, rest = two_part(value)
    return dot(mask, high) + dot(mask, rest)


def sigmoid(value):
    return 1.0 / (1.0 + jnp.exp(-value))


def pair_iota(size):
    return (
        lax.broadcasted_iota(jnp.int32, (size, size), 0),
        lax.broadcasted_iota(jnp.int32, (size, size), 1),
    )


def level_masks(size):
    row, col = pair_iota(size)
    out = []
    half = size // 2
    while half >= 1:
        block = 2 * half
        row_block = row // block
        middle = row_block * block + half - 1
        upper = row > middle
        sums = (upper & (col > middle) & (col <= row)) | (
            jnp.logical_not(upper) & (col > row) & (col <= middle)
        )
        same = row_block == col // block
        pairs = same & upper & (col <= middle)
        both = same & (upper != (col > middle))
        out.append((sums.astype(F32).astype(BF16), pairs, both, half))
        half //= 2
    return out


def upper_rows(half, width, size):
    row = lax.broadcasted_iota(jnp.int32, (size, width), 0)
    return row % (2 * half) >= half


def seat(idx_ref):
    return idx_ref[0], idx_ref[1]


def mine_at(idx_ref, width):
    return pl.ds(pl.multiple_of(idx_ref[0] * width, 128), width)


def theirs_at(idx_ref, width):
    return pl.ds(pl.multiple_of((1 - idx_ref[0]) * width, 128), width)


SMEM = pl.BlockSpec(memory_space=pltpu.SMEM)
VMEM = pl.BlockSpec(memory_space=pltpu.VMEM)


def call(name, body, idx, inputs, outs, scratch=(), limit=22, far=0):
    shapes = [jax.ShapeDtypeStruct(s, d) for s, d in outs]
    result = pl.pallas_call(
        body,
        name=name,
        out_shape=shapes,
        in_specs=[SMEM] + [VMEM] * (len(inputs) - far) + [pl.BlockSpec(memory_space=pl.ANY)] * far,
        out_specs=[VMEM] * len(shapes),
        scratch_shapes=[pltpu.VMEM(*s) if isinstance(s, tuple) else s for s in scratch],
        compiler_params=pltpu.CompilerParams(vmem_limit_bytes=limit * MIB),
        cost_estimate=pl.CostEstimate(flops=1, bytes_accessed=1, transcendentals=0),
    )(idx, *inputs)
    return result


def put_message(ref, rows, total):
    count = rows.shape[0]
    ref[pl.ds(0, count), :] = rows.astype(BF16)
    high = total.astype(BF16)
    rest = total - high.astype(F32)
    middle = rest.astype(BF16)
    low = (rest - middle.astype(F32)).astype(BF16)
    tail = jnp.concatenate(
        [high, middle, low, jnp.zeros((13,) + total.shape[1:], BF16)], axis=0
    )
    ref[pl.ds(count, 16), :] = tail


def get_message(ref):
    count = ref.shape[0] - 16
    tail = ref[pl.ds(count, 16), :].astype(F32)
    return ref[pl.ds(0, count), :].astype(F32), tail[0:1] + tail[1:2] + tail[2:3]


def write_quarters(idx_ref, state, totals, messages, seq_count):
    low = lax.rem(idx_ref[1], 4)
    for other in range(4):
        quarter = low ^ other
        total = totals[0]
        for one in range(1, seq_count):
            total = jnp.where(quarter * seq_count // 4 >= one, totals[one], total)
        put_message(messages[other], state[quarter], total)


def group_total(reverse, idx_ref, *refs):
    out_ref, kept, held = refs[4], refs[5], refs[6]
    low = lax.rem(idx_ref[1], 4)
    for other in range(4):
        rows, total = get_message(refs[other])
        kept[low ^ other] = rows
        held[low ^ other] = total
    order = (3, 2, 1, 0) if reverse else (0, 1, 2, 3)
    rows, total = kept[order[0]], held[order[0]]
    for one in order[1:]:
        rows = held[one] * rows + kept[one]
        total = total * held[one]
    put_message(out_ref, rows, total)


def group_entering(reverse, far_count, idx_ref, *refs):
    far, near = refs[:far_count], refs[far_count : far_count + 4]
    outs = refs[far_count + 4 : far_count + 8]
    kept, held, entering = refs[far_count + 8 :]
    low = lax.rem(idx_ref[1], 4)
    for other in range(4):
        rows, total = get_message(near[other])
        kept[low ^ other] = rows
        held[low ^ other] = total
    rows = jnp.zeros(kept.shape[1:], F32)
    for one in far[::-1]:
        part, total = get_message(one)
        rows = total * rows + part
    for one in (3, 2, 1, 0) if reverse else (0, 1, 2, 3):
        entering[one] = rows
        rows = held[one] * rows + kept[one]
    for other in range(4):
        outs[other][...] = entering[low ^ other].astype(BF16)


def load_state(idx_ref, pieces, state):
    low = lax.rem(idx_ref[1], 4)
    for other in range(4):
        state[low ^ other] = pieces[other][...]


def pack_kernel(idx_ref, li_ref, lo_ref, lines_ref, out_ref):
    at = 0
    for ref in (li_ref, lo_ref):
        rank = ref.shape[0]
        for tile in range(ref.shape[1] // 128):
            out_ref[at : at + rank, :] = ref[:, tile * 128 : (tile + 1) * 128]
            at += rank
    out_ref[at:, :] = lines_ref[...]


def packed_factors(pack_ref, half):
    rank = RANK
    high = pack_ref.shape[0] - 16
    tiles = [pack_ref[at : at + rank, :] for at in range(0, high, rank)]
    first = half // 128
    return jnp.concatenate(tiles[:first], axis=1), jnp.concatenate(tiles[first:], axis=1)


def packed_row(pack_ref, first, count):
    lines = pack_ref[pack_ref.shape[0] - 16 :, :].astype(F32)
    return jnp.concatenate([lines[t : t + 1, :] for t in range(first, first + count)], axis=1)


def packed_places(half, part, gain):
    g1, b, hg = half // 128, part // 128, gain // 128
    return (0, g1), (g1, g1), (2 * g1, b), (2 * g1 + b, hg)


def keys_kernel(dims, idx_ref, x_ref, wk_own, wk_oth, wv_own, wv_oth, own_ref, pack_ref,
                nm_ref, no_ref, k_ref, v_ref, lr_ref, lg_ref, kd_ref, tot_ref,
                m0, m1, m2, m3, state):
    seqs, span = dims
    half = wk_own.shape[0]
    part = wk_own.shape[1] // 2
    place_g1, _, place_b, _ = packed_places(half, part, 0)
    li_own, lo_own = packed_factors(own_ref, half)
    li_oth, lo_oth = packed_factors(pack_ref, half)
    g1_own, b_own = packed_row(own_ref, *place_g1), packed_row(own_ref, *place_b)
    g1_oth, b_oth = packed_row(pack_ref, *place_g1), packed_row(pack_ref, *place_b)
    xm = x_ref[:, mine_at(idx_ref, half)].astype(F32)
    xo = x_ref[:, theirs_at(idx_ref, half)].astype(F32)
    square = jnp.sum(xm * xm, axis=1, keepdims=True) + jnp.sum(xo * xo, axis=1, keepdims=True)
    root = lax.rsqrt(square / (2 * half) + 1e-6)
    nm = (xm * root * g1_own).astype(BF16)
    no = (xo * root * g1_oth).astype(BF16)
    nm_ref[...] = nm
    no_ref[...] = no
    lr = (dot_t(nm, li_own) + dot_t(no, li_oth)).astype(BF16)
    lr_ref[...] = lr
    lg_ref[:, mine_at(idx_ref, part)] = dot(lr, lo_own) + b_own
    lg_ref[:, theirs_at(idx_ref, part)] = dot(lr, lo_oth) + b_oth
    keys = (dot(nm, wk_own[...]) + dot(no, wk_oth[...])).astype(BF16)
    k_ref[...] = keys
    values = (dot(nm, wv_own[...]) + dot(no, wv_oth[...])).astype(BF16)
    v_ref[...] = values
    row, col = pair_iota(span)
    later = (col > row).astype(F32).astype(BF16)
    wide = keys.shape[1] // HEADS
    tall = values.shape[1] // HEADS
    quarter = state.shape[1]
    totals = []
    for s in range(seqs):
        at = slice(s * span, (s + 1) * span)
        logits = lg_ref[at, :]
        decays = (jnp.minimum(logits, 0.0) - jnp.log1p(jnp.exp(-jnp.abs(logits)))) / 16.0
        ahead = mask_dot(later, decays)
        totals.append(jnp.exp(jnp.sum(decays, axis=0, keepdims=True)))
        tot_ref[pl.ds(s, 1), :] = totals[s]
        faded = (keys[at].astype(F32) * jnp.exp(ahead)).astype(BF16)
        kd_ref[at, :] = faded
        for h in range(HEADS):
            part = t_dot(values[at, h * tall : (h + 1) * tall], faded[:, h * wide : (h + 1) * wide])
            per = tall // quarter
            for q in range(per):
                state[s * per + q, :, h * wide : (h + 1) * wide] = part[q * quarter : (q + 1) * quarter]
    write_quarters(idx_ref, state, totals, (m0, m1, m2, m3), seqs)


def inner_kernel(dims, idx_ref, nm_ref, no_ref, wq_own, wq_oth, wg_own, wg_oth, k_ref, v_ref, lg_ref, cot_ref,
                 q_ref, og_ref, mix_ref, a_ref, qb_ref, e_ref):
    seqs, span = dims
    for s in range(seqs):
        at = slice(s * span, (s + 1) * span)
        places = lax.broadcasted_iota(jnp.int32, (span, cot_ref.shape[1]), 0) + idx_ref[1] * span
        e_ref[at, :] = jnp.where(places < idx_ref[2 + s], cot_ref[at, :].astype(F32), 0.0).astype(BF16)
    nm, no = nm_ref[...], no_ref[...]
    queries = (dot(nm, wq_own[...]) + dot(no, wq_oth[...])).astype(BF16)
    q_ref[...] = queries
    og_ref[...] = dot(nm, wg_own[...]) + dot(no, wg_oth[...])
    row, col = pair_iota(span)
    upto = (col <= row).astype(F32).astype(BF16)
    diagonal = row == col
    levels = level_masks(span)
    wide = queries.shape[1] // HEADS
    tall = v_ref.shape[1] // HEADS
    def one_sequence(s, carry):
        at = pl.ds(pl.multiple_of(s * span, span), span)
        logits = lg_ref[at, :]
        decays = (jnp.minimum(logits, 0.0) - jnp.log1p(jnp.exp(-jnp.abs(logits)))) / 16.0
        high, rest = two_part(decays)
        qs, ks = q_ref[at, :], k_ref[at, :]
        qs32, ks32 = qs.astype(F32), ks.astype(F32)
        qb_ref[at, :] = (qs32 * jnp.exp(dot(upto, high) + dot(upto, rest))).astype(BF16)
        scores = []
        for h in range(HEADS):
            hs = slice(h * wide, (h + 1) * wide)
            scores.append(jnp.where(diagonal, dot_t(qs[:, hs], ks[:, hs]), 0.0))
        for sums, pairs, _, half in levels:
            fade = jnp.exp(dot(sums, high) + dot(sums, rest))
            side = (jnp.where(upper_rows(half, qs.shape[1], span), qs32, ks32) * fade).astype(BF16)
            for h in range(HEADS):
                part = side[:, h * wide : (h + 1) * wide]
                scores[h] = scores[h] + jnp.where(pairs, dot_t(part, part), 0.0)
        for h in range(HEADS):
            low = scores[h].astype(BF16)
            a_ref[s * HEADS + h] = low
            vs = slice(h * tall, (h + 1) * tall)
            mix_ref[at, vs] = dot(low, v_ref[at, vs])
        return carry

    lax.fori_loop(0, seqs, one_sequence, 0)


def hidden_kernel(dims, idx_ref, mix_ref, qb_ref, e0, e1, e2, e3, og_ref, x_ref, wo_own, wo_oth,
                  own_ref, pack_ref, mixture_ref, gm_ref, go_ref, hid_ref, sm_ref, so_ref, st_ref,
                  gain, gated):
    seqs, span = dims
    load_state(idx_ref, (e0, e1, e2, e3), st_ref)
    half = sm_ref.shape[1]
    gain_half = gain.shape[1] // 2
    _, place_g2, _, place_hg = packed_places(half, qb_ref.shape[1] // 2, gain_half)
    gain[:, mine_at(idx_ref, gain_half)] = packed_row(own_ref, *place_hg)
    gain[:, theirs_at(idx_ref, gain_half)] = packed_row(pack_ref, *place_hg)
    wide = qb_ref.shape[1] // HEADS
    tall = mix_ref.shape[1] // HEADS
    factor = wide ** (-0.5)
    quarter = st_ref.shape[1]
    per = tall // quarter
    head_gain = gain[...]
    for s in range(seqs):
        at = slice(s * span, (s + 1) * span)
        for h in range(HEADS):
            hs = slice(h * wide, (h + 1) * wide)
            for q in range(per):
                vs = slice(h * tall + q * quarter, h * tall + (q + 1) * quarter)
                carried = dot_t(qb_ref[at, hs], st_ref[s * per + q, :, hs])
                mixture_ref[at, vs] = (mix_ref[at, vs] + carried) * factor
            vs = slice(h * tall, (h + 1) * tall)
            mixture = mixture_ref[at, vs]
            root = lax.rsqrt(jnp.mean(mixture * mixture, axis=1, keepdims=True) + 1e-5)
            opened = og_ref[at, vs]
            gated[at, vs] = (mixture * root * head_gain * (opened * sigmoid(opened))).astype(BF16)
    half = wo_own.shape[0]
    gm = gated[:, mine_at(idx_ref, half)]
    go = gated[:, theirs_at(idx_ref, half)]
    gm_ref[...] = gm
    go_ref[...] = go
    hid_ref[...] = x_ref[...].astype(F32) + dot(gm, wo_own[...]) + dot(go, wo_oth[...])
    half = sm_ref.shape[1]
    hm = hid_ref[:, mine_at(idx_ref, half)]
    ho = hid_ref[:, theirs_at(idx_ref, half)]
    square = jnp.sum(hm * hm, axis=1, keepdims=True) + jnp.sum(ho * ho, axis=1, keepdims=True)
    root = lax.rsqrt(square / (2 * half) + 1e-6)
    sm_ref[...] = (hm * root * packed_row(own_ref, *place_g2)).astype(BF16)
    so_ref[...] = (ho * root * packed_row(pack_ref, *place_g2)).astype(BF16)


def ffn_kernel(dims, idx_ref, sm_ref, so_ref, hid_ref, e_ref, wg_own, wg_oth, wu_own, wu_oth, wd_own, wd_oth,
               out_ref, am_ref, g_ref, dm_ref, do_ref, gates_in, ups_in, downs_in, acts, sems):
    seqs, span = dims
    half = wd_own.shape[0]
    spots = (mine_at(idx_ref, half), theirs_at(idx_ref, half))
    cut = half // 256 * 128 + 128
    steps = []
    for side in range(2):
        for first, last in ((0, cut), (cut, half)):
            to_at = pl.ds(first, last - first)
            from_at = pl.ds(pl.multiple_of(spots[side].start + first, 128), last - first)
            now = []
            for to, sources in ((gates_in, (wg_own, wg_oth)), (ups_in, (wu_own, wu_oth))):
                for which in range(2):
                    now.append((sources[which].at[:, from_at], to.at[which, side, :, to_at]))
            now.append(((wd_own, wd_oth)[side].at[to_at, :], downs_in.at[side, to_at, :]))
            copies = [
                pltpu.make_async_copy(src, dst, sems.at[len(steps), i])
                for i, (src, dst) in enumerate(now)
            ]
            for one in copies:
                one.start()
            steps.append(copies)
    out_ref[...] = hid_ref[...]
    dm_ref[...] = jnp.zeros_like(dm_ref)
    do_ref[...] = jnp.zeros_like(do_ref)

    def one_side(side, carry):
        sm, so, cots = sm_ref[...], so_ref[...], e_ref[...]
        at = lax.rem(idx_ref[0] + side, 2) * half
        for part, (first, last) in enumerate(((0, cut), (cut, half))):
            for now in range(2):

                @pl.when(side == now)
                def _():
                    for one in steps[2 * now + part]:
                        one.wait()

            size = last - first
            g_own, g_oth = gates_in[0, side, :, first:last], gates_in[1, side, :, first:last]
            u_own, u_oth = ups_in[0, side, :, first:last], ups_in[1, side, :, first:last]
            down = downs_in[side, first:last, :]
            gates = dot(sm, g_own) + dot(so, g_oth)
            ups = dot(sm, u_own) + dot(so, u_oth)
            sig = sigmoid(gates)
            opened = gates * sig
            act = (opened * ups).astype(BF16)
            acts[side, :, first:last] = act
            grads = dot_t(cots, down)
            gate_grad = (grads * ups * sig * (1.0 + gates * (1.0 - sig))).astype(BF16)
            up_grad = (grads * opened).astype(BF16)
            g_ref[:, pl.ds(pl.multiple_of(at + first, 128), size)] = gate_grad
            g_ref[:, pl.ds(pl.multiple_of(at + first + 2 * half, 128), size)] = up_grad
            out_ref[...] += dot(act, down)
            dm_ref[...] += dot_t(gate_grad, g_own) + dot_t(up_grad, u_own)
            do_ref[...] += dot_t(gate_grad, g_oth) + dot_t(up_grad, u_oth)
        return carry

    lax.fori_loop(0, 2, one_side, 0)
    am_ref[...] = acts[0]
    g_ref[:, 4 * half :] = acts[1]
    width = out_ref.shape[1]
    for s in range(seqs):
        at = slice(s * span, (s + 1) * span)
        places = lax.broadcasted_iota(jnp.int32, (span, width), 0) + idx_ref[1] * span
        out_ref[at, :] = jnp.where(places < idx_ref[2 + s], out_ref[at, :], 0.0)


def gate_back_kernel(dims, idx_ref, hid_ref, dm_ref, do_ref, e_ref, wo_own, wo_oth, mixture_ref,
                     og_ref, qb_ref, tot_ref, own_ref, pack_ref,
                     hg_ref, hl_ref, mg_ref, ol_ref, g2m_ref, g2o_ref, hgm_ref, hgo_ref, m0, m1, m2, m3,
                     gain, gated, gain_sum, state):
    seqs, span = dims
    half = dm_ref.shape[1]
    gain_half = gain.shape[1] // 2
    _, place_g2, _, place_hg = packed_places(half, qb_ref.shape[1] // 2, gain_half)
    mine, theirs = mine_at(idx_ref, half), theirs_at(idx_ref, half)
    hm, ho = hid_ref[:, mine], hid_ref[:, theirs]
    square = jnp.sum(hm * hm, axis=1, keepdims=True) + jnp.sum(ho * ho, axis=1, keepdims=True)
    root = lax.rsqrt(square / (2 * half) + 1e-6)
    dm, do = dm_ref[...], do_ref[...]
    g2m_ref[...] = jnp.sum(dm * hm * root, axis=0, keepdims=True)
    g2o_ref[...] = jnp.sum(do * ho * root, axis=0, keepdims=True)
    dm = dm * packed_row(own_ref, *place_g2)
    do = do * packed_row(pack_ref, *place_g2)
    along = jnp.sum(dm * hm, axis=1, keepdims=True) + jnp.sum(do * ho, axis=1, keepdims=True)
    along = along * (root * root * root) / (2 * half)
    hg_ref[:, mine] = e_ref[:, mine].astype(F32) + dm * root - hm * along
    hg_ref[:, theirs] = e_ref[:, theirs].astype(F32) + do * root - ho * along
    low = hg_ref[...].astype(BF16)
    hl_ref[...] = low
    half = wo_own.shape[0]
    gated[:, mine_at(idx_ref, half)] = dot_t(low, wo_own[...])
    gated[:, theirs_at(idx_ref, half)] = dot_t(low, wo_oth[...])
    gain[:, mine_at(idx_ref, gain_half)] = packed_row(own_ref, *place_hg)
    gain[:, theirs_at(idx_ref, gain_half)] = packed_row(pack_ref, *place_hg)
    head_gain = gain[...]
    wide = qb_ref.shape[1] // HEADS
    tall = mixture_ref.shape[1] // HEADS
    factor = wide ** (-0.5)
    quarter = state.shape[1]
    per = tall // quarter
    gain_grad = jnp.zeros((1, tall), F32)
    for s in range(seqs):
        at = slice(s * span, (s + 1) * span)
        for h in range(HEADS):
            vs = slice(h * tall, (h + 1) * tall)
            hs = slice(h * wide, (h + 1) * wide)
            mixture, opened, grad = mixture_ref[at, vs], og_ref[at, vs], gated[at, vs]
            root = lax.rsqrt(jnp.mean(mixture * mixture, axis=1, keepdims=True) + 1e-5)
            sig = sigmoid(opened)
            flat = mixture * root
            ol_ref[at, vs] = (grad * flat * head_gain * sig * (1.0 + opened * (1.0 - sig))).astype(BF16)
            grad = grad * (opened * sig)
            gain_grad += jnp.sum(grad * flat, axis=0, keepdims=True)
            grad = grad * head_gain
            along = jnp.mean(grad * flat, axis=1, keepdims=True)
            mixed = (grad - flat * along) * (root * factor)
            mg_ref[at, vs] = mixed
            part = t_dot(mixed.astype(BF16), qb_ref[at, hs])
            for q in range(per):
                state[s * per + q, :, hs] = part[q * quarter : (q + 1) * quarter]
    gain_sum[...] = gain_grad
    hgm_ref[...] = gain_sum[:, mine_at(idx_ref, gain_half)]
    hgo_ref[...] = gain_sum[:, theirs_at(idx_ref, gain_half)]
    totals = [tot_ref[pl.ds(s, 1), :] for s in range(seqs)]
    write_quarters(idx_ref, state, totals, (m0, m1, m2, m3), seqs)


def inner_back_kernel(dims, idx_ref, q_ref, k_ref, v_ref, lg_ref, a_ref, mg_ref, qb_ref, st_ref,
                      dq_ref, dk_ref, dv_ref, dc_ref):
    seqs, span = dims
    row, col = pair_iota(span)
    upto = (col <= row).astype(F32).astype(BF16)
    diagonal = row == col
    levels = level_masks(span)
    wide = q_ref.shape[1] // HEADS
    tall = v_ref.shape[1] // HEADS
    quarter = st_ref.shape[1]
    per = tall // quarter
    def one_sequence(s, carry):
        at = pl.ds(pl.multiple_of(s * span, span), span)
        logits = lg_ref[at, :]
        decays = (jnp.minimum(logits, 0.0) - jnp.log1p(jnp.exp(-jnp.abs(logits)))) / 16.0
        high, rest = two_part(decays)
        qs32, ks32 = q_ref[at, :].astype(F32), k_ref[at, :].astype(F32)
        begun = jnp.exp(dot(upto, high) + dot(upto, rest))
        pair_grads = []
        for h in range(HEADS):
            hs = slice(h * wide, (h + 1) * wide)
            vs = slice(h * tall, (h + 1) * tall)
            mixed, more = two_part(mg_ref[at, vs])
            values = v_ref[at, vs]
            full = dot_t(mixed, values) + dot_t(more, values)
            back = dot_t(values, mixed) + dot_t(values, more)
            pair_grads.append(jnp.where(row >= col, full, back))
            dv_ref[at, vs] = t_dot(a_ref[s * HEADS + h], mixed)
            own = jnp.sum(jnp.where(diagonal, full, 0.0), axis=1, keepdims=True)
            crossed = jnp.zeros((span, wide), F32)
            for q in range(per):
                part = slice(h * tall + q * quarter, h * tall + (q + 1) * quarter)
                crossed += dot(mg_ref[at, part].astype(BF16), st_ref[s * per + q, :, hs])
            dq_ref[at, hs] = own * ks32[:, hs] + begun[:, hs] * crossed
            dk_ref[at, hs] = own * qs32[:, hs]
            dc_ref[at, hs] = qb_ref[at, hs].astype(F32) * crossed
        for sums, _, both, half in levels:
            fade = jnp.exp(dot(sums, high) + dot(sums, rest))
            upper = upper_rows(half, qs32.shape[1], span)
            side = (jnp.where(upper, qs32, ks32) * fade).astype(BF16)
            for h in range(HEADS):
                hs = slice(h * wide, (h + 1) * wide)
                grads = dot(jnp.where(both, pair_grads[h], 0.0).astype(BF16), side[:, hs])
                moved = side[:, hs].astype(F32) * grads
                faded = fade[:, hs] * grads
                over = upper[:, hs]
                dc_ref[at, hs] += jnp.where(over, moved, -moved)
                dq_ref[at, hs] += jnp.where(over, faded, 0.0)
                dk_ref[at, hs] += jnp.where(over, 0.0, faded)
        return carry

    lax.fori_loop(0, seqs, one_sequence, 0)


def inputs_back_kernel(dims, idx_ref, dq_ref, dk_ref, dv_ref, dc_ref, ol_ref, kd_ref, v_ref, lg_ref, tot_ref, st_ref,
                       l0, l1, l2, l3, x_ref, hg_ref, wq_own, wq_oth, wk_own, wk_oth, wv_own, wv_oth,
                       wg_own, wg_oth, own_ref, pack_ref, g2o_ref, hgo_ref,
                       tg_ref, ga_ref, llm_ref, g1m_ref, bm_ref, small_ref,
                       leaving, logit, bias):
    seqs, span = dims
    half = wq_own.shape[0]
    part = wq_own.shape[1] // 2
    place_g1, _, _, _ = packed_places(half, part, 0)
    li_own, lo_own = packed_factors(own_ref, half)
    li_oth, lo_oth = packed_factors(pack_ref, half)
    load_state(idx_ref, (l0, l1, l2, l3), leaving)
    row, col = pair_iota(span)
    later = (col > row).astype(F32).astype(BF16)
    since = (col >= row).astype(F32).astype(BF16)
    before = (col < row).astype(F32).astype(BF16)
    keys = kd_ref.shape[1]
    vals = v_ref.shape[1]
    wide, tall = keys // HEADS, vals // HEADS
    quarter = st_ref.shape[1]
    per = tall // quarter
    bias_sum = jnp.zeros((1, keys), F32)
    for s in range(seqs):
        at = slice(s * span, (s + 1) * span)
        logits = lg_ref[at, :]
        decays = (jnp.minimum(logits, 0.0) - jnp.log1p(jnp.exp(-jnp.abs(logits)))) / 16.0
        ahead = jnp.exp(mask_dot(later, decays))
        for h in range(HEADS):
            hs = slice(h * wide, (h + 1) * wide)
            faded = kd_ref[at, hs]
            grads = jnp.zeros((span, wide), F32)
            ends = jnp.zeros((1, wide), F32)
            for q in range(per):
                vs = slice(h * tall + q * quarter, h * tall + (q + 1) * quarter)
                at_v = slice(keys * 2 + vs.start, keys * 2 + vs.stop)
                part = leaving[s * per + q, :, hs]
                ga_ref[at, at_v] = (dv_ref[at, vs] + dot_t(faded, part)).astype(BF16)
                grads += dot(v_ref[at, vs], part)
                ends += jnp.sum(
                    st_ref[s * per + q, :, hs].astype(F32) * part.astype(F32), axis=0, keepdims=True
                )
            moved = faded.astype(F32) * grads
            ga_ref[at, keys + h * wide : keys + (h + 1) * wide] = (
                dk_ref[at, hs] + ahead[:, hs] * grads
            ).astype(BF16)
            decay_grad = (
                mask_dot(since, dc_ref[at, hs])
                + mask_dot(before, moved)
                + tot_ref[pl.ds(s, 1), hs] * ends
            )
            logit_grad = decay_grad * sigmoid(-logits[:, hs]) / 16.0
            bias[:, hs] = jnp.sum(logit_grad, axis=0, keepdims=True)
            logit[at, hs] = logit_grad.astype(BF16)
        bias_sum += bias[...]
    bias[...] = bias_sum
    part = keys // 2
    bm_ref[...] = bias[:, mine_at(idx_ref, part)]
    small_ref[:, 2 * half : 2 * half + part] = bias[:, theirs_at(idx_ref, part)]
    small_ref[:, half : 2 * half] = g2o_ref[...]
    small_ref[:, 2 * half + part :] = hgo_ref[...]
    ga_ref[:, 0:keys] = dq_ref[...].astype(BF16)
    ga_ref[:, 2 * keys + vals : 2 * keys + 2 * vals] = ol_ref[...]
    llm, llo = logit[:, mine_at(idx_ref, part)], logit[:, theirs_at(idx_ref, part)]
    llm_ref[...] = llm
    lrg = (dot_t(llm, lo_own) + dot_t(llo, lo_oth)).astype(BF16)
    rest = jnp.zeros((lrg.shape[0], 128 - RANK), BF16)
    lanes = 2 * keys + 2 * vals + 128
    ga_ref[:, lanes - 128 : lanes] = jnp.concatenate([lrg, rest], axis=1)
    ga_ref[:, lanes:] = llo
    qg, kg = ga_ref[:, 0:keys], ga_ref[:, keys : 2 * keys]
    vg = ga_ref[:, 2 * keys : 2 * keys + vals]
    og = ga_ref[:, 2 * keys + vals : 2 * keys + 2 * vals]
    dm = dot_t(qg, wq_own[...]) + dot_t(kg, wk_own[...]) + dot_t(vg, wv_own[...])
    dm = dm + dot_t(og, wg_own[...]) + dot(lrg, li_own)
    do = dot_t(qg, wq_oth[...]) + dot_t(kg, wk_oth[...]) + dot_t(vg, wv_oth[...])
    do = do + dot_t(og, wg_oth[...]) + dot(lrg, li_oth)
    mine, theirs = mine_at(idx_ref, half), theirs_at(idx_ref, half)
    xm, xo = x_ref[:, mine].astype(F32), x_ref[:, theirs].astype(F32)
    square = jnp.sum(xm * xm, axis=1, keepdims=True) + jnp.sum(xo * xo, axis=1, keepdims=True)
    root = lax.rsqrt(square / (2 * half) + 1e-6)
    g1m_ref[...] = jnp.sum(dm * xm * root, axis=0, keepdims=True)
    small_ref[:, 0:half] = jnp.sum(do * xo * root, axis=0, keepdims=True)
    dm = dm * packed_row(own_ref, *place_g1)
    do = do * packed_row(pack_ref, *place_g1)
    along = jnp.sum(dm * xm, axis=1, keepdims=True) + jnp.sum(do * xo, axis=1, keepdims=True)
    along = along * (root * root * root) / (2 * half)
    tg_ref[:, mine] = hg_ref[:, mine] + dm * root - xm * along
    tg_ref[:, theirs] = hg_ref[:, theirs] + do * root - xo * along


def block_of(position, order):
    block = 0
    for at, bit in enumerate(order):
        if (position >> (3 - at)) & 1:
            block |= bit
    return block


def deal(position, keep_ref, send_ref):
    return keep_ref.at[position] if position < 8 else send_ref.at[position - 8]


def wide_grad_kernel(orders, idx_ref, sm_ref, so_ref, gm_ref, go_ref, k0, s0, k1, s1, full):
    place = lax.rem(idx_ref[1], 16)
    width = full.shape[1]
    high = full.shape[0] // 16
    for which, refs in enumerate(((k0, s0), (k1, s1))):
        cols = slice(which * width, (which + 1) * width)
        full[...] = t_dot(sm_ref[...], gm_ref[:, cols]) + t_dot(so_ref[...], go_ref[:, cols])
        for position in range(16):
            block = block_of(position, orders[which]) ^ place
            rows = full[pl.ds(pl.multiple_of(block * high, high), high), :].astype(BF16)
            to = deal(position, *refs)
            for tile in range(width // 128):
                to[tile * high : (tile + 1) * high, :] = rows[:, tile * 128 : (tile + 1) * 128]


def down_grad_kernel(order, idx_ref, am_ref, go_ref, em_ref, eo_ref, keep_ref, send_ref, full):
    place = lax.rem(idx_ref[1], 16)
    first = go_ref.shape[1] - am_ref.shape[1]
    full[...] = t_dot(am_ref[...], em_ref[...]) + t_dot(go_ref[:, first:], eo_ref[...])
    high = full.shape[0] // 2
    for position in range(16):
        block = block_of(position, order) ^ place
        rows = pl.ds(pl.multiple_of(lax.div(block, 8) * high, 16), high)
        cols = pl.ds(pl.multiple_of(lax.rem(block, 8) * 128, 128), 128)
        deal(position, keep_ref, send_ref)[...] = full[rows, cols].astype(BF16)


def attention_grad_kernel(orders, cuts, idx_ref, nm_ref, no_ref, gm_ref, go_ref, am_ref, ao_ref, hm_ref, ho_ref,
                          lrm_ref, lro_ref, llm_ref, g1_ref, g2_ref, b_ref, hg_ref, small_ref, k0, s0, k1, s1, k2, s2, full, outer, small):
    place = lax.rem(idx_ref[1], 16)
    lanes = full.shape[1]
    full[...] = t_dot(nm_ref[...], gm_ref[:, 0:lanes]) + t_dot(no_ref[...], go_ref[:, 0:lanes])
    outer[...] = t_dot(am_ref[...], hm_ref[...]) + t_dot(ao_ref[...], ho_ref[...])
    low_out = t_dot(lrm_ref[...], llm_ref[...]) + t_dot(lro_ref[...], go_ref[:, lanes:])
    small[...] = jnp.zeros_like(small)
    small[0] = low_out[:, 0:128]
    small[1] = low_out[:, 128:256]
    line = 0
    for ref in (g1_ref, g2_ref, b_ref, hg_ref):
        row = ref[...] + small_ref[:, line * 128 : line * 128 + ref.shape[1]]
        for tile in range(row.shape[1] // 128):
            small[2, line : line + 1, :] = row[:, tile * 128 : (tile + 1) * 128]
            line += 1
    high = full.shape[0] // 16
    tiles = full.shape[1] // 128
    for which, refs in enumerate(((k0, s0), (k1, s1), (k2, s2))):
        first, last = cuts[which], cuts[which + 1]
        for position in range(16):
            block = block_of(position, orders[which]) ^ place
            at = pl.ds(pl.multiple_of(block * high, high), high)
            to = deal(position, *refs)
            for tile in range(first, last):
                if tile < tiles:
                    rows = full[at, tile * 128 : (tile + 1) * 128]
                else:
                    rows = outer[at, (tile - tiles) * 128 : (tile - tiles + 1) * 128]
                to[(tile - first) * high : (tile - first + 1) * high, :] = rows.astype(BF16)
            if which == 2:
                to[(last - first) * high :, :] = small[block].astype(BF16)


def wide_open_kernel(order, idx_ref, own_ref, got_ref, out_ref):
    place = lax.rem(idx_ref[1], 16)
    high = out_ref.shape[0] // 16
    for position in range(16):
        block = block_of(position, order) ^ place
        held = deal(position, own_ref, got_ref)
        at = pl.ds(pl.multiple_of(block * high, high), high)
        for tile in range(out_ref.shape[1] // 128):
            out_ref[at, tile * 128 : (tile + 1) * 128] = held[tile * high : (tile + 1) * high, :].astype(F32)


def down_open_kernel(order, idx_ref, own_ref, got_ref, out_ref):
    place = lax.rem(idx_ref[1], 16)
    high = out_ref.shape[0] // 2
    for position in range(16):
        block = block_of(position, order) ^ place
        rows = pl.ds(pl.multiple_of(lax.div(block, 8) * high, 16), high)
        cols = pl.ds(pl.multiple_of(lax.rem(block, 8) * 128, 128), 128)
        out_ref[rows, cols] = deal(position, own_ref, got_ref)[...].astype(F32)


def attention_open_kernel(orders, cuts, idx_ref, o0, r0, o1, r1, o2, r2, q_ref, k_ref, v_ref, og_ref, li_ref, w_ref,
                          lo_ref, g1_ref, g2_ref, b_ref, hg_ref, small, first_factor):
    place = lax.rem(idx_ref[1], 16)
    high = q_ref.shape[0] // 16
    homes = []
    for ref in (q_ref, k_ref, v_ref, og_ref):
        homes += [(ref, tile) for tile in range(ref.shape[1] // 128)]
    homes.append((first_factor, 0))
    homes += [(w_ref, tile) for tile in range(w_ref.shape[1] // 128)]
    for which, refs in enumerate(((o0, r0), (o1, r1), (o2, r2))):
        first, last = cuts[which], cuts[which + 1]
        for position in range(16):
            block = block_of(position, orders[which]) ^ place
            at = pl.ds(pl.multiple_of(block * high, high), high)
            held = deal(position, *refs)
            for tile in range(first, last):
                rows = held[(tile - first) * high : (tile - first + 1) * high, :].astype(F32)
                ref, column = homes[tile]
                ref[at, column * 128 : (column + 1) * 128] = rows
            if which == 2:
                small[block] = held[(last - first) * high :, :].astype(F32)
    li_ref[...] = first_factor[...].T[0 : li_ref.shape[0], :]
    lo_ref[:, 0:128] = small[0]
    lo_ref[:, 128:256] = small[1]
    line = 0
    for ref in (g1_ref, g2_ref, b_ref, hg_ref):
        for tile in range(ref.shape[1] // 128):
            ref[:, tile * 128 : (tile + 1) * 128] = small[2, line : line + 1, :]
            line += 1


def across(array):
    return lax.ppermute(array, "fsdp", ((0, 1), (1, 0)))


def swap(array, bit):
    count = lax.axis_size("seq")
    return lax.ppermute(array, "seq", tuple((one, one ^ bit) for one in range(count)))


def ahead(array, step):
    count = lax.axis_size("seq")
    return lax.ppermute(
        array,
        "seq",
        tuple((one, one + step) for one in range(count) if 0 <= one + step < count),
    )


def fence(*groups):
    return lax.optimization_barrier(groups)


class Portions:
    def __init__(self, parts, orders):
        self.kept = [keep for keep, _ in parts]
        self.sent = [send for _, send in parts]
        self.orders = orders

    def move(self, arrays, step):
        if step < 3:
            return [swap(a, order[step]) for a, order in zip(arrays, self.orders)]
        return self.move_all(arrays, self.orders[0][3])

    def move_all(self, arrays, bit):
        got = swap(jnp.concatenate(arrays, axis=1), bit)
        ends = [0]
        for a in arrays:
            ends.append(ends[-1] + a.shape[1])
        return [got[:, first:last] for first, last in zip(ends[:-1], ends[1:])]

    def reduce_start(self, step):
        return self.move(self.sent, step)

    def reduce_end(self, step, got):
        for one, more in enumerate(got):
            if step < 3:
                half = more.shape[0] // 2
                self.sent[one] = self.kept[one][half:] + more[half:]
                self.kept[one] = self.kept[one][:half] + more[:half]
            else:
                self.kept[one] = self.kept[one] + more
        bit = 16
        while step == 3 and bit < lax.axis_size("seq"):
            more = self.move_all(self.kept, bit)
            self.kept = [k + m for k, m in zip(self.kept, more)]
            bit *= 2

    def gather_start(self, step):
        return self.move(self.kept, step)

    def gather_end(self, step, got):
        if step:
            self.kept = [jnp.concatenate([k, more], axis=0) for k, more in zip(self.kept, got)]
        else:
            self.halves = list(zip(self.kept, got))


def scan_near(messages):
    return [messages[0]] + [swap(messages[o], o) for o in (1, 2, 3)]


def scan_scratch(messages):
    rows, lanes = messages[0].shape
    return [((4, rows - 16, lanes), F32), ((4, 1, lanes), F32)]


def scan_total(near, idx, reverse):
    return call("group_total", partial(group_total, reverse), idx, near, [(near[0].shape, BF16)], scan_scratch(near))[0]


def scan_far(total, reverse):
    sign = -4 if reverse else 4
    return [ahead(total, sign * step) for step in range(1, lax.axis_size("seq") // 4)]


def scan_entering(far, near, idx, reverse):
    rows, lanes = near[0].shape
    return call(
        "group_entering", partial(group_entering, reverse, len(far)), idx, list(far) + list(near),
        [((rows - 16, lanes), BF16)] * 4, scan_scratch(near) + [((4, rows - 16, lanes), F32)],
    )


def shards(
    tokens,
    lengths,
    first_gain,
    query_weight,
    key_weight,
    value_weight,
    outgate_weight,
    lowrank_in,
    lowrank_out,
    decay_bias,
    head_gain,
    output_weight,
    second_gain,
    gate_weight,
    up_weight,
    down_weight,
    cotangent,
):
    micro_count, pair_count, span, width = tokens.shape
    seqs = micro_count * pair_count
    rows = seqs * span
    dims = (seqs, span)
    core = lax.axis_index("fsdp")
    place = lax.axis_index("seq")
    own_lengths = lax.dynamic_slice_in_dim(lengths, core * pair_count, pair_count, 1).reshape(-1)
    idx = jnp.concatenate([jnp.stack([core, place]).astype(jnp.int32), own_lengths])
    keys, vals, ff = query_weight.shape[1], value_weight.shape[1], gate_weight.shape[1]
    half = query_weight.shape[0]
    tall = vals // HEADS
    quarter = seqs * tall // 4

    x = tokens.reshape(rows, width)
    cot = cotangent.reshape(rows, width)
    lrank = lowrank_in.shape[1]
    lines, at = 0, 0
    for a in (first_gain, second_gain, decay_bias, head_gain):
        lines = lines + jnp.pad(a, (at, 16 * 128 - at - a.size))
        at += a.size
    lines = lines.reshape(16, 128)
    pack = call(
        "pack", pack_kernel, idx, [lowrank_in.T, lowrank_out, lines],
        [((lrank * (half + lowrank_out.shape[1]) // 128 + 16, 128), BF16)],
    )[0]
    pack2, wk2, wv2 = (across(a) for a in (pack, key_weight, value_weight))

    message = ((quarter + 16, keys), BF16)
    state = ((4, quarter, keys), F32)
    nm, no, k, v, lr, lg, kd, tot, *messages = call(
        "keys", partial(keys_kernel, dims), idx,
        [x, key_weight, wk2, value_weight, wv2, pack, pack2],
        [((rows, half), BF16), ((rows, half), BF16), ((rows, keys), BF16), ((rows, vals), BF16),
         ((rows, lrank), BF16), ((rows, keys), F32), ((rows, keys), BF16), ((seqs, keys), F32)]
        + [message] * 4,
        [state],
    )
    messages, outgate_send, query_send = fence(messages, outgate_weight, query_weight)
    near = scan_near(messages)
    wg2, wq2 = across(outgate_send), across(query_send)
    q, og, mix, scores, qb, cots = call(
        "inner", partial(inner_kernel, dims), idx,
        [nm, no, query_weight, wq2, outgate_weight, wg2, k, v, lg, cot],
        [((rows, keys), BF16), ((rows, vals), F32), ((rows, vals), F32), ((seqs * HEADS, span, span), BF16),
         ((rows, keys), BF16), ((rows, width), BF16)],
    )
    near, mix, gate_send, up_send = fence(near, mix, gate_weight, up_weight)
    total = scan_total(near, idx, False)
    total, gate_send, up_send = fence(total, gate_send, up_send)
    far = scan_far(total, False)
    wgate2, wup2 = across(gate_send), across(up_send)
    far, wgate2, wup2 = fence(far, wgate2, wup2)
    pieces = scan_entering(far, near, idx, False)
    pieces, output_send, down_send = fence(pieces, output_weight, down_weight)
    pieces = [pieces[0]] + [swap(pieces[o], o) for o in (1, 2, 3)]
    wo2, wdown2 = across(output_send), across(down_send)
    mixture, gm, go, hid, sm, so, st = call(
        "hidden", partial(hidden_kernel, dims), idx,
        [mix, qb, *pieces, og, x, output_weight, wo2, pack, pack2],
        [((rows, vals), F32), ((rows, vals // 2), BF16), ((rows, vals // 2), BF16), ((rows, width), F32),
         ((rows, half), BF16), ((rows, half), BF16), ((4, quarter, keys), BF16)],
        [((1, tall), F32), ((rows, vals), BF16)],
    )
    so, no_send, lr_send, cots_send = fence(so, no, lr, cots)
    so2, no2, go2, lr2, cots2 = (across(a) for a in (so, no_send, go, lr_send, cots_send))
    out, am, gu, dm, do = call(
        "ffn", partial(ffn_kernel, dims), idx,
        [sm, so, hid, cots, gate_weight, wgate2, up_weight, wup2, down_weight, wdown2],
        [((rows, width), F32), ((rows, ff // 2), BF16), ((rows, 5 * ff // 2), BF16),
         ((rows, half), F32), ((rows, half), F32)],
        [((2, 2, half, ff // 2), BF16), ((2, 2, half, ff // 2), BF16), ((2, ff // 2, width), BF16),
         ((2, rows, ff // 2), BF16), pltpu.SemaphoreType.DMA((4, 5))], limit=42, far=6,
    )
    so2, no2, go2, lr2, cots2, gu = fence(so2, no2, go2, lr2, cots2, gu)

    orders = ((1, 2, 4, 8), (2, 4, 1, 8), (4, 1, 2, 8))
    hg, hl, mg, ol, g2m, g2o, hgm, hgo, *messages = call(
        "gate_back", partial(gate_back_kernel, dims), idx,
        [hid, dm, do, cots, output_weight, wo2, mixture, og, qb, tot, pack, pack2],
        [((rows, width), F32), ((rows, width), BF16), ((rows, vals), F32), ((rows, vals), BF16),
         ((1, half), F32), ((1, half), F32), ((1, tall // 2), F32), ((1, tall // 2), F32)] + [message] * 4,
        [((1, tall), F32), ((rows, vals), F32), ((1, tall), F32), state],
    )
    messages, gu_send, mg = fence(messages, gu, mg)
    near = scan_near(messages)
    gu2 = across(gu_send)
    dq, dk, dv, dc = call(
        "inner_back", partial(inner_back_kernel, dims), idx, [q, k, v, lg, scores, mg, qb, st],
        [((rows, keys), F32), ((rows, keys), F32), ((rows, vals), F32), ((rows, keys), F32)],
    )
    near, gu2, dq = fence(near, gu2, dq)
    total = scan_total(near, idx, True)
    total, gu2 = fence(total, gu2)
    far = scan_far(total, True)
    portion = ff // 128 * (half // 16)
    flat = [((8, portion, 128), BF16)] * 2
    wide_parts = call("wide_grad", partial(wide_grad_kernel, orders), idx, [sm, so2, gu, gu2], flat * 2,
                      [((half, ff), F32)], limit=32)
    am, wide_parts = fence(am, wide_parts)
    down_parts = call("down_grad", partial(down_grad_kernel, orders[2]), idx, [am, gu2, cots, cots2], flat,
                      [((ff // 2, width), F32)])
    far, down_parts = fence(far, down_parts)
    first = Portions([wide_parts[0:2], wide_parts[2:4], down_parts], orders)
    got = first.reduce_start(0)
    pieces = scan_entering(far, near, idx, True)
    pieces = [pieces[0]] + [swap(pieces[o], o) for o in (1, 2, 3)]
    got, pieces = fence(got, pieces)
    first.reduce_end(0, got)
    first.sent, pieces = fence(first.sent, pieces)
    got = first.reduce_start(1)
    lanes = 2 * keys + 2 * vals + 128
    tg, ga, llm, g1m, bm, small = call(
        "inputs_back", partial(inputs_back_kernel, dims), idx,
        [dq, dk, dv, dc, ol, kd, v, lg, tot, st, *pieces, x, hg, query_weight, wq2, key_weight, wk2,
         value_weight, wv2, outgate_weight, wg2, pack, pack2, g2o, hgo],
        [((rows, width), F32), ((rows, lanes + keys // 2), BF16), ((rows, keys // 2), BF16),
         ((1, half), F32), ((1, keys // 2), F32), ((1, 2 * half + keys // 2 + tall // 2), F32)],
        [((4, quarter, keys), BF16), ((rows, keys), BF16), ((1, keys), F32)], limit=32,
    )
    got, ga, small = fence(got, ga, small)
    first.reduce_end(1, got)
    got = first.reduce_start(2)
    ga2, small2, hl2 = across(ga), across(small), across(hl)
    tiles = lanes // 128 + width // 128
    cuts = (0, tiles // 3, 2 * tiles // 3, tiles)
    high = half // 16
    shapes = []
    for which in range(3):
        size = (cuts[which + 1] - cuts[which]) * high + (16 if which == 2 else 0)
        shapes += [((8, size, 128), BF16)] * 2
    parts = call(
        "attention_grad", partial(attention_grad_kernel, orders, cuts), idx,
        [nm, no2, ga, ga2, gm, go2, hl, hl2, lr, lr2, llm, g1m, g2m, bm, hgm, small2],
        shapes, [((half, lanes), F32), ((vals // 2, width), F32), ((16, 16, 128), F32)], limit=32,
    )
    got, parts = fence(got, parts)
    first.reduce_end(2, got)
    second = Portions([parts[0:2], parts[2:4], parts[4:6]], orders)
    got, more = fence(first.reduce_start(3), second.reduce_start(0))
    first.reduce_end(3, got)
    second.reduce_end(0, more)
    got, more = fence(first.gather_start(3), second.reduce_start(1))
    first.gather_end(3, got)
    second.reduce_end(1, more)
    both = [jnp.concatenate([k, a], axis=1) for k, a in zip(first.kept, second.sent)]
    both = fence(*[swap(a, order[2]) for a, order in zip(both, orders)])
    got = [a[:, : k.shape[1]] for a, k in zip(both, first.kept)]
    more = [a[:, k.shape[1] :] for a, k in zip(both, first.kept)]
    first.gather_end(2, got)
    second.reduce_end(2, more)
    got, more = fence(first.gather_start(1), second.reduce_start(3))
    first.gather_end(1, got)
    second.reduce_end(3, more)
    got, more = fence(first.gather_start(0), second.gather_start(3))
    first.gather_end(0, got)
    second.gather_end(3, more)
    gate_halves, up_halves, down_halves = first.halves
    more = second.gather_start(2)
    gate_out = call("gate_open", partial(wide_open_kernel, orders[0]), idx, gate_halves, [((half, ff), F32)])[0]
    more, gate_out = fence(more, gate_out)
    second.gather_end(2, more)
    more = second.gather_start(1)
    up_out = call("up_open", partial(wide_open_kernel, orders[1]), idx, up_halves, [((half, ff), F32)])[0]
    more, up_out = fence(more, up_out)
    second.gather_end(1, more)
    more = second.gather_start(0)
    down_out = call("down_open", partial(down_open_kernel, orders[2]), idx, down_halves, [((ff // 2, width), F32)])[0]
    more, down_out = fence(more, down_out)
    second.gather_end(0, more)
    opened = call(
        "attention_open", partial(attention_open_kernel, orders, cuts), idx, [a for pair in second.halves for a in pair],
        [((half, keys), F32), ((half, keys), F32), ((half, vals), F32), ((half, vals), F32),
         ((lrank, half), F32), ((vals // 2, width), F32), ((lrank, keys // 2), F32),
         ((1, half), F32), ((1, half), F32), ((1, keys // 2), F32), ((1, tall // 2), F32)],
        [((16, 16, 128), F32), ((half, 128), F32)],
    )
    q_out, k_out, v_out, og_out, li_out, w_out, lo_out, g1_out, g2_out, b_out, hg_out = opened
    return (
        out.reshape(tokens.shape),
        tg.reshape(tokens.shape),
        g1_out.reshape(-1),
        q_out,
        k_out,
        v_out,
        og_out,
        li_out.T,
        lo_out,
        b_out.reshape(-1),
        hg_out.reshape(-1),
        w_out,
        g2_out.reshape(-1),
        gate_out,
        up_out,
        down_out,
    )


def solution(mesh):
    shard, column = P("fsdp", None), P(None, "fsdp")
    stream, line = P(None, "fsdp", "seq", None), P("fsdp")
    weights = (line, shard, shard, shard, shard, shard, column, line, line, shard, line, shard, shard, shard)
    return jax.shard_map(
        shards,
        mesh=mesh,
        in_specs=(stream, P()) + weights + (stream,),
        out_specs=(stream, stream) + weights,
        check_vma=False,
    )
```

```python
from functools import partial

import jax
import jax.numpy as jnp
from jax import lax
from jax.experimental import pallas as pl
from jax.experimental.pallas import tpu as pltpu
from jax.sharding import PartitionSpec as P

HEADS = 4
RANK = 16
F32 = jnp.float32
BF16 = jnp.bfloat16
MIB = 1024 * 1024


def dot(first_op, second_op):
    return jnp.dot(first_op, second_op, preferred_element_type=F32)


def dot_t(first_op, second_op):
    return lax.dot_general(
        first_op, second_op, (((1,), (1,)), ((), ())), preferred_element_type=F32
    )


def t_dot(first_op, second_op):
    return lax.dot_general(
        first_op, second_op, (((0,), (0,)), ((), ())), preferred_element_type=F32
    )


def two_part(value):
    high = value.astype(BF16)
    return high, (value - high.astype(F32)).astype(BF16)


def mask_dot(mask, value):
    high, rest = two_part(value)
    return dot(mask, high) + dot(mask, rest)


def sigmoid(value):
    return 1.0 / (1.0 + jnp.exp(-value))


def pair_iota(size):
    return (
        lax.broadcasted_iota(jnp.int32, (size, size), 0),
        lax.broadcasted_iota(jnp.int32, (size, size), 1),
    )


def level_masks(size):
    row, col = pair_iota(size)
    out = []
    half = size // 2
    while half >= 1:
        block = 2 * half
        row_block = row // block
        middle = row_block * block + half - 1
        upper = row > middle
        sums = (upper & (col > middle) & (col <= row)) | (
            jnp.logical_not(upper) & (col > row) & (col <= middle)
        )
        same = row_block == col // block
        pairs = same & upper & (col <= middle)
        both = same & (upper != (col > middle))
        out.append((sums.astype(F32).astype(BF16), pairs, both, half))
        half //= 2
    return out


def upper_rows(half, width, size):
    row = lax.broadcasted_iota(jnp.int32, (size, width), 0)
    return row % (2 * half) >= half


def seat(idx_ref):
    return idx_ref[0], idx_ref[1]


def mine_at(idx_ref, width):
    return pl.ds(pl.multiple_of(idx_ref[0] * width, 128), width)


def theirs_at(idx_ref, width):
    return pl.ds(pl.multiple_of((1 - idx_ref[0]) * width, 128), width)


SMEM = pl.BlockSpec(memory_space=pltpu.SMEM)
VMEM = pl.BlockSpec(memory_space=pltpu.VMEM)


def call(name, body, idx, inputs, outs, scratch=(), limit=24, far=0):
    shapes = [jax.ShapeDtypeStruct(s, d) for s, d in outs]
    result = pl.pallas_call(
        body,
        name=name,
        out_shape=shapes,
        in_specs=[SMEM] + [VMEM] * (len(inputs) - far) + [pl.BlockSpec(memory_space=pl.ANY)] * far,
        out_specs=[VMEM] * len(shapes),
        scratch_shapes=[pltpu.VMEM(*s) if isinstance(s, tuple) else s for s in scratch],
        compiler_params=pltpu.CompilerParams(vmem_limit_bytes=limit * MIB),
        cost_estimate=pl.CostEstimate(flops=1, bytes_accessed=1, transcendentals=0),
    )(idx, *inputs)
    return result


def put_message(ref, rows, total):
    count = rows.shape[0]
    ref[pl.ds(0, count), :] = rows.astype(BF16)
    high = total.astype(BF16)
    rest = total - high.astype(F32)
    middle = rest.astype(BF16)
    low = (rest - middle.astype(F32)).astype(BF16)
    tail = jnp.concatenate(
        [high, middle, low, jnp.zeros((13,) + total.shape[1:], BF16)], axis=0
    )
    ref[pl.ds(count, 16), :] = tail


def get_message(ref):
    count = ref.shape[0] - 16
    tail = ref[pl.ds(count, 16), :].astype(F32)
    return ref[pl.ds(0, count), :].astype(F32), tail[0:1] + tail[1:2] + tail[2:3]


def write_quarters(idx_ref, state, totals, messages, seq_count):
    low = lax.rem(idx_ref[1], 4)
    for other in range(4):
        quarter = low ^ other
        total = totals[0]
        for one in range(1, seq_count):
            total = jnp.where(quarter * seq_count // 4 >= one, totals[one], total)
        put_message(messages[other], state[quarter], total)


def group_total(reverse, idx_ref, *refs):
    out_ref, kept, held = refs[4], refs[5], refs[6]
    low = lax.rem(idx_ref[1], 4)
    for other in range(4):
        rows, total = get_message(refs[other])
        kept[low ^ other] = rows
        held[low ^ other] = total
    order = (3, 2, 1, 0) if reverse else (0, 1, 2, 3)
    rows, total = kept[order[0]], held[order[0]]
    for one in order[1:]:
        rows = held[one] * rows + kept[one]
        total = total * held[one]
    put_message(out_ref, rows, total)


def group_entering(reverse, far_count, idx_ref, *refs):
    far, near = refs[:far_count], refs[far_count : far_count + 4]
    outs = refs[far_count + 4 : far_count + 8]
    kept, held, entering = refs[far_count + 8 :]
    low = lax.rem(idx_ref[1], 4)
    for other in range(4):
        rows, total = get_message(near[other])
        kept[low ^ other] = rows
        held[low ^ other] = total
    rows = jnp.zeros(kept.shape[1:], F32)
    for one in far[::-1]:
        part, total = get_message(one)
        rows = total * rows + part
    for one in (3, 2, 1, 0) if reverse else (0, 1, 2, 3):
        entering[one] = rows
        rows = held[one] * rows + kept[one]
    for other in range(4):
        outs[other][...] = entering[low ^ other].astype(BF16)


def load_state(idx_ref, pieces, state):
    low = lax.rem(idx_ref[1], 4)
    for other in range(4):
        state[low ^ other] = pieces[other][...]


def pack_kernel(idx_ref, li_ref, lo_ref, lines_ref, out_ref):
    at = 0
    for ref in (li_ref, lo_ref):
        rank = ref.shape[0]
        for tile in range(ref.shape[1] // 128):
            out_ref[at : at + rank, :] = ref[:, tile * 128 : (tile + 1) * 128]
            at += rank
    out_ref[at:, :] = lines_ref[...]


def packed_factors(pack_ref, half):
    rank = RANK
    high = pack_ref.shape[0] - 16
    tiles = [pack_ref[at : at + rank, :] for at in range(0, high, rank)]
    first = half // 128
    return jnp.concatenate(tiles[:first], axis=1), jnp.concatenate(tiles[first:], axis=1)


def packed_row(pack_ref, first, count):
    lines = pack_ref[pack_ref.shape[0] - 16 :, :].astype(F32)
    return jnp.concatenate([lines[t : t + 1, :] for t in range(first, first + count)], axis=1)


def packed_places(half, part, gain):
    g1, b, hg = half // 128, part // 128, gain // 128
    return (0, g1), (g1, g1), (2 * g1, b), (2 * g1 + b, hg)


def keys_kernel(dims, idx_ref, x_ref, wk_own, wk_oth, wv_own, wv_oth, own_ref, pack_ref,
                nm_ref, no_ref, k_ref, v_ref, lr_ref, lg_ref, kd_ref, tot_ref,
                m0, m1, m2, m3, state):
    seqs, span = dims
    half = wk_own.shape[0]
    part = wk_own.shape[1] // 2
    place_g1, _, place_b, _ = packed_places(half, part, 0)
    li_own, lo_own = packed_factors(own_ref, half)
    li_oth, lo_oth = packed_factors(pack_ref, half)
    g1_own, b_own = packed_row(own_ref, *place_g1), packed_row(own_ref, *place_b)
    g1_oth, b_oth = packed_row(pack_ref, *place_g1), packed_row(pack_ref, *place_b)
    xm = x_ref[:, mine_at(idx_ref, half)].astype(F32)
    xo = x_ref[:, theirs_at(idx_ref, half)].astype(F32)
    square = jnp.sum(xm * xm, axis=1, keepdims=True) + jnp.sum(xo * xo, axis=1, keepdims=True)
    root = lax.rsqrt(square / (2 * half) + 1e-6)
    nm = (xm * root * g1_own).astype(BF16)
    no = (xo * root * g1_oth).astype(BF16)
    nm_ref[...] = nm
    no_ref[...] = no
    lr = (dot_t(nm, li_own) + dot_t(no, li_oth)).astype(BF16)
    lr_ref[...] = lr
    lg_ref[:, mine_at(idx_ref, part)] = dot(lr, lo_own) + b_own
    lg_ref[:, theirs_at(idx_ref, part)] = dot(lr, lo_oth) + b_oth
    keys = (dot(nm, wk_own[...]) + dot(no, wk_oth[...])).astype(BF16)
    k_ref[...] = keys
    values = (dot(nm, wv_own[...]) + dot(no, wv_oth[...])).astype(BF16)
    v_ref[...] = values
    row, col = pair_iota(span)
    later = (col > row).astype(F32).astype(BF16)
    wide = keys.shape[1] // HEADS
    tall = values.shape[1] // HEADS
    quarter = state.shape[1]
    totals = []
    for s in range(seqs):
        at = slice(s * span, (s + 1) * span)
        logits = lg_ref[at, :]
        decays = (jnp.minimum(logits, 0.0) - jnp.log1p(jnp.exp(-jnp.abs(logits)))) / 16.0
        ahead = mask_dot(later, decays)
        totals.append(jnp.exp(jnp.sum(decays, axis=0, keepdims=True)))
        tot_ref[pl.ds(s, 1), :] = totals[s]
        faded = (keys[at].astype(F32) * jnp.exp(ahead)).astype(BF16)
        kd_ref[at, :] = faded
        for h in range(HEADS):
            part = t_dot(values[at, h * tall : (h + 1) * tall], faded[:, h * wide : (h + 1) * wide])
            per = tall // quarter
            for q in range(per):
                state[s * per + q, :, h * wide : (h + 1) * wide] = part[q * quarter : (q + 1) * quarter]
    write_quarters(idx_ref, state, totals, (m0, m1, m2, m3), seqs)


def inner_kernel(dims, idx_ref, nm_ref, no_ref, wq_own, wq_oth, wg_own, wg_oth, k_ref, v_ref, lg_ref, cot_ref,
                 q_ref, og_ref, mix_ref, a_ref, qb_ref, e_ref):
    seqs, span = dims
    for s in range(seqs):
        at = slice(s * span, (s + 1) * span)
        places = lax.broadcasted_iota(jnp.int32, (span, cot_ref.shape[1]), 0) + idx_ref[1] * span
        e_ref[at, :] = jnp.where(places < idx_ref[2 + s], cot_ref[at, :].astype(F32), 0.0).astype(BF16)
    nm, no = nm_ref[...], no_ref[...]
    queries = (dot(nm, wq_own[...]) + dot(no, wq_oth[...])).astype(BF16)
    q_ref[...] = queries
    og_ref[...] = dot(nm, wg_own[...]) + dot(no, wg_oth[...])
    row, col = pair_iota(span)
    upto = (col <= row).astype(F32).astype(BF16)
    diagonal = row == col
    levels = level_masks(span)
    wide = queries.shape[1] // HEADS
    tall = v_ref.shape[1] // HEADS
    def one_sequence(s, carry):
        at = pl.ds(pl.multiple_of(s * span, span), span)
        logits = lg_ref[at, :]
        decays = (jnp.minimum(logits, 0.0) - jnp.log1p(jnp.exp(-jnp.abs(logits)))) / 16.0
        high, rest = two_part(decays)
        qs, ks = q_ref[at, :], k_ref[at, :]
        qs32, ks32 = qs.astype(F32), ks.astype(F32)
        qb_ref[at, :] = (qs32 * jnp.exp(dot(upto, high) + dot(upto, rest))).astype(BF16)
        scores = []
        for h in range(HEADS):
            hs = slice(h * wide, (h + 1) * wide)
            scores.append(jnp.where(diagonal, dot_t(qs[:, hs], ks[:, hs]), 0.0))
        for sums, pairs, _, half in levels:
            fade = jnp.exp(dot(sums, high) + dot(sums, rest))
            side = (jnp.where(upper_rows(half, qs.shape[1], span), qs32, ks32) * fade).astype(BF16)
            for h in range(HEADS):
                part = side[:, h * wide : (h + 1) * wide]
                scores[h] = scores[h] + jnp.where(pairs, dot_t(part, part), 0.0)
        for h in range(HEADS):
            low = scores[h].astype(BF16)
            a_ref[s * HEADS + h] = low
            vs = slice(h * tall, (h + 1) * tall)
            mix_ref[at, vs] = dot(low, v_ref[at, vs])
        return carry

    lax.fori_loop(0, seqs, one_sequence, 0)


def hidden_kernel(dims, idx_ref, mix_ref, qb_ref, e0, e1, e2, e3, og_ref, x_ref, wo_own, wo_oth,
                  own_ref, pack_ref, mixture_ref, gm_ref, go_ref, hid_ref, sm_ref, so_ref, st_ref,
                  gain, gated):
    seqs, span = dims
    load_state(idx_ref, (e0, e1, e2, e3), st_ref)
    half = sm_ref.shape[1]
    gain_half = gain.shape[1] // 2
    _, place_g2, _, place_hg = packed_places(half, qb_ref.shape[1] // 2, gain_half)
    gain[:, mine_at(idx_ref, gain_half)] = packed_row(own_ref, *place_hg)
    gain[:, theirs_at(idx_ref, gain_half)] = packed_row(pack_ref, *place_hg)
    wide = qb_ref.shape[1] // HEADS
    tall = mix_ref.shape[1] // HEADS
    factor = wide ** (-0.5)
    quarter = st_ref.shape[1]
    per = tall // quarter
    head_gain = gain[...]
    for s in range(seqs):
        at = slice(s * span, (s + 1) * span)
        for h in range(HEADS):
            hs = slice(h * wide, (h + 1) * wide)
            for q in range(per):
                vs = slice(h * tall + q * quarter, h * tall + (q + 1) * quarter)
                carried = dot_t(qb_ref[at, hs], st_ref[s * per + q, :, hs])
                mixture_ref[at, vs] = (mix_ref[at, vs] + carried) * factor
            vs = slice(h * tall, (h + 1) * tall)
            mixture = mixture_ref[at, vs]
            root = lax.rsqrt(jnp.mean(mixture * mixture, axis=1, keepdims=True) + 1e-5)
            opened = og_ref[at, vs]
            gated[at, vs] = (mixture * root * head_gain * (opened * sigmoid(opened))).astype(BF16)
    half = wo_own.shape[0]
    gm = gated[:, mine_at(idx_ref, half)]
    go = gated[:, theirs_at(idx_ref, half)]
    gm_ref[...] = gm
    go_ref[...] = go
    hid_ref[...] = x_ref[...].astype(F32) + dot(gm, wo_own[...]) + dot(go, wo_oth[...])
    half = sm_ref.shape[1]
    hm = hid_ref[:, mine_at(idx_ref, half)]
    ho = hid_ref[:, theirs_at(idx_ref, half)]
    square = jnp.sum(hm * hm, axis=1, keepdims=True) + jnp.sum(ho * ho, axis=1, keepdims=True)
    root = lax.rsqrt(square / (2 * half) + 1e-6)
    sm_ref[...] = (hm * root * packed_row(own_ref, *place_g2)).astype(BF16)
    so_ref[...] = (ho * root * packed_row(pack_ref, *place_g2)).astype(BF16)


def ffn_kernel(dims, idx_ref, sm_ref, so_ref, hid_ref, e_ref, wg_own, wg_oth, wu_own, wu_oth, wd_own, wd_oth,
               out_ref, am_ref, g_ref, dm_ref, do_ref, gates_in, ups_in, downs_in, acts, sems):
    seqs, span = dims
    half = wd_own.shape[0]
    spots = (mine_at(idx_ref, half), theirs_at(idx_ref, half))
    cut = half // 256 * 128 + 128
    steps = []
    for side in range(2):
        for first, last in ((0, cut), (cut, half)):
            to_at = pl.ds(first, last - first)
            from_at = pl.ds(pl.multiple_of(spots[side].start + first, 128), last - first)
            now = []
            for to, sources in ((gates_in, (wg_own, wg_oth)), (ups_in, (wu_own, wu_oth))):
                for which in range(2):
                    now.append((sources[which].at[:, from_at], to.at[which, side, :, to_at]))
            now.append(((wd_own, wd_oth)[side].at[to_at, :], downs_in.at[side, to_at, :]))
            copies = [
                pltpu.make_async_copy(src, dst, sems.at[len(steps), i])
                for i, (src, dst) in enumerate(now)
            ]
            for one in copies:
                one.start()
            steps.append(copies)
    out_ref[...] = hid_ref[...]
    dm_ref[...] = jnp.zeros_like(dm_ref)
    do_ref[...] = jnp.zeros_like(do_ref)

    def one_side(side, carry):
        sm, so, cots = sm_ref[...], so_ref[...], e_ref[...]
        at = lax.rem(idx_ref[0] + side, 2) * half
        for part, (first, last) in enumerate(((0, cut), (cut, half))):
            for now in range(2):

                @pl.when(side == now)
                def _():
                    for one in steps[2 * now + part]:
                        one.wait()

            size = last - first
            g_own, g_oth = gates_in[0, side, :, first:last], gates_in[1, side, :, first:last]
            u_own, u_oth = ups_in[0, side, :, first:last], ups_in[1, side, :, first:last]
            down = downs_in[side, first:last, :]
            gates = dot(sm, g_own) + dot(so, g_oth)
            ups = dot(sm, u_own) + dot(so, u_oth)
            sig = sigmoid(gates)
            opened = gates * sig
            act = (opened * ups).astype(BF16)
            acts[side, :, first:last] = act
            grads = dot_t(cots, down)
            gate_grad = (grads * ups * sig * (1.0 + gates * (1.0 - sig))).astype(BF16)
            up_grad = (grads * opened).astype(BF16)
            g_ref[:, pl.ds(pl.multiple_of(at + first, 128), size)] = gate_grad
            g_ref[:, pl.ds(pl.multiple_of(at + first + 2 * half, 128), size)] = up_grad
            out_ref[...] += dot(act, down)
            dm_ref[...] += dot_t(gate_grad, g_own) + dot_t(up_grad, u_own)
            do_ref[...] += dot_t(gate_grad, g_oth) + dot_t(up_grad, u_oth)
        return carry

    lax.fori_loop(0, 2, one_side, 0)
    am_ref[...] = acts[0]
    g_ref[:, 4 * half :] = acts[1]
    width = out_ref.shape[1]
    for s in range(seqs):
        at = slice(s * span, (s + 1) * span)
        places = lax.broadcasted_iota(jnp.int32, (span, width), 0) + idx_ref[1] * span
        out_ref[at, :] = jnp.where(places < idx_ref[2 + s], out_ref[at, :], 0.0)


def gate_back_kernel(dims, idx_ref, hid_ref, dm_ref, do_ref, e_ref, wo_own, wo_oth, mixture_ref,
                     og_ref, qb_ref, tot_ref, own_ref, pack_ref,
                     hg_ref, hl_ref, mg_ref, ol_ref, g2m_ref, g2o_ref, hgm_ref, hgo_ref, m0, m1, m2, m3,
                     gain, gated, gain_sum, state):
    seqs, span = dims
    half = dm_ref.shape[1]
    gain_half = gain.shape[1] // 2
    _, place_g2, _, place_hg = packed_places(half, qb_ref.shape[1] // 2, gain_half)
    mine, theirs = mine_at(idx_ref, half), theirs_at(idx_ref, half)
    hm, ho = hid_ref[:, mine], hid_ref[:, theirs]
    square = jnp.sum(hm * hm, axis=1, keepdims=True) + jnp.sum(ho * ho, axis=1, keepdims=True)
    root = lax.rsqrt(square / (2 * half) + 1e-6)
    dm, do = dm_ref[...], do_ref[...]
    g2m_ref[...] = jnp.sum(dm * hm * root, axis=0, keepdims=True)
    g2o_ref[...] = jnp.sum(do * ho * root, axis=0, keepdims=True)
    dm = dm * packed_row(own_ref, *place_g2)
    do = do * packed_row(pack_ref, *place_g2)
    along = jnp.sum(dm * hm, axis=1, keepdims=True) + jnp.sum(do * ho, axis=1, keepdims=True)
    along = along * (root * root * root) / (2 * half)
    hg_ref[:, mine] = e_ref[:, mine].astype(F32) + dm * root - hm * along
    hg_ref[:, theirs] = e_ref[:, theirs].astype(F32) + do * root - ho * along
    low = hg_ref[...].astype(BF16)
    hl_ref[...] = low
    half = wo_own.shape[0]
    gated[:, mine_at(idx_ref, half)] = dot_t(low, wo_own[...])
    gated[:, theirs_at(idx_ref, half)] = dot_t(low, wo_oth[...])
    gain[:, mine_at(idx_ref, gain_half)] = packed_row(own_ref, *place_hg)
    gain[:, theirs_at(idx_ref, gain_half)] = packed_row(pack_ref, *place_hg)
    head_gain = gain[...]
    wide = qb_ref.shape[1] // HEADS
    tall = mixture_ref.shape[1] // HEADS
    factor = wide ** (-0.5)
    quarter = state.shape[1]
    per = tall // quarter
    gain_grad = jnp.zeros((1, tall), F32)
    for s in range(seqs):
        at = slice(s * span, (s + 1) * span)
        for h in range(HEADS):
            vs = slice(h * tall, (h + 1) * tall)
            hs = slice(h * wide, (h + 1) * wide)
            mixture, opened, grad = mixture_ref[at, vs], og_ref[at, vs], gated[at, vs]
            root = lax.rsqrt(jnp.mean(mixture * mixture, axis=1, keepdims=True) + 1e-5)
            sig = sigmoid(opened)
            flat = mixture * root
            ol_ref[at, vs] = (grad * flat * head_gain * sig * (1.0 + opened * (1.0 - sig))).astype(BF16)
            grad = grad * (opened * sig)
            gain_grad += jnp.sum(grad * flat, axis=0, keepdims=True)
            grad = grad * head_gain
            along = jnp.mean(grad * flat, axis=1, keepdims=True)
            mixed = (grad - flat * along) * (root * factor)
            mg_ref[at, vs] = mixed
            part = t_dot(mixed.astype(BF16), qb_ref[at, hs])
            for q in range(per):
                state[s * per + q, :, hs] = part[q * quarter : (q + 1) * quarter]
    gain_sum[...] = gain_grad
    hgm_ref[...] = gain_sum[:, mine_at(idx_ref, gain_half)]
    hgo_ref[...] = gain_sum[:, theirs_at(idx_ref, gain_half)]
    totals = [tot_ref[pl.ds(s, 1), :] for s in range(seqs)]
    write_quarters(idx_ref, state, totals, (m0, m1, m2, m3), seqs)


def inner_back_kernel(dims, idx_ref, q_ref, k_ref, v_ref, lg_ref, a_ref, mg_ref, qb_ref, st_ref,
                      dq_ref, dk_ref, dv_ref, dc_ref):
    seqs, span = dims
    row, col = pair_iota(span)
    upto = (col <= row).astype(F32).astype(BF16)
    diagonal = row == col
    levels = level_masks(span)
    wide = q_ref.shape[1] // HEADS
    tall = v_ref.shape[1] // HEADS
    quarter = st_ref.shape[1]
    per = tall // quarter
    def one_sequence(s, carry):
        at = pl.ds(pl.multiple_of(s * span, span), span)
        logits = lg_ref[at, :]
        decays = (jnp.minimum(logits, 0.0) - jnp.log1p(jnp.exp(-jnp.abs(logits)))) / 16.0
        high, rest = two_part(decays)
        qs32, ks32 = q_ref[at, :].astype(F32), k_ref[at, :].astype(F32)
        begun = jnp.exp(dot(upto, high) + dot(upto, rest))
        pair_grads = []
        for h in range(HEADS):
            hs = slice(h * wide, (h + 1) * wide)
            vs = slice(h * tall, (h + 1) * tall)
            mixed, more = two_part(mg_ref[at, vs])
            values = v_ref[at, vs]
            full = dot_t(mixed, values) + dot_t(more, values)
            back = dot_t(values, mixed) + dot_t(values, more)
            pair_grads.append(jnp.where(row >= col, full, back))
            dv_ref[at, vs] = t_dot(a_ref[s * HEADS + h], mixed)
            own = jnp.sum(jnp.where(diagonal, full, 0.0), axis=1, keepdims=True)
            crossed = jnp.zeros((span, wide), F32)
            for q in range(per):
                part = slice(h * tall + q * quarter, h * tall + (q + 1) * quarter)
                crossed += dot(mg_ref[at, part].astype(BF16), st_ref[s * per + q, :, hs])
            dq_ref[at, hs] = own * ks32[:, hs] + begun[:, hs] * crossed
            dk_ref[at, hs] = own * qs32[:, hs]
            dc_ref[at, hs] = qb_ref[at, hs].astype(F32) * crossed
        for sums, _, both, half in levels:
            fade = jnp.exp(dot(sums, high) + dot(sums, rest))
            upper = upper_rows(half, qs32.shape[1], span)
            side = (jnp.where(upper, qs32, ks32) * fade).astype(BF16)
            for h in range(HEADS):
                hs = slice(h * wide, (h + 1) * wide)
                grads = dot(jnp.where(both, pair_grads[h], 0.0).astype(BF16), side[:, hs])
                moved = side[:, hs].astype(F32) * grads
                faded = fade[:, hs] * grads
                over = upper[:, hs]
                dc_ref[at, hs] += jnp.where(over, moved, -moved)
                dq_ref[at, hs] += jnp.where(over, faded, 0.0)
                dk_ref[at, hs] += jnp.where(over, 0.0, faded)
        return carry

    lax.fori_loop(0, seqs, one_sequence, 0)


def inputs_back_kernel(dims, idx_ref, dq_ref, dk_ref, dv_ref, dc_ref, ol_ref, kd_ref, v_ref, lg_ref, tot_ref, st_ref,
                       l0, l1, l2, l3, x_ref, hg_ref, wq_own, wq_oth, wk_own, wk_oth, wv_own, wv_oth,
                       wg_own, wg_oth, own_ref, pack_ref, g2o_ref, hgo_ref,
                       tg_ref, ga_ref, llm_ref, g1m_ref, bm_ref, small_ref,
                       leaving, logit, bias):
    seqs, span = dims
    half = wq_own.shape[0]
    part = wq_own.shape[1] // 2
    place_g1, _, _, _ = packed_places(half, part, 0)
    li_own, lo_own = packed_factors(own_ref, half)
    li_oth, lo_oth = packed_factors(pack_ref, half)
    load_state(idx_ref, (l0, l1, l2, l3), leaving)
    row, col = pair_iota(span)
    later = (col > row).astype(F32).astype(BF16)
    since = (col >= row).astype(F32).astype(BF16)
    before = (col < row).astype(F32).astype(BF16)
    keys = kd_ref.shape[1]
    vals = v_ref.shape[1]
    wide, tall = keys // HEADS, vals // HEADS
    quarter = st_ref.shape[1]
    per = tall // quarter
    bias_sum = jnp.zeros((1, keys), F32)
    for s in range(seqs):
        at = slice(s * span, (s + 1) * span)
        logits = lg_ref[at, :]
        decays = (jnp.minimum(logits, 0.0) - jnp.log1p(jnp.exp(-jnp.abs(logits)))) / 16.0
        ahead = jnp.exp(mask_dot(later, decays))
        for h in range(HEADS):
            hs = slice(h * wide, (h + 1) * wide)
            faded = kd_ref[at, hs]
            grads = jnp.zeros((span, wide), F32)
            ends = jnp.zeros((1, wide), F32)
            for q in range(per):
                vs = slice(h * tall + q * quarter, h * tall + (q + 1) * quarter)
                at_v = slice(keys * 2 + vs.start, keys * 2 + vs.stop)
                part = leaving[s * per + q, :, hs]
                ga_ref[at, at_v] = (dv_ref[at, vs] + dot_t(faded, part)).astype(BF16)
                grads += dot(v_ref[at, vs], part)
                ends += jnp.sum(
                    st_ref[s * per + q, :, hs].astype(F32) * part.astype(F32), axis=0, keepdims=True
                )
            moved = faded.astype(F32) * grads
            ga_ref[at, keys + h * wide : keys + (h + 1) * wide] = (
                dk_ref[at, hs] + ahead[:, hs] * grads
            ).astype(BF16)
            decay_grad = (
                mask_dot(since, dc_ref[at, hs])
                + mask_dot(before, moved)
                + tot_ref[pl.ds(s, 1), hs] * ends
            )
            logit_grad = decay_grad * sigmoid(-logits[:, hs]) / 16.0
            bias[:, hs] = jnp.sum(logit_grad, axis=0, keepdims=True)
            logit[at, hs] = logit_grad.astype(BF16)
        bias_sum += bias[...]
    bias[...] = bias_sum
    part = keys // 2
    bm_ref[...] = bias[:, mine_at(idx_ref, part)]
    small_ref[:, 2 * half : 2 * half + part] = bias[:, theirs_at(idx_ref, part)]
    small_ref[:, half : 2 * half] = g2o_ref[...]
    small_ref[:, 2 * half + part :] = hgo_ref[...]
    ga_ref[:, 0:keys] = dq_ref[...].astype(BF16)
    ga_ref[:, 2 * keys + vals : 2 * keys + 2 * vals] = ol_ref[...]
    llm, llo = logit[:, mine_at(idx_ref, part)], logit[:, theirs_at(idx_ref, part)]
    llm_ref[...] = llm
    lrg = (dot_t(llm, lo_own) + dot_t(llo, lo_oth)).astype(BF16)
    rest = jnp.zeros((lrg.shape[0], 128 - RANK), BF16)
    lanes = 2 * keys + 2 * vals + 128
    ga_ref[:, lanes - 128 : lanes] = jnp.concatenate([lrg, rest], axis=1)
    ga_ref[:, lanes:] = llo
    qg, kg = ga_ref[:, 0:keys], ga_ref[:, keys : 2 * keys]
    vg = ga_ref[:, 2 * keys : 2 * keys + vals]
    og = ga_ref[:, 2 * keys + vals : 2 * keys + 2 * vals]
    dm = dot_t(qg, wq_own[...]) + dot_t(kg, wk_own[...]) + dot_t(vg, wv_own[...])
    dm = dm + dot_t(og, wg_own[...]) + dot(lrg, li_own)
    do = dot_t(qg, wq_oth[...]) + dot_t(kg, wk_oth[...]) + dot_t(vg, wv_oth[...])
    do = do + dot_t(og, wg_oth[...]) + dot(lrg, li_oth)
    mine, theirs = mine_at(idx_ref, half), theirs_at(idx_ref, half)
    xm, xo = x_ref[:, mine].astype(F32), x_ref[:, theirs].astype(F32)
    square = jnp.sum(xm * xm, axis=1, keepdims=True) + jnp.sum(xo * xo, axis=1, keepdims=True)
    root = lax.rsqrt(square / (2 * half) + 1e-6)
    g1m_ref[...] = jnp.sum(dm * xm * root, axis=0, keepdims=True)
    small_ref[:, 0:half] = jnp.sum(do * xo * root, axis=0, keepdims=True)
    dm = dm * packed_row(own_ref, *place_g1)
    do = do * packed_row(pack_ref, *place_g1)
    along = jnp.sum(dm * xm, axis=1, keepdims=True) + jnp.sum(do * xo, axis=1, keepdims=True)
    along = along * (root * root * root) / (2 * half)
    tg_ref[:, mine] = hg_ref[:, mine] + dm * root - xm * along
    tg_ref[:, theirs] = hg_ref[:, theirs] + do * root - xo * along


def block_of(position, order):
    block = 0
    for at, bit in enumerate(order):
        if (position >> (3 - at)) & 1:
            block |= bit
    return block


def deal(position, keep_ref, send_ref):
    return keep_ref.at[position] if position < 8 else send_ref.at[position - 8]


def wide_grad_kernel(orders, idx_ref, sm_ref, so_ref, gm_ref, go_ref, k0, s0, k1, s1, full):
    place = lax.rem(idx_ref[1], 16)
    width = full.shape[1]
    high = full.shape[0] // 16
    for which, refs in enumerate(((k0, s0), (k1, s1))):
        cols = slice(which * width, (which + 1) * width)
        full[...] = t_dot(sm_ref[...], gm_ref[:, cols]) + t_dot(so_ref[...], go_ref[:, cols])
        for position in range(16):
            block = block_of(position, orders[which]) ^ place
            rows = full[pl.ds(pl.multiple_of(block * high, high), high), :].astype(BF16)
            to = deal(position, *refs)
            for tile in range(width // 128):
                to[tile * high : (tile + 1) * high, :] = rows[:, tile * 128 : (tile + 1) * 128]


def down_grad_kernel(order, idx_ref, am_ref, go_ref, em_ref, eo_ref, keep_ref, send_ref, full):
    place = lax.rem(idx_ref[1], 16)
    first = go_ref.shape[1] - am_ref.shape[1]
    full[...] = t_dot(am_ref[...], em_ref[...]) + t_dot(go_ref[:, first:], eo_ref[...])
    high = full.shape[0] // 2
    for position in range(16):
        block = block_of(position, order) ^ place
        rows = pl.ds(pl.multiple_of(lax.div(block, 8) * high, 16), high)
        cols = pl.ds(pl.multiple_of(lax.rem(block, 8) * 128, 128), 128)
        deal(position, keep_ref, send_ref)[...] = full[rows, cols].astype(BF16)


def attention_grad_kernel(orders, cuts, idx_ref, nm_ref, no_ref, gm_ref, go_ref, am_ref, ao_ref, hm_ref, ho_ref,
                          lrm_ref, lro_ref, llm_ref, g1_ref, g2_ref, b_ref, hg_ref, small_ref, k0, s0, k1, s1, k2, s2, full, outer, small):
    place = lax.rem(idx_ref[1], 16)
    lanes = full.shape[1]
    full[...] = t_dot(nm_ref[...], gm_ref[:, 0:lanes]) + t_dot(no_ref[...], go_ref[:, 0:lanes])
    outer[...] = t_dot(am_ref[...], hm_ref[...]) + t_dot(ao_ref[...], ho_ref[...])
    low_out = t_dot(lrm_ref[...], llm_ref[...]) + t_dot(lro_ref[...], go_ref[:, lanes:])
    small[...] = jnp.zeros_like(small)
    small[0] = low_out[:, 0:128]
    small[1] = low_out[:, 128:256]
    line = 0
    for ref in (g1_ref, g2_ref, b_ref, hg_ref):
        row = ref[...] + small_ref[:, line * 128 : line * 128 + ref.shape[1]]
        for tile in range(row.shape[1] // 128):
            small[2, line : line + 1, :] = row[:, tile * 128 : (tile + 1) * 128]
            line += 1
    high = full.shape[0] // 16
    tiles = full.shape[1] // 128
    for which, refs in enumerate(((k0, s0), (k1, s1), (k2, s2))):
        first, last = cuts[which], cuts[which + 1]
        for position in range(16):
            block = block_of(position, orders[which]) ^ place
            at = pl.ds(pl.multiple_of(block * high, high), high)
            to = deal(position, *refs)
            for tile in range(first, last):
                if tile < tiles:
                    rows = full[at, tile * 128 : (tile + 1) * 128]
                else:
                    rows = outer[at, (tile - tiles) * 128 : (tile - tiles + 1) * 128]
                to[(tile - first) * high : (tile - first + 1) * high, :] = rows.astype(BF16)
            if which == 2:
                to[(last - first) * high :, :] = small[block].astype(BF16)


def wide_open_kernel(order, idx_ref, own_ref, got_ref, out_ref):
    place = lax.rem(idx_ref[1], 16)
    high = out_ref.shape[0] // 16
    for position in range(16):
        block = block_of(position, order) ^ place
        held = deal(position, own_ref, got_ref)
        at = pl.ds(pl.multiple_of(block * high, high), high)
        for tile in range(out_ref.shape[1] // 128):
            out_ref[at, tile * 128 : (tile + 1) * 128] = held[tile * high : (tile + 1) * high, :].astype(F32)


def down_open_kernel(order, idx_ref, own_ref, got_ref, out_ref):
    place = lax.rem(idx_ref[1], 16)
    high = out_ref.shape[0] // 2
    for position in range(16):
        block = block_of(position, order) ^ place
        rows = pl.ds(pl.multiple_of(lax.div(block, 8) * high, 16), high)
        cols = pl.ds(pl.multiple_of(lax.rem(block, 8) * 128, 128), 128)
        out_ref[rows, cols] = deal(position, own_ref, got_ref)[...].astype(F32)


def attention_open_kernel(orders, cuts, idx_ref, o0, r0, o1, r1, o2, r2, q_ref, k_ref, v_ref, og_ref, li_ref, w_ref,
                          lo_ref, g1_ref, g2_ref, b_ref, hg_ref, small, first_factor):
    place = lax.rem(idx_ref[1], 16)
    high = q_ref.shape[0] // 16
    homes = []
    for ref in (q_ref, k_ref, v_ref, og_ref):
        homes += [(ref, tile) for tile in range(ref.shape[1] // 128)]
    homes.append((first_factor, 0))
    homes += [(w_ref, tile) for tile in range(w_ref.shape[1] // 128)]
    for which, refs in enumerate(((o0, r0), (o1, r1), (o2, r2))):
        first, last = cuts[which], cuts[which + 1]
        for position in range(16):
            block = block_of(position, orders[which]) ^ place
            at = pl.ds(pl.multiple_of(block * high, high), high)
            held = deal(position, *refs)
            for tile in range(first, last):
                rows = held[(tile - first) * high : (tile - first + 1) * high, :].astype(F32)
                ref, column = homes[tile]
                ref[at, column * 128 : (column + 1) * 128] = rows
            if which == 2:
                small[block] = held[(last - first) * high :, :].astype(F32)
    li_ref[...] = first_factor[...].T[0 : li_ref.shape[0], :]
    lo_ref[:, 0:128] = small[0]
    lo_ref[:, 128:256] = small[1]
    line = 0
    for ref in (g1_ref, g2_ref, b_ref, hg_ref):
        for tile in range(ref.shape[1] // 128):
            ref[:, tile * 128 : (tile + 1) * 128] = small[2, line : line + 1, :]
            line += 1


def across(array):
    return lax.ppermute(array, "fsdp", ((0, 1), (1, 0)))


def swap(array, bit):
    count = lax.axis_size("seq")
    return lax.ppermute(array, "seq", tuple((one, one ^ bit) for one in range(count)))


def ahead(array, step):
    count = lax.axis_size("seq")
    return lax.ppermute(
        array,
        "seq",
        tuple((one, one + step) for one in range(count) if 0 <= one + step < count),
    )


def fence(*groups):
    return lax.optimization_barrier(groups)


class Portions:
    def __init__(self, parts, orders):
        self.kept = [keep for keep, _ in parts]
        self.sent = [send for _, send in parts]
        self.orders = orders

    def move(self, arrays, step):
        if step < 3:
            return [swap(a, order[step]) for a, order in zip(arrays, self.orders)]
        return self.move_all(arrays, self.orders[0][3])

    def move_all(self, arrays, bit):
        got = swap(jnp.concatenate(arrays, axis=1), bit)
        ends = [0]
        for a in arrays:
            ends.append(ends[-1] + a.shape[1])
        return [got[:, first:last] for first, last in zip(ends[:-1], ends[1:])]

    def reduce_start(self, step):
        return self.move(self.sent, step)

    def reduce_end(self, step, got):
        for one, more in enumerate(got):
            if step < 3:
                half = more.shape[0] // 2
                self.sent[one] = self.kept[one][half:] + more[half:]
                self.kept[one] = self.kept[one][:half] + more[:half]
            else:
                self.kept[one] = self.kept[one] + more
        bit = 16
        while step == 3 and bit < lax.axis_size("seq"):
            more = self.move_all(self.kept, bit)
            self.kept = [k + m for k, m in zip(self.kept, more)]
            bit *= 2

    def gather_start(self, step):
        return self.move(self.kept, step)

    def gather_end(self, step, got):
        if step:
            self.kept = [jnp.concatenate([k, more], axis=0) for k, more in zip(self.kept, got)]
        else:
            self.halves = list(zip(self.kept, got))


def scan_near(messages):
    return [messages[0]] + [swap(messages[o], o) for o in (1, 2, 3)]


def scan_scratch(messages):
    rows, lanes = messages[0].shape
    return [((4, rows - 16, lanes), F32), ((4, 1, lanes), F32)]


def scan_total(near, idx, reverse):
    return call("group_total", partial(group_total, reverse), idx, near, [(near[0].shape, BF16)], scan_scratch(near))[0]


def scan_far(total, reverse):
    sign = -4 if reverse else 4
    return [ahead(total, sign * step) for step in range(1, lax.axis_size("seq") // 4)]


def scan_entering(far, near, idx, reverse):
    rows, lanes = near[0].shape
    return call(
        "group_entering", partial(group_entering, reverse, len(far)), idx, list(far) + list(near),
        [((rows - 16, lanes), BF16)] * 4, scan_scratch(near) + [((4, rows - 16, lanes), F32)],
    )


def shards(
    tokens,
    lengths,
    first_gain,
    query_weight,
    key_weight,
    value_weight,
    outgate_weight,
    lowrank_in,
    lowrank_out,
    decay_bias,
    head_gain,
    output_weight,
    second_gain,
    gate_weight,
    up_weight,
    down_weight,
    cotangent,
):
    micro_count, pair_count, span, width = tokens.shape
    seqs = micro_count * pair_count
    rows = seqs * span
    dims = (seqs, span)
    core = lax.axis_index("fsdp")
    place = lax.axis_index("seq")
    own_lengths = lax.dynamic_slice_in_dim(lengths, core * pair_count, pair_count, 1).reshape(-1)
    idx = jnp.concatenate([jnp.stack([core, place]).astype(jnp.int32), own_lengths])
    keys, vals, ff = query_weight.shape[1], value_weight.shape[1], gate_weight.shape[1]
    half = query_weight.shape[0]
    tall = vals // HEADS
    quarter = seqs * tall // 4

    x = tokens.reshape(rows, width)
    cot = cotangent.reshape(rows, width)
    lrank = lowrank_in.shape[1]
    lines, at = 0, 0
    for a in (first_gain, second_gain, decay_bias, head_gain):
        lines = lines + jnp.pad(a, (at, 16 * 128 - at - a.size))
        at += a.size
    lines = lines.reshape(16, 128)
    pack = call(
        "pack", pack_kernel, idx, [lowrank_in.T, lowrank_out, lines],
        [((lrank * (half + lowrank_out.shape[1]) // 128 + 16, 128), BF16)],
    )[0]
    pack2, wk2, wv2 = (across(a) for a in (pack, key_weight, value_weight))

    message = ((quarter + 16, keys), BF16)
    state = ((4, quarter, keys), F32)
    nm, no, k, v, lr, lg, kd, tot, *messages = call(
        "keys", partial(keys_kernel, dims), idx,
        [x, key_weight, wk2, value_weight, wv2, pack, pack2],
        [((rows, half), BF16), ((rows, half), BF16), ((rows, keys), BF16), ((rows, vals), BF16),
         ((rows, lrank), BF16), ((rows, keys), F32), ((rows, keys), BF16), ((seqs, keys), F32)]
        + [message] * 4,
        [state],
    )
    messages, outgate_send, query_send = fence(messages, outgate_weight, query_weight)
    near = scan_near(messages)
    wg2, wq2 = across(outgate_send), across(query_send)
    q, og, mix, scores, qb, cots = call(
        "inner", partial(inner_kernel, dims), idx,
        [nm, no, query_weight, wq2, outgate_weight, wg2, k, v, lg, cot],
        [((rows, keys), BF16), ((rows, vals), F32), ((rows, vals), F32), ((seqs * HEADS, span, span), BF16),
         ((rows, keys), BF16), ((rows, width), BF16)],
    )
    near, mix, gate_send, up_send = fence(near, mix, gate_weight, up_weight)
    total = scan_total(near, idx, False)
    total, gate_send, up_send = fence(total, gate_send, up_send)
    far = scan_far(total, False)
    wgate2, wup2 = across(gate_send), across(up_send)
    far, wgate2, wup2 = fence(far, wgate2, wup2)
    pieces = scan_entering(far, near, idx, False)
    pieces, output_send, down_send = fence(pieces, output_weight, down_weight)
    pieces = [pieces[0]] + [swap(pieces[o], o) for o in (1, 2, 3)]
    wo2, wdown2 = across(output_send), across(down_send)
    mixture, gm, go, hid, sm, so, st = call(
        "hidden", partial(hidden_kernel, dims), idx,
        [mix, qb, *pieces, og, x, output_weight, wo2, pack, pack2],
        [((rows, vals), F32), ((rows, vals // 2), BF16), ((rows, vals // 2), BF16), ((rows, width), F32),
         ((rows, half), BF16), ((rows, half), BF16), ((4, quarter, keys), BF16)],
        [((1, tall), F32), ((rows, vals), BF16)],
    )
    so, no_send, lr_send, cots_send = fence(so, no, lr, cots)
    so2, no2, go2, lr2, cots2 = (across(a) for a in (so, no_send, go, lr_send, cots_send))
    out, am, gu, dm, do = call(
        "ffn", partial(ffn_kernel, dims), idx,
        [sm, so, hid, cots, gate_weight, wgate2, up_weight, wup2, down_weight, wdown2],
        [((rows, width), F32), ((rows, ff // 2), BF16), ((rows, 5 * ff // 2), BF16),
         ((rows, half), F32), ((rows, half), F32)],
        [((2, 2, half, ff // 2), BF16), ((2, 2, half, ff // 2), BF16), ((2, ff // 2, width), BF16),
         ((2, rows, ff // 2), BF16), pltpu.SemaphoreType.DMA((4, 5))], limit=42, far=6,
    )
    so2, no2, go2, lr2, cots2, gu, dm = fence(so2, no2, go2, lr2, cots2, gu, dm)

    orders = ((1, 2, 4, 8), (2, 4, 1, 8), (4, 1, 2, 8))
    hg, hl, mg, ol, g2m, g2o, hgm, hgo, *messages = call(
        "gate_back", partial(gate_back_kernel, dims), idx,
        [hid, dm, do, cots, output_weight, wo2, mixture, og, qb, tot, pack, pack2],
        [((rows, width), F32), ((rows, width), BF16), ((rows, vals), F32), ((rows, vals), BF16),
         ((1, half), F32), ((1, half), F32), ((1, tall // 2), F32), ((1, tall // 2), F32)] + [message] * 4,
        [((1, tall), F32), ((rows, vals), F32), ((1, tall), F32), state],
    )
    messages, gu_send, mg = fence(messages, gu, mg)
    near = scan_near(messages)
    gu2 = across(gu_send)
    dq, dk, dv, dc = call(
        "inner_back", partial(inner_back_kernel, dims), idx, [q, k, v, lg, scores, mg, qb, st],
        [((rows, keys), F32), ((rows, keys), F32), ((rows, vals), F32), ((rows, keys), F32)],
    )
    near, gu2, dq = fence(near, gu2, dq)
    total = scan_total(near, idx, True)
    total, gu2 = fence(total, gu2)
    far = scan_far(total, True)
    portion = ff // 128 * (half // 16)
    flat = [((8, portion, 128), BF16)] * 2
    wide_parts = call("wide_grad", partial(wide_grad_kernel, orders), idx, [sm, so2, gu, gu2], flat * 2,
                      [((half, ff), F32)], limit=32)
    am, wide_parts = fence(am, wide_parts)
    down_parts = call("down_grad", partial(down_grad_kernel, orders[2]), idx, [am, gu2, cots, cots2], flat,
                      [((ff // 2, width), F32)])
    far, down_parts = fence(far, down_parts)
    first = Portions([wide_parts[0:2], wide_parts[2:4], down_parts], orders)
    got = first.reduce_start(0)
    pieces = scan_entering(far, near, idx, True)
    pieces = [pieces[0]] + [swap(pieces[o], o) for o in (1, 2, 3)]
    got, pieces = fence(got, pieces)
    first.reduce_end(0, got)
    first.sent, pieces = fence(first.sent, pieces)
    got = first.reduce_start(1)
    lanes = 2 * keys + 2 * vals + 128
    tg, ga, llm, g1m, bm, small = call(
        "inputs_back", partial(inputs_back_kernel, dims), idx,
        [dq, dk, dv, dc, ol, kd, v, lg, tot, st, *pieces, x, hg, query_weight, wq2, key_weight, wk2,
         value_weight, wv2, outgate_weight, wg2, pack, pack2, g2o, hgo],
        [((rows, width), F32), ((rows, lanes + keys // 2), BF16), ((rows, keys // 2), BF16),
         ((1, half), F32), ((1, keys // 2), F32), ((1, 2 * half + keys // 2 + tall // 2), F32)],
        [((4, quarter, keys), BF16), ((rows, keys), BF16), ((1, keys), F32)], limit=32,
    )
    got, ga, small = fence(got, ga, small)
    first.reduce_end(1, got)
    got = first.reduce_start(2)
    ga2, small2, hl2 = across(ga), across(small), across(hl)
    tiles = lanes // 128 + width // 128
    third = tiles // 3 + 1
    cuts = (0, third, 2 * third, tiles)
    high = half // 16
    shapes = []
    for which in range(3):
        size = (cuts[which + 1] - cuts[which]) * high + (16 if which == 2 else 0)
        shapes += [((8, size, 128), BF16)] * 2
    parts = call(
        "attention_grad", partial(attention_grad_kernel, orders, cuts), idx,
        [nm, no2, ga, ga2, gm, go2, hl, hl2, lr, lr2, llm, g1m, g2m, bm, hgm, small2],
        shapes, [((half, lanes), F32), ((vals // 2, width), F32), ((16, 16, 128), F32)], limit=32,
    )
    got, parts = fence(got, parts)
    first.reduce_end(2, got)
    second = Portions([parts[0:2], parts[2:4], parts[4:6]], orders)
    got, more = fence(first.reduce_start(3), second.reduce_start(0))
    first.reduce_end(3, got)
    second.reduce_end(0, more)
    got, more = fence(first.gather_start(3), second.reduce_start(1))
    first.gather_end(3, got)
    second.reduce_end(1, more)
    both = [jnp.concatenate([k, a], axis=1) for k, a in zip(first.kept, second.sent)]
    both = fence(*[swap(a, order[2]) for a, order in zip(both, orders)])
    got = [a[:, : k.shape[1]] for a, k in zip(both, first.kept)]
    more = [a[:, k.shape[1] :] for a, k in zip(both, first.kept)]
    first.gather_end(2, got)
    second.reduce_end(2, more)
    got, more = fence(first.gather_start(1), second.reduce_start(3))
    first.gather_end(1, got)
    second.reduce_end(3, more)
    got, more = fence(first.gather_start(0), second.gather_start(3))
    first.gather_end(0, got)
    second.gather_end(3, more)
    gate_halves, up_halves, down_halves = first.halves
    more = second.gather_start(2)
    gate_out = call("gate_open", partial(wide_open_kernel, orders[0]), idx, gate_halves, [((half, ff), F32)])[0]
    more, gate_out = fence(more, gate_out)
    second.gather_end(2, more)
    more = second.gather_start(1)
    up_out = call("up_open", partial(wide_open_kernel, orders[1]), idx, up_halves, [((half, ff), F32)])[0]
    more, up_out = fence(more, up_out)
    second.gather_end(1, more)
    more = second.gather_start(0)
    down_out = call("down_open", partial(down_open_kernel, orders[2]), idx, down_halves, [((ff // 2, width), F32)])[0]
    more, down_out = fence(more, down_out)
    second.gather_end(0, more)
    opened = call(
        "attention_open", partial(attention_open_kernel, orders, cuts), idx, [a for pair in second.halves for a in pair],
        [((half, keys), F32), ((half, keys), F32), ((half, vals), F32), ((half, vals), F32),
         ((lrank, half), F32), ((vals // 2, width), F32), ((lrank, keys // 2), F32),
         ((1, half), F32), ((1, half), F32), ((1, keys // 2), F32), ((1, tall // 2), F32)],
        [((16, 16, 128), F32), ((half, 128), F32)],
    )
    q_out, k_out, v_out, og_out, li_out, w_out, lo_out, g1_out, g2_out, b_out, hg_out = opened
    return (
        out.reshape(tokens.shape),
        tg.reshape(tokens.shape),
        g1_out.reshape(-1),
        q_out,
        k_out,
        v_out,
        og_out,
        li_out.T,
        lo_out,
        b_out.reshape(-1),
        hg_out.reshape(-1),
        w_out,
        g2_out.reshape(-1),
        gate_out,
        up_out,
        down_out,
    )


def solution(mesh):
    shard, column = P("fsdp", None), P(None, "fsdp")
    stream, line = P(None, "fsdp", "seq", None), P("fsdp")
    weights = (line, shard, shard, shard, shard, shard, column, line, line, shard, line, shard, shard, shard)
    return jax.shard_map(
        shards,
        mesh=mesh,
        in_specs=(stream, P()) + weights + (stream,),
        out_specs=(stream, stream) + weights,
        check_vma=False,
    )
```
